32 devices in a mesh: fsdp: 4 (over y, x), ctx: 4 (over z), tp: 2 (over core).
Axes of the slice: x: 2, y: 2, z: 4, core: 2. Of those that a mesh axis runs over, the one named last changes fastest.
Arguments:
- hidden_in: bfloat16 [8, 1024, 1024], P('fsdp', ('ctx', 'tp')), may hold values from -6 to 6
- seq_lengths: int32 [8], P('fsdp'), may hold values from 512 to 1024, as said below
- attn_gain: float32 [1024], replicated, may hold values from 0.1 to 1.9
- query_gain: float32 [64], replicated, may hold values from 0.1 to 1.9
- key_gain: float32 [64], replicated, may hold values from 0.1 to 1.9
- query_weight: bfloat16 [1024, 1024], P(('fsdp', 'ctx'), 'tp'), may hold values from -0.1875 to 0.1875
- key_projection: bfloat16 [1024, 512], P(('fsdp', 'ctx'), 'tp'), may hold values from -0.1875 to 0.1875
- value_projection: bfloat16 [1024, 512], P(('fsdp', 'ctx'), 'tp'), may hold values from -0.1875 to 0.1875
- out_weight: bfloat16 [1024, 1024], P('tp', ('fsdp', 'ctx')), may hold values from -1 to 1
- ffn_gain: float32 [1024], replicated, may hold values from 0.1 to 1.9
- gate_weight: bfloat16 [1024, 4608], P(('fsdp', 'ctx'), 'tp'), may hold values from -0.1875 to 0.1875
- up_weight: bfloat16 [1024, 4608], P(('fsdp', 'ctx'), 'tp'), may hold values from -0.1875 to 0.1875
- down_weight: bfloat16 [4608, 1024], P('tp', ('fsdp', 'ctx')), may hold values from -0.09375 to 0.09375
- cotangent: bfloat16 [8, 1024, 1024], P('fsdp', ('ctx', 'tp')), may hold values from -6 to 6
Outputs:
- block_out: bfloat16 [8, 1024, 1024], P('fsdp', ('ctx', 'tp'))
- input_grad: bfloat16 [8, 1024, 1024], P('fsdp', ('ctx', 'tp'))
- attn_gain_grad: float32 [1024], replicated
- query_gain_grad: float32 [64], replicated
- key_gain_grad: float32 [64], replicated
- query_weight_grad: float32 [1024, 1024], P(('fsdp', 'ctx'), 'tp')
- key_weight_grad: float32 [1024, 512], P(('fsdp', 'ctx'), 'tp')
- value_weight_grad: float32 [1024, 512], P(('fsdp', 'ctx'), 'tp')
- out_weight_grad: float32 [1024, 1024], P('tp', ('fsdp', 'ctx'))
- ffn_gain_grad: float32 [1024], replicated
- gate_weight_grad: float32 [1024, 4608], P(('fsdp', 'ctx'), 'tp')
- up_weight_grad: float32 [1024, 4608], P(('fsdp', 'ctx'), 'tp')
- down_weight_grad: float32 [4608, 1024], P('tp', ('fsdp', 'ctx'))
The draws below stay inside these ranges and needn't reach their ends.
Inputs may be any that keep to these rules, and one draw needn't show every extreme that they name: `seq_lengths`: among the 2 slots of each index of fsdp (aligned blocks of 2 slots) at least one has length 1024.
All inputs are finite; a program needn't handle non-finite values.
Results may differ from the reference program's by a relative error of at most 0.017.
Values may be sent and summed in bfloat16 or wider, within the bound.
No kernel may reach another device: no remote copies, remote signals or barrier semaphores. Data moves between devices by JAX's collectives and lax.ppermute only.
A program may use at most 88 MiB of HBM per device.

```python
import jax
import jax.numpy as jnp
from jax import lax

MODEL_WIDTH = 1024
QUERY_HEADS = 16
KEY_VALUE_HEADS = 8
HEAD_SIZE = 64
FF = 4608
SLOT_POSITIONS = 1024
MB = 2
SLOTS = 8


def draw_seq_lengths(key, part):
    groups = SLOTS // MB
    base = jax.random.randint(jax.random.fold_in(key, 11), (groups, MB), SLOT_POSITIONS // 2, SLOT_POSITIONS + 1)
    chosen = jax.random.randint(jax.random.fold_in(key, 12), (groups, 1), 0, MB)
    full = jnp.arange(MB)[None, :] == chosen
    return jnp.where(full, SLOT_POSITIONS, base).reshape(SLOTS).astype(jnp.int32)


def raised(drawn, own_key, source, target, parts, factor):
    owner, partner = [(jnp.arange(drawn.shape[axis_at]) // (drawn.shape[axis_at] // parts)).reshape([-1 if axis == axis_at else 1 for axis in range(drawn.ndim)]) for axis_at in (source, target)]
    chosen = jax.random.permutation(own_key, parts)[partner]
    strong = (owner == chosen) | (owner == (partner + parts // 2) % parts)
    return jnp.where(strong, factor * drawn, drawn)


def steps_of(stream_key, dims, split, least, largest):
    factor_of = 1.0
    for dim, parts in split:
        draws = jax.random.uniform(jax.random.fold_in(jax.random.fold_in(stream_key, 6), dim), (parts,), jnp.float32, least / len(split), largest / len(split))
        factor_of = factor_of * jnp.repeat(jnp.exp(draws), dims[dim] // parts).reshape((-1,) + (1,) * (len(dims) - 1 - dim))
    return factor_of


def noise(stream_key, dims, scale, reach, split=(), held_as=jnp.bfloat16):
    loudness = steps_of(stream_key, dims, split, -0.22, 0.18) if split else 1.0
    entries = jax.random.normal(stream_key, dims, jnp.float32) * scale * loudness
    return jnp.minimum(jnp.maximum(entries, -reach), reach).astype(held_as)


def bell_draw_with(own_key, extent, scale, most, split, heavy, dtype=jnp.bfloat16):
    array = scale * jax.random.normal(own_key, extent, jnp.float32)
    if split:
        array = array * steps_of(own_key, extent, split, -0.22, 0.18)
    return jnp.clip(raised(array, jax.random.fold_in(own_key, 3), *heavy), -most, most).astype(dtype)


def setup_inputs(seed: int = 0) -> dict:
    arg_keys = jax.random.split(jax.random.key(seed), 15)
    hidden_in = noise(arg_keys[0], (SLOTS, SLOT_POSITIONS, MODEL_WIDTH), 1.0, 6.0, ((0, 4), (1, 8)))
    seq_lengths = draw_seq_lengths(jax.random.fold_in(arg_keys[14], 71), 0)
    attn_gain = jnp.clip(1.0 + 0.18 * jax.random.normal(arg_keys[2], (MODEL_WIDTH,), jnp.float32), 0.1, 1.9)
    query_gain = jnp.clip(1.0 + 0.18 * jax.random.normal(arg_keys[3], (HEAD_SIZE,), jnp.float32), 0.1, 1.9)
    key_gain = jnp.clip(1.0 + 0.18 * jax.random.normal(arg_keys[4], (HEAD_SIZE,), jnp.float32), 0.1, 1.9)
    query_weight = noise(arg_keys[5], (MODEL_WIDTH, QUERY_HEADS * HEAD_SIZE), MODEL_WIDTH ** -0.5, 0.1875, ((0, 16), (1, 2)))
    key_projection = noise(arg_keys[6], (MODEL_WIDTH, KEY_VALUE_HEADS * HEAD_SIZE), MODEL_WIDTH ** -0.5, 0.1875, ((0, 16), (1, 2)))
    value_projection = noise(arg_keys[7], (MODEL_WIDTH, KEY_VALUE_HEADS * HEAD_SIZE), MODEL_WIDTH ** -0.5, 0.1875, ((0, 16), (1, 2)))
    out_weight = noise(arg_keys[8], (QUERY_HEADS * HEAD_SIZE, MODEL_WIDTH), (QUERY_HEADS * HEAD_SIZE // 32) ** -0.5, 1.0, ((0, 2), (1, 16)))
    ffn_gain = jnp.clip(1.0 + 0.18 * jax.random.normal(arg_keys[9], (MODEL_WIDTH,), jnp.float32), 0.1, 1.9)
    gate_weight = noise(arg_keys[10], (MODEL_WIDTH, FF), MODEL_WIDTH ** -0.5, 0.1875, ((0, 16), (1, 2)))
    up_weight = noise(arg_keys[11], (MODEL_WIDTH, FF), MODEL_WIDTH ** -0.5, 0.1875, ((0, 16), (1, 2)))
    down_weight = noise(arg_keys[12], (FF, MODEL_WIDTH), FF ** -0.5, 0.09375, ((0, 2), (1, 16)))
    cotangent = bell_draw_with(arg_keys[13], (SLOTS, SLOT_POSITIONS, MODEL_WIDTH), 1.0, 6.0, ((0, 4), (1, 8)), (0, 2, 4, 2.0))
    return {"hidden_in": hidden_in, "seq_lengths": seq_lengths, "attn_gain": attn_gain, "query_gain": query_gain, "key_gain": key_gain, "query_weight": query_weight, "key_projection": key_projection, "value_projection": value_projection, "out_weight": out_weight, "ffn_gain": ffn_gain, "gate_weight": gate_weight, "up_weight": up_weight, "down_weight": down_weight, "cotangent": cotangent}


EPS = 1e-05
THETA = 1000000.0

@jax.custom_vjp
def reduced_precision(v):
    return lax.optimization_barrier(v.astype(jnp.bfloat16)).astype(jnp.float32)

@jax.custom_vjp
def reduced_backward(v):
    return v

def low_keep(v):
    return (reduced_precision(v), None)

def low_pass(kept, grad):
    return (grad,)

def back_keep(v):
    return (v, None)

def back_low(kept, grad):
    return (reduced_precision(grad),)
reduced_precision.defvjp(low_keep, low_pass)
reduced_backward.defvjp(back_keep, back_low)

def matrix_product(left, right):
    return jnp.dot(left, right, precision=lax.Precision.HIGHEST)

def rms_scale(values, gain):
    return values * lax.rsqrt(lax.optimization_barrier(jnp.mean(values * values, axis=-1, keepdims=True)) + EPS) * gain

def rotate(values, places):
    half = HEAD_SIZE // 2
    freqs = THETA ** (-(jnp.arange(half).astype(jnp.float32) * 2.0 / HEAD_SIZE))
    angles = places.astype(jnp.float32)[:, None] * freqs[None, :]
    cosine = jnp.cos(angles)[:, None, :]
    sine = jnp.sin(angles)[:, None, :]
    first = values[..., :half]
    second = values[..., half:]
    return jnp.concatenate([first * cosine - second * sine, second * cosine + first * sine], axis=-1)

def attend(query_rows, keys, values, length):
    head_group = QUERY_HEADS // KEY_VALUE_HEADS
    block_rows = min(512, SLOT_POSITIONS)
    scale_factor = HEAD_SIZE ** (-0.5)
    grouped_rows = query_rows.reshape(SLOT_POSITIONS, KEY_VALUE_HEADS, head_group, HEAD_SIZE)
    key_places = jnp.arange(SLOT_POSITIONS).astype(jnp.int32)

    def one_block(first_row):
        part = lax.dynamic_slice_in_dim(grouped_rows, first_row, block_rows, 0)
        scores = jnp.einsum('qhgd,khd->hgqk', part, keys, precision=lax.Precision.HIGHEST)
        scores = reduced_backward(scores * scale_factor)
        query_positions = first_row + jnp.arange(block_rows).astype(jnp.int32)
        allowed = (key_places[None, :] <= query_positions[:, None]) & (key_places[None, :] < length)
        scores = jnp.where(allowed, scores, -1e+30)
        top = lax.optimization_barrier(jnp.max(scores, axis=-1, keepdims=True))
        exp_scores = jnp.exp(scores - top)
        probs = exp_scores / lax.optimization_barrier(jnp.sum(exp_scores, axis=-1, keepdims=True))
        mixed = jnp.einsum('hgqk,khd->qhgd', reduced_precision(probs), values, precision=lax.Precision.HIGHEST)
        return mixed.reshape(block_rows, QUERY_HEADS * HEAD_SIZE)
    firsts = jnp.arange(SLOT_POSITIONS // block_rows).astype(jnp.int32) * block_rows
    return lax.map(jax.checkpoint(one_block), firsts).reshape(SLOT_POSITIONS, QUERY_HEADS * HEAD_SIZE)

def slot_forward(hidden, length, params):
    attn_g, query_g, key_g, query_w, key_matrix, value_matrix, out_w, ffn_g, gate_w, up_w, down_w = params
    places = jnp.arange(SLOT_POSITIONS).astype(jnp.int32)
    normalized_input = reduced_precision(rms_scale(hidden, attn_g))
    query_raw = reduced_backward(matrix_product(normalized_input, query_w)).reshape(SLOT_POSITIONS, QUERY_HEADS, HEAD_SIZE)
    key_unrotated = reduced_backward(matrix_product(normalized_input, key_matrix)).reshape(SLOT_POSITIONS, KEY_VALUE_HEADS, HEAD_SIZE)
    value_rows = reduced_precision(reduced_backward(matrix_product(normalized_input, value_matrix))).reshape(SLOT_POSITIONS, KEY_VALUE_HEADS, HEAD_SIZE)
    query_rows = reduced_precision(rotate(rms_scale(query_raw, query_g), places))
    key = reduced_precision(rotate(rms_scale(key_unrotated, key_g), places))
    attn = reduced_precision(reduced_backward(attend(query_rows, key, value_rows, length)))
    middle = hidden + reduced_backward(matrix_product(attn, out_w))
    normed_two = reduced_precision(rms_scale(middle, ffn_g))
    gate = reduced_backward(matrix_product(normed_two, gate_w))
    upper = reduced_backward(matrix_product(normed_two, up_w))
    act = reduced_precision(jax.nn.silu(gate) * upper)
    result = middle + reduced_backward(matrix_product(act, down_w))
    valid = places < length
    return jnp.where(valid[:, None], result, 0.0)

def reference(hidden_in, seq_lengths, attn_gain, query_gain, key_gain, query_weight, key_projection, value_projection, out_weight, ffn_gain, gate_weight, up_weight, down_weight, cotangent):
    params = tuple((item.astype(jnp.float32) for item in (attn_gain, query_gain, key_gain, query_weight, key_projection, value_projection, out_weight, ffn_gain, gate_weight, up_weight, down_weight)))
    slot_step = jax.checkpoint(slot_forward)

    def forward(hidden, weights):

        def per_slot(carry, pair):
            return (carry, slot_step(pair[0], pair[1], weights))
        unused, stacked = lax.scan(per_slot, None, (hidden, seq_lengths))
        return stacked
    primal, pullback = jax.vjp(forward, hidden_in.astype(jnp.float32), params)
    grad_hidden, grads = pullback(cotangent.astype(jnp.float32))
    return (primal.astype(jnp.bfloat16), grad_hidden.astype(jnp.bfloat16), grads[0], grads[1], grads[2], grads[3], grads[4], grads[5], grads[6], grads[7], grads[8], grads[9], grads[10])
```

```python
import functools

import jax
import jax.numpy as jnp
import numpy as np
from jax import lax
from jax.experimental import pallas as pl
from jax.experimental.pallas import tpu as pltpu
from jax.sharding import PartitionSpec as P

HEAD = 64
TILE = 128
EPS = 1e-05
THETA = 1000000.0
SCALE = HEAD**-0.5
EXP2_SCALE = SCALE * float(np.log2(np.e))
FAR = -1e30
BF = jnp.bfloat16
F32 = jnp.float32
VMEM_LIMIT = 56 * 1024 * 1024


def dot(left, right, dims):
    return lax.dot_general(left, right, (dims, ((), ())), preferred_element_type=F32)


NN = ((1,), (0,))
NT = ((1,), (1,))
TN = ((0,), (0,))


def swap_cores(value):
    return lax.ppermute(value, "tp", [(0, 1), (1, 0)])


def fsdp_xor(value, mask):
    size = lax.axis_size("fsdp")
    return lax.ppermute(value, "fsdp", [(i, i ^ mask) for i in range(size)])


def ctx_up(value, step=1):
    size = lax.axis_size("ctx")
    return lax.ppermute(value, "ctx", [(i, i + step) for i in range(size - step)])


def ctx_down(value, step=1):
    size = lax.axis_size("ctx")
    return lax.ppermute(value, "ctx", [(i + step, i) for i in range(size - step)])


def ctx_shift(value, step):
    size = lax.axis_size("ctx")
    return lax.ppermute(value, "ctx", [(i, (i + step) % size) for i in range(size)])


def sum_everywhere(value):
    for axis in ("tp", "fsdp", "ctx"):
        size = lax.axis_size(axis)
        step = 1
        while step < size:
            value = value + lax.ppermute(value, axis, [(i, i ^ step) for i in range(size)])
            step *= 2
    return value


def lane_ids(rows):
    return lax.broadcasted_iota(jnp.int32, (rows, TILE), 1)


def half_swap(x):
    low = lane_ids(x.shape[0]) % HEAD < HEAD // 2
    return jnp.where(low, pltpu.roll(x, TILE - HEAD // 2, 1), pltpu.roll(x, HEAD // 2, 1))


def head_mean(x):
    first = lane_ids(x.shape[0]) < HEAD
    left = jnp.sum(jnp.where(first, x, 0.0), axis=1, keepdims=True)
    right = jnp.sum(jnp.where(first, 0.0, x), axis=1, keepdims=True)
    return jnp.where(first, left, right) * (1.0 / HEAD)


def prepare(x, gain, cosine, sine):
    scaled = x * lax.rsqrt(head_mean(x * x) + EPS) * gain
    return scaled * cosine + half_swap(scaled) * sine


def prepare_back(x, gain, cosine, sine, grad):
    grad = grad * cosine - half_swap(grad) * sine
    inverse = lax.rsqrt(head_mean(x * x) + EPS)
    normal = x * inverse
    gain_grad = jnp.sum(grad * normal, axis=0, keepdims=True)
    grad = grad * gain
    return inverse * (grad - normal * head_mean(grad * normal)), gain_grad


def key_bias(scal_ref, slot, keys, block_rows):
    c = scal_ref[0]
    core = scal_ref[1]
    length = scal_ref[2 + slot]
    half = block_rows // 2

    def places(index):
        block = index // block_rows
        side = (index // half) % 2
        return (c - block) * block_rows + (side + core - 2 * side * core) * half + index % half

    key_at = places(lax.broadcasted_iota(jnp.int32, (keys, block_rows), 0))
    query_at = places(lax.broadcasted_iota(jnp.int32, (keys, block_rows), 1))
    seen = (key_at >= 0) & (key_at <= query_at) & (key_at < length)
    return jnp.where(seen, 0.0, FAR)


def twins(x):
    first = lane_ids(x.shape[0]) < HEAD
    turned = pltpu.roll(x, HEAD, 1)
    return jnp.where(first, x, turned).astype(BF), jnp.where(first, turned, x).astype(BF)


def attend_kernel(scal_ref, q_ref, k_ref, v_ref, cos_ref, sin_ref, qg_ref, kg_ref, o_ref, l_ref, qh_ref, kh_ref, bias_ref):
    rows = q_ref.shape[1]
    keys = k_ref.shape[1]

    @pl.when(pl.program_id(1) == 0)
    def _():
        bias_ref[...] = key_bias(scal_ref, pl.program_id(0), keys, rows)

    key = prepare(k_ref[0], kg_ref[...], cos_ref[...], sin_ref[...]).astype(BF)
    kh_ref[0] = key
    key_twins = twins(key.astype(F32))
    value = v_ref[0].astype(F32)
    value_twins = twins(value)
    first = lane_ids(rows) < HEAD
    for pair in range(2):
        lanes = slice(pair * TILE, (pair + 1) * TILE)
        query = prepare(q_ref[0, :, lanes], qg_ref[...], cos_ref[:rows], sin_ref[:rows]).astype(BF)
        qh_ref[0, :, lanes] = query
        turned_value = value_twins[pair].astype(F32).T.astype(BF)
        mixed = []
        for head in range(2):
            mine = first if head == 0 else jnp.logical_not(first)
            scores = dot(key_twins[pair], jnp.where(mine, query, jnp.zeros_like(query)), NT)
            weights = jnp.exp2(scores * EXP2_SCALE + bias_ref[...])
            inverse = 1.0 / jnp.sum(weights, axis=0, keepdims=True)
            l_ref[0, 0, pl.ds(2 * pair + head, 1), :] = inverse
            mixed.append(dot(turned_value, weights.astype(BF), NN) * inverse)
        row_first = lax.broadcasted_iota(jnp.int32, (TILE, rows), 0) < HEAD
        o_ref[0, :, lanes] = jnp.where(row_first, mixed[0], mixed[1]).T.astype(BF)


def attend_back_kernel(
    scal_ref, q_ref, k_ref, v_ref, cos_ref, sin_ref, qg_ref, kg_ref, qh_ref, kh_ref, o_ref, l_ref, d_ref,
    dq_ref, dk_ref, dv_ref, gq_ref, gk_ref, bias_ref
):
    rows = q_ref.shape[1]
    keys = k_ref.shape[1]

    @pl.when(pl.program_id(1) == 0)
    def _():
        bias_ref[...] = key_bias(scal_ref, pl.program_id(0), keys, rows)

    key_twins = twins(kh_ref[0].astype(F32))
    value_twins = twins(v_ref[0].astype(F32))
    first = lane_ids(rows) < HEAD
    key_first = lane_ids(keys) < HEAD
    row_first = lax.broadcasted_iota(jnp.int32, (TILE, rows), 0) < HEAD
    key_grads = []
    value_grads = []
    query_gain = jnp.zeros((1, TILE), F32)
    for pair in range(2):
        lanes = slice(pair * TILE, (pair + 1) * TILE)
        query = qh_ref[0, :, lanes]
        grad = d_ref[0, :, lanes]
        product = (grad.astype(F32) * o_ref[0, :, lanes].astype(F32)).T
        key_grad = jnp.zeros((keys, TILE), F32)
        value_grad = jnp.zeros((keys, TILE), F32)
        query_grads = []
        for head in range(2):
            mine = first if head == 0 else jnp.logical_not(first)
            own_query = jnp.where(mine, query, jnp.zeros_like(query))
            own_grad = jnp.where(mine, grad, jnp.zeros_like(grad))
            inner = jnp.sum(product[head * HEAD : (head + 1) * HEAD], axis=0, keepdims=True)
            inverse = l_ref[0, 0, pl.ds(2 * pair + head, 1), :]
            scores = dot(key_twins[pair], own_query, NT)
            probs = jnp.exp2(scores * EXP2_SCALE + bias_ref[...]) * inverse
            grad_probs = dot(value_twins[pair], own_grad, NT)
            grad_scores = (probs * (grad_probs - inner)).astype(BF)
            query_grads.append(dot(grad_scores, key_twins[pair], TN))
            key_grad = key_grad + dot(grad_scores, own_query, NN)
            value_grad = value_grad + dot(probs.astype(BF), own_grad, NN)
        query_rot = jnp.where(first, query_grads[0], query_grads[1]) * SCALE
        raw, gain_part = prepare_back(q_ref[0, :, lanes], qg_ref[...], cos_ref[:rows], sin_ref[:rows], query_rot)
        dq_ref[0, :, lanes] = raw.astype(BF)
        query_gain = query_gain + gain_part
        key_grads.append(key_grad + pltpu.roll(key_grad, HEAD, 1))
        value_grads.append(value_grad + pltpu.roll(value_grad, HEAD, 1))
    dv_ref[0] = jnp.where(key_first, value_grads[0], value_grads[1]).astype(BF)
    key_rot = jnp.where(key_first, key_grads[0], key_grads[1]) * SCALE
    raw, key_gain = prepare_back(k_ref[0], kg_ref[...], cos_ref[...], sin_ref[...], key_rot)
    dk_ref[0] = raw.astype(BF)

    @pl.when((pl.program_id(0) == 0) & (pl.program_id(1) == 0))
    def _():
        gq_ref[...] = jnp.zeros_like(gq_ref)
        gk_ref[...] = jnp.zeros_like(gk_ref)

    gq_ref[...] += query_gain
    gk_ref[...] += key_gain


def attention_specs(slots, rows, keys):
    smem = pl.BlockSpec(memory_space=pltpu.SMEM)
    query = pl.BlockSpec((1, rows, 2 * TILE), lambda s, p: (s, 0, p))
    key = pl.BlockSpec((1, keys, TILE), lambda s, p: (s, 0, p))
    table = pl.BlockSpec((keys, TILE), lambda s, p: (0, 0))
    gain = pl.BlockSpec((1, TILE), lambda s, p: (0, 0))
    stat = pl.BlockSpec((1, 1, 8, rows), lambda s, p: (s, p, 0, 0))
    return smem, query, key, table, gain, stat


def attend(scal, q_raw, k_raw, value, cosine, sine, query_gain, key_gain):
    slots, rows, width = q_raw.shape
    keys, kv_width = k_raw.shape[1:]
    smem, query, key, table, gain, stat = attention_specs(slots, rows, keys)
    pairs = kv_width // TILE
    return pl.pallas_call(
        attend_kernel,
        grid=(slots, pairs),
        in_specs=[smem, query, key, key, table, table, gain, gain],
        out_specs=[query, stat, query, key],
        out_shape=[
            jax.ShapeDtypeStruct((slots, rows, width), BF),
            jax.ShapeDtypeStruct((slots, pairs, 8, rows), F32),
            jax.ShapeDtypeStruct((slots, rows, width), BF),
            jax.ShapeDtypeStruct((slots, keys, kv_width), BF),
        ],
        scratch_shapes=[pltpu.VMEM((keys, rows), F32)],
        compiler_params=pltpu.CompilerParams(vmem_limit_bytes=VMEM_LIMIT),
        cost_estimate=pl.CostEstimate(
            flops=8 * slots * rows * keys * width, bytes_accessed=8 << 20, transcendentals=slots * rows * keys * width // HEAD
        ),
        name="attend",
    )(scal, q_raw, k_raw, value, cosine, sine, query_gain, key_gain)


def attend_back(scal, q_raw, k_raw, value, cosine, sine, query_gain, key_gain, q_hat, k_hat, out, stats, grad):
    slots, rows, width = q_raw.shape
    keys, kv_width = k_raw.shape[1:]
    smem, query, key, table, gain, stat = attention_specs(slots, rows, keys)
    pairs = kv_width // TILE
    return pl.pallas_call(
        attend_back_kernel,
        grid=(slots, pairs),
        in_specs=[smem, query, key, key, table, table, gain, gain, query, key, query, stat, query],
        out_specs=[query, key, key, gain, gain],
        out_shape=[
            jax.ShapeDtypeStruct((slots, rows, width), BF),
            jax.ShapeDtypeStruct((slots, keys, kv_width), BF),
            jax.ShapeDtypeStruct((slots, keys, kv_width), BF),
            jax.ShapeDtypeStruct((1, TILE), F32),
            jax.ShapeDtypeStruct((1, TILE), F32),
        ],
        scratch_shapes=[pltpu.VMEM((keys, rows), F32)],
        compiler_params=pltpu.CompilerParams(vmem_limit_bytes=VMEM_LIMIT),
        cost_estimate=pl.CostEstimate(
            flops=20 * slots * rows * keys * width, bytes_accessed=12 << 20, transcendentals=slots * rows * keys * width // HEAD
        ),
        name="attend_back",
    )(scal, q_raw, k_raw, value, cosine, sine, query_gain, key_gain, q_hat, k_hat, out, stats, grad)


def ffn_kernel(x_ref, g_ref, w_ref, y_ref, dx_ref, grad_ref, sum_ref):
    units = w_ref.shape[1] // 3
    step = pl.program_id(0)
    x = x_ref[...]
    g = g_ref[...]
    raised = dot(x, w_ref[:, : 2 * units], NN)
    gate = raised[:, :units]
    upper = raised[:, units:]
    sig = 1.0 / (1.0 + jnp.exp(-gate))
    silu = gate * sig
    act = (silu * upper).astype(BF)
    y_ref[...] = dot(act, w_ref[:, 2 * units :], NT).astype(BF)
    d_act = dot(g, w_ref[:, 2 * units :], NN)
    d_gate = (d_act * upper * (sig + silu * (1.0 - sig))).astype(BF)
    d_up = (d_act * silu).astype(BF)
    both = jnp.concatenate([d_gate, d_up], axis=1)
    dx_ref[...] = dot(both, w_ref[:, : 2 * units], NT).astype(BF)
    left = dot(x, both, TN)
    right = dot(g, act, TN)

    @pl.when(step == 0)
    def _():
        sum_ref[:, : 2 * units] = left
        sum_ref[:, 2 * units :] = right

    @pl.when(step > 0)
    def _():
        sum_ref[:, : 2 * units] += left
        sum_ref[:, 2 * units :] += right

    @pl.when(step == pl.num_programs(0) - 1)
    def _():
        grad_ref[...] = sum_ref[...].astype(BF)


def feed_forward(x, g, w, rows):
    tokens, width = x.shape
    units3 = w.shape[1]
    block = pl.BlockSpec((rows, width), lambda i: (i, 0))
    whole = pl.BlockSpec((width, units3), lambda i: (0, 0))
    return pl.pallas_call(
        ffn_kernel,
        grid=(tokens // rows,),
        in_specs=[block, block, whole],
        out_specs=[block, block, whole],
        out_shape=[
            jax.ShapeDtypeStruct((tokens, width), BF),
            jax.ShapeDtypeStruct((tokens, width), BF),
            jax.ShapeDtypeStruct((width, units3), BF),
        ],
        scratch_shapes=[pltpu.VMEM((width, units3), F32)],
        compiler_params=pltpu.CompilerParams(vmem_limit_bytes=VMEM_LIMIT),
        cost_estimate=pl.CostEstimate(
            flops=6 * tokens * width * units3, bytes_accessed=24 << 20, transcendentals=tokens * units3 // 3
        ),
        name="feed_forward",
    )(x, g, w)


def inverse_rms(values):
    return lax.rsqrt(jnp.mean(values * values, axis=-1, keepdims=True) + EPS)


def norm_back(values, gain, grad):
    inverse = inverse_rms(values)
    normal = values * inverse
    scaled = grad * gain
    return inverse * (scaled - normal * jnp.mean(scaled * normal, axis=-1, keepdims=True))


def body(
    hidden_in,
    seq_lengths,
    attn_gain,
    query_gain,
    key_gain,
    query_weight,
    key_projection,
    value_projection,
    out_weight,
    ffn_gain,
    gate_weight,
    up_weight,
    down_weight,
    cotangent,
):
    slots, shard_rows, width = hidden_in.shape
    n_fsdp = lax.axis_size("fsdp")
    n_ctx = lax.axis_size("ctx")
    f = lax.axis_index("fsdp")
    c = lax.axis_index("ctx")
    core = lax.axis_index("tp")
    rows = 2 * shard_rows
    keys = n_ctx * rows
    q_cols = query_weight.shape[1]
    k_cols = key_projection.shape[1]
    shard = query_weight.shape[0]
    ff_half = gate_weight.shape[1]
    units = ff_half // n_fsdp
    padded = -(-units // TILE) * TILE

    at = jnp.arange(keys)
    places = (c - at // rows) * rows + ((at // shard_rows) % 2 ^ core) * shard_rows + at % shard_rows
    lanes = jnp.arange(TILE)
    freqs = THETA ** (-((lanes % (HEAD // 2)).astype(F32) * 2.0 / HEAD))
    angles = places.astype(F32)[:, None] * freqs[None, :]
    cosine = jnp.cos(angles)
    sine = jnp.sin(angles) * jnp.where(lanes % HEAD < HEAD // 2, -1.0, 1.0)[None, :]
    scal = jnp.concatenate([jnp.stack([c, core]).astype(jnp.int32), seq_lengths])
    own_places = places[:shard_rows]
    valid = own_places[None, :, None] < seq_lengths[:, None, None]

    hidden = hidden_in.astype(F32)
    inverse_one = inverse_rms(hidden)
    normed = (hidden * inverse_one * attn_gain).astype(BF)

    packed = jnp.concatenate([query_weight, key_projection, value_projection, out_weight.T], axis=1)
    stack = jnp.zeros((n_ctx,) + packed.shape, BF)
    stack = lax.dynamic_update_index_in_dim(stack, packed, c, 0)
    for k in range(1, n_ctx):
        stack = lax.dynamic_update_index_in_dim(stack, ctx_shift(packed, k), (c - k) % n_ctx, 0)
    stack = stack.reshape(n_ctx * shard, -1)
    full = jnp.zeros((n_fsdp,) + stack.shape, BF)
    full = lax.dynamic_update_index_in_dim(full, stack, f, 0)
    for m in range(1, n_fsdp):
        full = lax.dynamic_update_index_in_dim(full, fsdp_xor(stack, m), f ^ m, 0)
    attn_w = full.reshape(width, -1)
    query_w = attn_w[:, :q_cols]
    kv_w = attn_w[:, q_cols : q_cols + 2 * k_cols]
    out_w = attn_w[:, q_cols + 2 * k_cols :]

    def quarters(array):
        array = array.reshape(shard, n_fsdp, units)
        return jnp.pad(array, ((0, 0), (0, 0), (0, padded - units)))

    ffn_packed = jnp.concatenate(
        [quarters(gate_weight), quarters(up_weight), quarters(down_weight.T)], axis=2
    ).transpose(1, 0, 2)
    ffn_rows = jnp.zeros_like(ffn_packed)
    ffn_rows = lax.dynamic_update_index_in_dim(
        ffn_rows, lax.dynamic_index_in_dim(ffn_packed, f, 0, keepdims=False), f, 0
    )
    for m in range(1, n_fsdp):
        piece = fsdp_xor(lax.dynamic_index_in_dim(ffn_packed, f ^ m, 0, keepdims=False), m)
        ffn_rows = lax.dynamic_update_index_in_dim(ffn_rows, piece, f ^ m, 0)
    ffn_w = lax.all_gather(ffn_rows, "ctx", axis=1, tiled=True).reshape(width, 3 * padded)

    blocks = []
    for r in range(n_ctx):
        piece = ctx_up(normed, r) if r else normed
        blocks.append(jnp.concatenate([piece, swap_cores(piece)], axis=1))
    x_all = jnp.concatenate(blocks, axis=1)
    x_own = blocks[0]

    q_raw = jnp.einsum("std,dh->sth", x_own, query_w, preferred_element_type=F32)
    k_raw = jnp.einsum("std,dh->sth", x_all, kv_w[:, :k_cols], preferred_element_type=F32)
    value = jnp.einsum("std,dh->sth", x_all, kv_w[:, k_cols:], preferred_element_type=F32).astype(BF)
    query_gain2 = jnp.tile(query_gain, 2)[None, :]
    key_gain2 = jnp.tile(key_gain, 2)[None, :]
    attn, stats, q_hat, k_hat = attend(scal, q_raw, k_raw, value, cosine, sine, query_gain2, key_gain2)

    branch = jnp.einsum("sth,dh->std", attn, out_w, preferred_element_type=F32)
    middle = hidden + (branch[:, :shard_rows] + swap_cores(branch[:, shard_rows:]))
    normed_two = (middle * inverse_rms(middle) * ffn_gain).astype(BF)
    grad_rows = jnp.where(valid, cotangent, jnp.zeros_like(cotangent))

    def gather_tokens(value):
        pieces = jnp.stack([value] + [fsdp_xor(value, m) for m in range(1, n_fsdp)])
        return jnp.concatenate([pieces, swap_cores(pieces)]).reshape(-1, width)

    def scatter_tokens(value):
        value = value.reshape(2, n_fsdp, slots, shard_rows, width)
        mine = value[0].astype(F32) + swap_cores(value[1]).astype(F32)
        total = mine[0]
        for m in range(1, n_fsdp):
            total = total + fsdp_xor(mine[m].astype(BF), m).astype(F32)
        return total

    y_part, dx_part, ffn_grads = feed_forward(gather_tokens(normed_two), gather_tokens(grad_rows), ffn_w, 2 * slots * shard_rows)
    result = jnp.where(valid, middle + scatter_tokens(y_part), 0.0).astype(BF)
    d_normed_two = scatter_tokens(dx_part)
    d_middle = grad_rows.astype(F32) + norm_back(middle, ffn_gain, d_normed_two)

    reduced = lax.psum_scatter(
        ffn_grads.reshape(n_fsdp, n_ctx * shard, 3 * padded), "ctx", scatter_dimension=1, tiled=True
    )
    ffn_out = jnp.zeros((n_fsdp,) + reduced.shape[1:], BF)
    ffn_out = lax.dynamic_update_index_in_dim(
        ffn_out, lax.dynamic_index_in_dim(reduced, f, 0, keepdims=False), f, 0
    )
    for m in range(1, n_fsdp):
        piece = fsdp_xor(lax.dynamic_index_in_dim(reduced, f ^ m, 0, keepdims=False), m)
        ffn_out = lax.dynamic_update_index_in_dim(ffn_out, piece, f ^ m, 0)
    ffn_out = ffn_out.reshape(n_fsdp, shard, 3, padded)[..., :units].astype(F32)
    ffn_out = ffn_out.transpose(2, 1, 0, 3).reshape(3, shard, ff_half)
    gate_grad, up_grad = ffn_out[0], ffn_out[1]
    down_grad = ffn_out[2].T

    d_branch = d_middle.astype(BF)
    d_branch = jnp.concatenate([d_branch, swap_cores(d_branch)], axis=1)
    d_attn = jnp.einsum("std,dh->sth", d_branch, out_w, preferred_element_type=F32).astype(BF)
    out_w_grad = jnp.einsum("std,sth->dh", d_branch, attn, preferred_element_type=F32)
    d_q, d_k, d_v, gq, gk = attend_back(
        scal, q_raw, k_raw, value, cosine, sine, query_gain2, key_gain2, q_hat, k_hat, attn, stats, d_attn
    )
    d_kv = jnp.concatenate([d_k, d_v], axis=2)
    d_own = jnp.einsum("sth,dh->std", d_q, query_w, preferred_element_type=F32)
    d_all = jnp.einsum("sth,dh->std", d_kv, kv_w, preferred_element_type=F32)
    d_all = d_all.at[:, :rows].add(d_own).reshape(slots, n_ctx, 2, shard_rows, width)
    mine = d_all[:, :, 0] + swap_cores(d_all[:, :, 1].astype(BF)).astype(F32)
    total = mine[:, n_ctx - 1]
    for r in range(n_ctx - 2, -1, -1):
        total = mine[:, r] + ctx_down(total.astype(BF)).astype(F32)
    input_grad = (d_middle + norm_back(hidden, attn_gain, total)).astype(BF)

    q_grad = jnp.einsum("std,sth->dh", x_own, d_q, preferred_element_type=F32)
    kv_grad = jnp.einsum("std,sth->dh", x_all, d_kv, preferred_element_type=F32)
    attn_grads = jnp.concatenate([q_grad, kv_grad, out_w_grad], axis=1)
    sends = attn_grads.astype(BF).reshape(n_fsdp, n_ctx * shard, -1)
    total = lax.dynamic_index_in_dim(sends, f, 0, keepdims=False).astype(F32)
    for m in range(1, n_fsdp):
        total = total + fsdp_xor(lax.dynamic_index_in_dim(sends, f ^ m, 0, keepdims=False), m).astype(F32)
    sends = total.reshape(n_ctx, shard, -1)
    total = lax.dynamic_index_in_dim(sends, c, 0, keepdims=False)
    sends = sends.astype(BF)
    for k in range(1, n_ctx):
        total = total + ctx_shift(lax.dynamic_index_in_dim(sends, (c + k) % n_ctx, 0, keepdims=False), k).astype(F32)
    query_weight_grad = total[:, :q_cols]
    key_weight_grad = total[:, q_cols : q_cols + k_cols]
    value_weight_grad = total[:, q_cols + k_cols : q_cols + 2 * k_cols]
    out_weight_grad = total[:, q_cols + 2 * k_cols :].T

    attn_gain_part = jnp.sum(attn_w[:, : q_cols + 2 * k_cols].astype(F32) * attn_grads[:, : q_cols + 2 * k_cols], axis=1) / attn_gain
    ffn_gain_part = (
        jnp.sum(ffn_w[:, : 2 * padded].astype(F32) * ffn_grads[:, : 2 * padded].astype(F32), axis=1) / ffn_gain
    )
    small = jnp.concatenate(
        [attn_gain_part, ffn_gain_part, gq[0, :HEAD] + gq[0, HEAD:], gk[0, :HEAD] + gk[0, HEAD:]]
    )
    small = sum_everywhere(small)
    return (
        result,
        input_grad,
        small[:width],
        small[2 * width : 2 * width + HEAD],
        small[2 * width + HEAD :],
        query_weight_grad,
        key_weight_grad,
        value_weight_grad,
        out_weight_grad,
        small[width : 2 * width],
        gate_grad,
        up_grad,
        down_grad,
    )


def solution(mesh):
    in_specs = (
        P("fsdp", ("ctx", "tp"), None),
        P("fsdp"),
        P(),
        P(),
        P(),
        P(("fsdp", "ctx"), "tp"),
        P(("fsdp", "ctx"), "tp"),
        P(("fsdp", "ctx"), "tp"),
        P("tp", ("fsdp", "ctx")),
        P(),
        P(("fsdp", "ctx"), "tp"),
        P(("fsdp", "ctx"), "tp"),
        P("tp", ("fsdp", "ctx")),
        P("fsdp", ("ctx", "tp"), None),
    )
    out_specs = (
        P("fsdp", ("ctx", "tp"), None),
        P("fsdp", ("ctx", "tp"), None),
        P(),
        P(),
        P(),
        P(("fsdp", "ctx"), "tp"),
        P(("fsdp", "ctx"), "tp"),
        P(("fsdp", "ctx"), "tp"),
        P("tp", ("fsdp", "ctx")),
        P(),
        P(("fsdp", "ctx"), "tp"),
        P(("fsdp", "ctx"), "tp"),
        P("tp", ("fsdp", "ctx")),
    )
    return jax.shard_map(body, mesh=mesh, in_specs=in_specs, out_specs=out_specs, check_vma=False)
```

```python
import functools

import jax
import jax.numpy as jnp
import numpy as np
from jax import lax
from jax.experimental import pallas as pl
from jax.experimental.pallas import tpu as pltpu
from jax.sharding import PartitionSpec as P

HEAD = 64
TILE = 128
EPS = 1e-05
THETA = 1000000.0
SCALE = HEAD**-0.5
EXP2_SCALE = SCALE * float(np.log2(np.e))
FAR = -1e30
BF = jnp.bfloat16
F32 = jnp.float32
VMEM_LIMIT = 56 * 1024 * 1024


def dot(left, right, dims):
    return lax.dot_general(left, right, (dims, ((), ())), preferred_element_type=F32)


NN = ((1,), (0,))
NT = ((1,), (1,))
TN = ((0,), (0,))


def swap_cores(value):
    return lax.ppermute(value, "tp", [(0, 1), (1, 0)])


def fsdp_xor(value, mask):
    size = lax.axis_size("fsdp")
    return lax.ppermute(value, "fsdp", [(i, i ^ mask) for i in range(size)])


def ctx_up(value, step=1):
    size = lax.axis_size("ctx")
    return lax.ppermute(value, "ctx", [(i, i + step) for i in range(size - step)])


def ctx_down(value, step=1):
    size = lax.axis_size("ctx")
    return lax.ppermute(value, "ctx", [(i + step, i) for i in range(size - step)])


def ctx_shift(value, step):
    size = lax.axis_size("ctx")
    return lax.ppermute(value, "ctx", [(i, (i + step) % size) for i in range(size)])


def tree_sum(values):
    while len(values) > 1:
        half = len(values) // 2
        values = [values[i] + values[i + half] for i in range(half)]
    return values[0]


def two_parts(rows):
    first = rows.astype(BF)
    left = (rows - first.astype(F32)).astype(BF)
    return jnp.pad(jnp.concatenate([first, left]), ((0, 16 - 2 * rows.shape[0]), (0, 0)))


def one_part(rows):
    return rows[:2].astype(F32) + rows[2:4].astype(F32)


def tie(*values):
    return lax.optimization_barrier(values)


def lane_ids(rows):
    return lax.broadcasted_iota(jnp.int32, (rows, TILE), 1)


def half_swap(x):
    low = lane_ids(x.shape[0]) % HEAD < HEAD // 2
    return jnp.where(low, pltpu.roll(x, TILE - HEAD // 2, 1), pltpu.roll(x, HEAD // 2, 1))


def head_mean(x):
    first = lane_ids(x.shape[0]) < HEAD
    left = jnp.sum(jnp.where(first, x, 0.0), axis=1, keepdims=True)
    right = jnp.sum(jnp.where(first, 0.0, x), axis=1, keepdims=True)
    return jnp.where(first, left, right) * (1.0 / HEAD)


def prepare(x, gain, cosine, sine):
    scaled = x * lax.rsqrt(head_mean(x * x) + EPS) * gain
    return scaled * cosine + half_swap(scaled) * sine


def prepare_back(x, gain, cosine, sine, grad):
    grad = grad * cosine - half_swap(grad) * sine
    inverse = lax.rsqrt(head_mean(x * x) + EPS)
    normal = x * inverse
    gain_grad = jnp.sum(grad * normal, axis=0, keepdims=True)
    grad = grad * gain
    return inverse * (grad - normal * head_mean(grad * normal)), gain_grad


def key_bias(scal_ref, slot, keys, block_rows):
    c = scal_ref[0]
    core = scal_ref[1]
    length = scal_ref[3 + slot]
    half = block_rows // 2

    def places(index):
        block = index // block_rows
        side = (index // half) % 2
        return (c - block) * block_rows + (side + core - 2 * side * core) * half + index % half

    key_at = places(lax.broadcasted_iota(jnp.int32, (keys, block_rows), 0))
    query_at = places(lax.broadcasted_iota(jnp.int32, (keys, block_rows), 1))
    seen = (key_at >= 0) & (key_at <= query_at) & (key_at < length)
    return jnp.where(seen, 0.0, FAR)


def twins(x):
    first = lane_ids(x.shape[0]) < HEAD
    turned = pltpu.roll(x, HEAD, 1)
    return jnp.where(first, x, turned).astype(BF), jnp.where(first, turned, x).astype(BF)


def attend_kernel(n_pieces, n_parts, scal_ref, *refs):
    pieces = refs[:n_pieces]
    (
        tq_ref, tk_ref, tv_ref, bq_ref, bk_ref, bv_ref, cos_ref, sin_ref, qg_ref, kg_ref,
        o_ref, l_ref, qr_ref, kr_ref, v_ref, qh_ref, kh_ref, x_ref, bias_ref, wq_ref, wkv_ref,
    ) = refs[n_pieces:]
    rows = qr_ref.shape[1]
    keys = kr_ref.shape[1]
    half = rows // 2

    @pl.when(pl.program_id(1) == 0)
    def _():
        bias_ref[...] = key_bias(scal_ref, pl.program_id(0), keys, rows)
        for i, piece in enumerate(pieces):
            x_ref[0, i * half : (i + 1) * half] = piece[0]

    depth = tq_ref.shape[1]
    bits = [1 << i for i in range(8) if 1 << i < n_parts]
    for side, (query_w, key_w, value_w) in enumerate(((tq_ref, tk_ref, tv_ref), (bq_ref, bk_ref, bv_ref))):
        order = bits[::-1] if side else bits
        for i in range(n_parts):
            mask = sum(bit for j, bit in enumerate(order) if i >> j & 1)
            at = pl.ds(pl.multiple_of(((scal_ref[2] ^ mask) * 2 + side) * depth, depth), depth)
            wq_ref[at, :] = query_w[i]
            wkv_ref[at, :TILE] = key_w[i]
            wkv_ref[at, TILE:] = value_w[i]
    key_value = dot(x_ref[0], wkv_ref[...], NN)
    query_raw = dot(x_ref[0, :rows], wq_ref[...], NN)
    kr_ref[0] = key_value[:, :TILE]
    v_ref[0] = key_value[:, TILE:].astype(BF)
    qr_ref[0] = query_raw

    key = prepare(kr_ref[0], kg_ref[...], cos_ref[...], sin_ref[...]).astype(BF)
    kh_ref[0] = key
    key_twins = twins(key.astype(F32))
    value_twins = twins(v_ref[0].astype(F32))
    first = lane_ids(rows) < HEAD
    for pair in range(2):
        lanes = slice(pair * TILE, (pair + 1) * TILE)
        query = prepare(qr_ref[0, :, lanes], qg_ref[...], cos_ref[:rows], sin_ref[:rows]).astype(BF)
        qh_ref[0, :, lanes] = query
        turned_value = value_twins[pair].astype(F32).T.astype(BF)
        mixed = []
        for head in range(2):
            mine = first if head == 0 else jnp.logical_not(first)
            scores = dot(key_twins[pair], jnp.where(mine, query, jnp.zeros_like(query)), NT)
            weights = jnp.exp2(scores * EXP2_SCALE + bias_ref[...])
            inverse = 1.0 / jnp.sum(weights, axis=0, keepdims=True)
            l_ref[0, 0, pl.ds(2 * pair + head, 1), :] = inverse
            mixed.append(dot(turned_value, weights.astype(BF), NN) * inverse)
        row_first = lax.broadcasted_iota(jnp.int32, (TILE, rows), 0) < HEAD
        o_ref[0, :, lanes] = jnp.where(row_first, mixed[0], mixed[1]).T.astype(BF)


def attend_back_kernel(
    scal_ref, q_ref, k_ref, v_ref, cos_ref, sin_ref, qg_ref, kg_ref, qh_ref, kh_ref, o_ref, l_ref, d_ref,
    dq_ref, dk_ref, dv_ref, gq_ref, gk_ref, bias_ref
):
    rows = q_ref.shape[1]
    keys = k_ref.shape[1]

    @pl.when(pl.program_id(1) == 0)
    def _():
        bias_ref[...] = key_bias(scal_ref, pl.program_id(0), keys, rows)

    key_twins = twins(kh_ref[0].astype(F32))
    value_twins = twins(v_ref[0].astype(F32))
    first = lane_ids(rows) < HEAD
    key_first = lane_ids(keys) < HEAD
    row_first = lax.broadcasted_iota(jnp.int32, (TILE, rows), 0) < HEAD
    key_grads = []
    value_grads = []
    query_gain = jnp.zeros((1, TILE), F32)
    for pair in range(2):
        lanes = slice(pair * TILE, (pair + 1) * TILE)
        query = qh_ref[0, :, lanes]
        grad = d_ref[0, :, lanes]
        product = (grad.astype(F32) * o_ref[0, :, lanes].astype(F32)).T
        key_grad = jnp.zeros((keys, TILE), F32)
        value_grad = jnp.zeros((keys, TILE), F32)
        query_grads = []
        for head in range(2):
            mine = first if head == 0 else jnp.logical_not(first)
            own_query = jnp.where(mine, query, jnp.zeros_like(query))
            own_grad = jnp.where(mine, grad, jnp.zeros_like(grad))
            inner = jnp.sum(product[head * HEAD : (head + 1) * HEAD], axis=0, keepdims=True)
            inverse = l_ref[0, 0, pl.ds(2 * pair + head, 1), :]
            scores = dot(key_twins[pair], own_query, NT)
            probs = jnp.exp2(scores * EXP2_SCALE + bias_ref[...]) * inverse
            grad_probs = dot(value_twins[pair], own_grad, NT)
            grad_scores = (probs * (grad_probs - inner)).astype(BF)
            query_grads.append(dot(grad_scores, key_twins[pair], TN))
            key_grad = key_grad + dot(grad_scores, own_query, NN)
            value_grad = value_grad + dot(probs.astype(BF), own_grad, NN)
        query_rot = jnp.where(first, query_grads[0], query_grads[1]) * SCALE
        raw, gain_part = prepare_back(q_ref[0, :, lanes], qg_ref[...], cos_ref[:rows], sin_ref[:rows], query_rot)
        dq_ref[0, :, lanes] = raw.astype(BF)
        query_gain = query_gain + gain_part
        key_grads.append(key_grad + pltpu.roll(key_grad, HEAD, 1))
        value_grads.append(value_grad + pltpu.roll(value_grad, HEAD, 1))
    dv_ref[0] = jnp.where(key_first, value_grads[0], value_grads[1]).astype(BF)
    key_rot = jnp.where(key_first, key_grads[0], key_grads[1]) * SCALE
    raw, key_gain = prepare_back(k_ref[0], kg_ref[...], cos_ref[...], sin_ref[...], key_rot)
    dk_ref[0] = raw.astype(BF)

    @pl.when((pl.program_id(0) == 0) & (pl.program_id(1) == 0))
    def _():
        gq_ref[...] = jnp.zeros_like(gq_ref)
        gk_ref[...] = jnp.zeros_like(gk_ref)

    gq_ref[...] += query_gain
    gk_ref[...] += key_gain


def attention_specs(slots, rows, keys):
    smem = pl.BlockSpec(memory_space=pltpu.SMEM)
    query = pl.BlockSpec((1, rows, 2 * TILE), lambda s, p: (s, 0, p))
    key = pl.BlockSpec((1, keys, TILE), lambda s, p: (s, 0, p))
    table = pl.BlockSpec((keys, TILE), lambda s, p: (0, 0))
    gain = pl.BlockSpec((1, TILE), lambda s, p: (0, 0))
    stat = pl.BlockSpec((1, 1, 8, rows), lambda s, p: (s, p, 0, 0))
    return smem, query, key, table, gain, stat


def attend(scal, pieces, weights, widths, cosine, sine, query_gain, key_gain):
    width, kv_width = widths
    slots, half, model = pieces[0].shape
    rows = 2 * half
    keys = len(pieces) * half
    smem, query, key, table, gain, stat = attention_specs(slots, rows, keys)
    pairs = kv_width // TILE
    piece = pl.BlockSpec((1, half, model), lambda s, p: (s, 0, 0))
    parts, depth = weights[0].shape[:2]
    w_query = pl.BlockSpec((parts, depth, 2 * TILE), lambda s, p: (0, 0, p))
    w_key = pl.BlockSpec((parts, depth, TILE), lambda s, p: (0, 0, width // TILE + p))
    w_value = pl.BlockSpec((parts, depth, TILE), lambda s, p: (0, 0, (width + kv_width) // TILE + p))
    return pl.pallas_call(
        functools.partial(attend_kernel, len(pieces), parts),
        grid=(slots, pairs),
        in_specs=[smem] + [piece] * len(pieces) + [w_query, w_key, w_value] * 2 + [table, table, gain, gain],
        out_specs=[query, stat, query, key, key, query, key, pl.BlockSpec((1, keys, model), lambda s, p: (s, 0, 0))],
        out_shape=[
            jax.ShapeDtypeStruct((slots, rows, width), BF),
            jax.ShapeDtypeStruct((slots, pairs, 8, rows), F32),
            jax.ShapeDtypeStruct((slots, rows, width), F32),
            jax.ShapeDtypeStruct((slots, keys, kv_width), F32),
            jax.ShapeDtypeStruct((slots, keys, kv_width), BF),
            jax.ShapeDtypeStruct((slots, rows, width), BF),
            jax.ShapeDtypeStruct((slots, keys, kv_width), BF),
            jax.ShapeDtypeStruct((slots, keys, model), BF),
        ],
        scratch_shapes=[
            pltpu.VMEM((keys, rows), F32),
            pltpu.VMEM((model, 2 * TILE), BF),
            pltpu.VMEM((model, 2 * TILE), BF),
        ],
        compiler_params=pltpu.CompilerParams(vmem_limit_bytes=VMEM_LIMIT),
        cost_estimate=pl.CostEstimate(flops=1 << 20, bytes_accessed=1 << 20, transcendentals=0),
        name="attend",
    )(scal, *pieces, *[item for item in weights for _ in range(3)], cosine, sine, query_gain, key_gain)


def attend_back(scal, q_raw, k_raw, value, cosine, sine, query_gain, key_gain, q_hat, k_hat, out, stats, grad):
    slots, rows, width = q_raw.shape
    keys, kv_width = k_raw.shape[1:]
    smem, query, key, table, gain, stat = attention_specs(slots, rows, keys)
    pairs = kv_width // TILE
    return pl.pallas_call(
        attend_back_kernel,
        grid=(slots, pairs),
        in_specs=[smem, query, key, key, table, table, gain, gain, query, key, query, stat, query],
        out_specs=[query, key, key, gain, gain],
        out_shape=[
            jax.ShapeDtypeStruct((slots, rows, width), BF),
            jax.ShapeDtypeStruct((slots, keys, kv_width), BF),
            jax.ShapeDtypeStruct((slots, keys, kv_width), BF),
            jax.ShapeDtypeStruct((1, TILE), F32),
            jax.ShapeDtypeStruct((1, TILE), F32),
        ],
        scratch_shapes=[pltpu.VMEM((keys, rows), F32)],
        compiler_params=pltpu.CompilerParams(vmem_limit_bytes=VMEM_LIMIT),
        cost_estimate=pl.CostEstimate(
            flops=20 * slots * rows * keys * width, bytes_accessed=12 << 20, transcendentals=slots * rows * keys * width // HEAD
        ),
        name="attend_back",
    )(scal, q_raw, k_raw, value, cosine, sine, query_gain, key_gain, q_hat, k_hat, out, stats, grad)


def weight_kernel(at_ref, x_ref, dq_ref, dk_ref, dv_ref, b_ref, o_ref, more_ref, *out_refs):
    slots, rows, q_cols = dq_ref.shape
    k_cols = dk_ref.shape[2]
    total = jnp.zeros((x_ref.shape[2], q_cols), F32)
    key_total = jnp.zeros((x_ref.shape[2], k_cols), F32)
    value_total = jnp.zeros((x_ref.shape[2], k_cols), F32)
    out_total = jnp.zeros((x_ref.shape[2], q_cols), F32)
    for s in range(slots):
        out_total = out_total + dot(b_ref[s], o_ref[s], TN)
        x = x_ref[s]
        total = total + dot(x[:rows], dq_ref[s], TN)
        key_total = key_total + dot(x, dk_ref[s], TN)
        value_total = value_total + dot(x, dv_ref[s], TN)
    depth = x_ref.shape[2]
    for m, ref in enumerate(out_refs):

        @pl.when(pl.program_id(0) == m)
        def _(ref=ref):
            ref[:depth, :q_cols] = total.astype(BF)
            ref[:depth, q_cols : q_cols + k_cols] = key_total.astype(BF)
            ref[:depth, q_cols + k_cols : q_cols + 2 * k_cols] = value_total.astype(BF)
            ref[:depth, q_cols + 2 * k_cols :] = out_total.astype(BF)
            ref[depth:] = more_ref[...]


def weight_grads(at, x, d_q, d_k, d_v, d_branch, attn, more, parts):
    slots, keys, width = x.shape
    cols = 2 * d_q.shape[2] + 2 * d_k.shape[2]
    depth = width // parts + more.shape[0]
    spec = pltpu.PrefetchScalarGridSpec(
        num_scalar_prefetch=1,
        grid=(parts,),
        in_specs=[
            pl.BlockSpec((slots, keys, width // parts), lambda m, at: (0, 0, at[0] ^ m)),
            pl.BlockSpec(d_q.shape, lambda m, at: (0, 0, 0)),
            pl.BlockSpec(d_k.shape, lambda m, at: (0, 0, 0)),
            pl.BlockSpec(d_v.shape, lambda m, at: (0, 0, 0)),
            pl.BlockSpec(d_branch.shape[:2] + (width // parts,), lambda m, at: (0, 0, at[0] ^ m)),
            pl.BlockSpec(attn.shape, lambda m, at: (0, 0, 0)),
            pl.BlockSpec(more.shape, lambda m, at: (0, 0)),
        ],
        out_specs=[pl.BlockSpec((depth, cols), lambda m, at: (0, 0))] * parts,
    )
    return pl.pallas_call(
        weight_kernel,
        grid_spec=spec,
        out_shape=[jax.ShapeDtypeStruct((depth, cols), BF)] * parts,
        compiler_params=pltpu.CompilerParams(vmem_limit_bytes=VMEM_LIMIT),
        cost_estimate=pl.CostEstimate(flops=4 << 30, bytes_accessed=8 << 20, transcendentals=0),
        name="weight_grads",
    )(at, x, d_q, d_k, d_v, d_branch, attn, more)


def input_kernel(dq_ref, dk_ref, dv_ref, x_ref, w_ref, mine_ref, other_ref, gain_ref):
    slots, rows, q_cols = dq_ref.shape
    k_cols = dk_ref.shape[2]
    half = rows // 2
    gain = jnp.zeros((1, x_ref.shape[2]), F32)
    for s in range(slots):
        d_x = dot(dk_ref[s], w_ref[:, q_cols : q_cols + k_cols], NT)
        d_x = d_x + dot(dv_ref[s], w_ref[:, q_cols + k_cols : q_cols + 2 * k_cols], NT)
        gain = gain + jnp.sum(d_x * x_ref[s].astype(F32), axis=0, keepdims=True)
        mine_ref[0, s] = d_x[:half]
        other_ref[0, s] = d_x[half:].astype(BF)

    @pl.when(pl.program_id(0) == 0)
    def _():
        more = jnp.zeros_like(gain)
        for s in range(slots):
            d_x = dot(dq_ref[s], w_ref[:, :q_cols], NT)
            more = more + jnp.sum(d_x * x_ref[s].astype(F32), axis=0, keepdims=True)
            mine_ref[0, s] += d_x[:half]
            other_ref[0, s] = (other_ref[0, s].astype(F32) + d_x[half:]).astype(BF)
        gain_ref[...] = gain + more

    @pl.when(pl.program_id(0) > 0)
    def _():
        gain_ref[...] += gain


def input_grads(d_q, d_k, d_v, x, w):
    slots, rows, q_cols = d_q.shape
    keys, k_cols = d_k.shape[1:]
    width = w.shape[0]
    blocks = keys // rows
    part = pl.BlockSpec((slots, rows, k_cols), lambda r: (0, r, 0))
    out = pl.BlockSpec((1, slots, rows // 2, width), lambda r: (r, 0, 0, 0))
    return pl.pallas_call(
        input_kernel,
        grid=(blocks,),
        in_specs=[
            pl.BlockSpec(d_q.shape, lambda r: (0, 0, 0)),
            part,
            part,
            pl.BlockSpec((slots, rows, width), lambda r: (0, r, 0)),
            pl.BlockSpec(w.shape, lambda r: (0, 0)),
        ],
        out_specs=[out, out, pl.BlockSpec((1, width), lambda r: (0, 0))],
        out_shape=[
            jax.ShapeDtypeStruct((blocks, slots, rows // 2, width), F32),
            jax.ShapeDtypeStruct((blocks, slots, rows // 2, width), BF),
            jax.ShapeDtypeStruct((1, width), F32),
        ],
        compiler_params=pltpu.CompilerParams(vmem_limit_bytes=VMEM_LIMIT),
        cost_estimate=pl.CostEstimate(flops=3 << 30, bytes_accessed=12 << 20, transcendentals=0),
        name="input_grads",
    )(d_q, d_k, d_v, x, w)


def ffn_kernel(xo_ref, xm_ref, go_ref, gm_ref, w_ref, yo_ref, ym_ref, do_ref, dm_ref, grad_ref, gain_ref, sum_ref):
    units = w_ref.shape[1] // 3
    step = pl.program_id(0)
    early = step < pl.num_programs(0) // 2
    x = jnp.where(early, xo_ref[...], xm_ref[...])
    g = jnp.where(early, go_ref[...], gm_ref[...])
    raised = dot(x, w_ref[:, : 2 * units], NN)
    gate = raised[:, :units]
    upper = raised[:, units:]
    sig = 1.0 / (1.0 + jnp.exp(-gate))
    silu = gate * sig
    act = (silu * upper).astype(BF)
    y = dot(act, w_ref[:, 2 * units :], NT).astype(BF)
    d_act = dot(g, w_ref[:, 2 * units :], NN)
    d_gate = (d_act * upper * (sig + silu * (1.0 - sig))).astype(BF)
    d_up = (d_act * silu).astype(BF)
    both = jnp.concatenate([d_gate, d_up], axis=1)
    d_x = dot(both, w_ref[:, : 2 * units], NT)
    gain_row = jnp.sum(d_x * x.astype(F32), axis=0, keepdims=True)
    dx = d_x.astype(BF)

    @pl.when(early)
    def _():
        yo_ref[...] = y
        do_ref[...] = dx

    @pl.when(jnp.logical_not(early))
    def _():
        ym_ref[...] = y
        dm_ref[...] = dx

    left = dot(x, both, TN)
    right = dot(g, act, TN)

    @pl.when(step == 0)
    def _():
        sum_ref[:, : 2 * units] = left
        sum_ref[:, 2 * units :] = right
        gain_ref[...] = gain_row

    @pl.when(step > 0)
    def _():
        sum_ref[:, : 2 * units] += left
        sum_ref[:, 2 * units :] += right
        gain_ref[...] += gain_row

    @pl.when(step == pl.num_programs(0) - 1)
    def _():
        grad_ref[...] = sum_ref[...].astype(BF)


def feed_forward(x_mine, x_other, g_mine, g_other, w, rows):
    tokens, width = x_mine.shape
    units3 = w.shape[1]
    steps = tokens // rows
    other = pl.BlockSpec((rows, width), lambda i: (jnp.minimum(i, steps - 1), 0))
    mine = pl.BlockSpec((rows, width), lambda i: (jnp.maximum(i - steps, 0), 0))
    whole = pl.BlockSpec((width, units3), lambda i: (0, 0))
    part = jax.ShapeDtypeStruct((tokens, width), BF)
    y_other, y_mine, dx_other, dx_mine, grads, gain_row = pl.pallas_call(
        ffn_kernel,
        grid=(2 * steps,),
        in_specs=[other, mine, other, mine, whole],
        out_specs=[other, mine, other, mine, whole, pl.BlockSpec((1, width), lambda i: (0, 0))],
        out_shape=[
            part, part, part, part,
            jax.ShapeDtypeStruct((width, units3), BF), jax.ShapeDtypeStruct((1, width), F32),
        ],
        scratch_shapes=[pltpu.VMEM((width, units3), F32)],
        compiler_params=pltpu.CompilerParams(vmem_limit_bytes=VMEM_LIMIT),
        cost_estimate=pl.CostEstimate(
            flops=12 * tokens * width * units3, bytes_accessed=24 << 20, transcendentals=2 * tokens * units3 // 3
        ),
        name="feed_forward",
    )(x_other, x_mine, g_other, g_mine, w)
    return y_mine, y_other, dx_mine, dx_other, grads, gain_row[0]


def same_kernel(in_ref, out_ref):
    pass


def same(value, flops):
    return pl.pallas_call(
        same_kernel,
        in_specs=[pl.BlockSpec(memory_space=pl.ANY)],
        out_specs=pl.BlockSpec(memory_space=pl.ANY),
        out_shape=jax.ShapeDtypeStruct(value.shape, value.dtype),
        input_output_aliases={0: 0},
        cost_estimate=pl.CostEstimate(flops=flops, bytes_accessed=0, transcendentals=0),
        name="same",
    )(value)


def pack_kernel(gate_ref, up_ref, down_ref, out_ref):
    parts, shard, units3 = out_ref.shape
    units = units3 // 3
    have = gate_ref.shape[1]
    for t in range(parts):
        for j, ref in enumerate((gate_ref, up_ref, down_ref)):
            first = min(t * units, have)
            count = min((t + 1) * units, have) - first
            if count:
                out_ref[t, :, j * units : j * units + count] = ref[:, first : first + count]
            if count < units:
                out_ref[t, :, j * units + count : (j + 1) * units] = jnp.zeros((shard, units - count), BF)


def pack(gate, up, down, parts, units):
    shard = gate.shape[0]
    return pl.pallas_call(
        pack_kernel,
        out_shape=jax.ShapeDtypeStruct((parts, shard, 3 * units), BF),
        compiler_params=pltpu.CompilerParams(vmem_limit_bytes=VMEM_LIMIT),
        name="pack",
    )(gate, up, down)


def finish_kernel(parts_ref, gate_ref, up_ref, down_ref):
    parts, shard, units3 = parts_ref.shape
    units = units3 // 3
    have = gate_ref.shape[1]
    for t in range(parts):
        for j, ref in enumerate((gate_ref, up_ref, down_ref)):
            first = min(t * units, have)
            count = min((t + 1) * units, have) - first
            if count:
                ref[:, first : first + count] = parts_ref[t, :, j * units : j * units + count].astype(F32)


def finish(parts, columns):
    whole = jax.ShapeDtypeStruct((parts.shape[1], columns), F32)
    return pl.pallas_call(
        finish_kernel,
        out_shape=[whole, whole, whole],
        compiler_params=pltpu.CompilerParams(vmem_limit_bytes=VMEM_LIMIT),
        name="finish",
    )(parts)


def inverse_rms(values):
    return lax.rsqrt(jnp.mean(values * values, axis=-1, keepdims=True) + EPS)


def norm_back(values, gain, grad):
    inverse = inverse_rms(values)
    normal = values * inverse
    scaled = grad * gain
    return inverse * (scaled - normal * jnp.mean(scaled * normal, axis=-1, keepdims=True))


def body(
    hidden_in,
    seq_lengths,
    attn_gain,
    query_gain,
    key_gain,
    query_weight,
    key_projection,
    value_projection,
    out_weight,
    ffn_gain,
    gate_weight,
    up_weight,
    down_weight,
    cotangent,
):
    slots, shard_rows, width = hidden_in.shape
    n_fsdp = lax.axis_size("fsdp")
    n_ctx = lax.axis_size("ctx")
    f = lax.axis_index("fsdp")
    c = lax.axis_index("ctx")
    core = lax.axis_index("tp")
    rows = 2 * shard_rows
    keys = n_ctx * rows
    q_cols = query_weight.shape[1]
    k_cols = key_projection.shape[1]
    shard = query_weight.shape[0]
    ff_half = gate_weight.shape[1]
    units = ff_half // n_fsdp
    padded = -(-units // TILE) * TILE

    at = jnp.arange(keys)
    places = (c - at // rows) * rows + ((at // shard_rows) % 2 ^ core) * shard_rows + at % shard_rows
    lanes = jnp.arange(TILE)
    freqs = THETA ** (-((lanes % (HEAD // 2)).astype(F32) * 2.0 / HEAD))
    angles = places.astype(F32)[:, None] * freqs[None, :]
    cosine = jnp.cos(angles)
    sine = jnp.sin(angles) * jnp.where(lanes % HEAD < HEAD // 2, -1.0, 1.0)[None, :]
    scal = jnp.concatenate([jnp.stack([c, core, f]).astype(jnp.int32), seq_lengths])
    own_places = places[:shard_rows]
    valid = own_places[None, :, None] < seq_lengths[:, None, None]

    hidden = hidden_in.astype(F32)
    inverse_one = inverse_rms(hidden)
    normed = (hidden * inverse_one * attn_gain).astype(BF)

    def ctx_stack(pieces):
        stack = jnp.zeros((n_ctx,) + pieces[0].shape, pieces[0].dtype)
        for k, piece in enumerate(pieces):
            stack = lax.dynamic_update_index_in_dim(stack, piece, (c - k) % n_ctx, 0)
        return stack

    def fsdp_stack(pieces):
        stack = jnp.zeros((n_fsdp,) + pieces[0].shape, pieces[0].dtype)
        for m, piece in enumerate(pieces):
            stack = lax.dynamic_update_index_in_dim(stack, piece, f ^ m, 0)
        return stack

    def spread_halves(value):
        masks = [1 << i for i in range(8) if 1 << i < n_fsdp]
        halves = []
        for half, order in zip(jnp.split(value, 2), (masks, masks[::-1])):
            half = half[None]
            for mask in order:
                half = jnp.concatenate([half, fsdp_xor(half, mask)])
            halves.append(half)
        return halves

    def in_order(half, order):
        got = jnp.zeros_like(half)
        for i in range(n_fsdp):
            mask = sum(bit for j, bit in enumerate(order) if i >> j & 1)
            got = lax.dynamic_update_index_in_dim(got, half[i], f ^ mask, 0)
        return got

    def over_ctx(value):
        return [value] + [ctx_shift(value, k) for k in range(1, n_ctx)]

    def over_fsdp(value):
        return [value] + [fsdp_xor(value, m) for m in range(1, n_fsdp)]

    def part(array, index):
        return lax.dynamic_index_in_dim(array, index, 0, keepdims=False)

    def trade_parts(parts):
        return [part(parts, f)] + [fsdp_xor(part(parts, f ^ m), m) for m in range(1, n_fsdp)]

    ffn_packed = pack(gate_weight, up_weight, down_weight.T, n_fsdp, padded)
    packed = jnp.concatenate([query_weight, key_projection, value_projection, out_weight.T], axis=1)
    grad_rows = jnp.where(valid, cotangent, jnp.zeros_like(cotangent))
    x_pieces = [normed, ctx_up(normed)]
    ffn_rows = lax.all_to_all(ffn_packed, "fsdp", 0, 0, tiled=True)
    held = tie(*x_pieces, *over_ctx(packed))
    x_pieces = list(held[:2])
    stack = ctx_stack(held[2:]).reshape(n_ctx * shard, -1)

    top, bottom = spread_halves(stack)
    others = [swap_cores(piece) for piece in x_pieces]
    while len(x_pieces) < n_ctx:
        x_pieces.append(ctx_up(x_pieces[-1]))
        if len(x_pieces) == n_ctx:
            ffn_rows, x_pieces[-1] = tie(ffn_rows, x_pieces[-1])
        others.append(swap_cores(x_pieces[-1]))
    ffn_w = lax.all_gather(ffn_rows, "ctx", axis=1, tiled=True).reshape(width, 3 * padded)
    ffn_w = same(ffn_w, 20 << 30)
    held = tie(*x_pieces, *others, grad_rows, top, bottom)
    x_pieces = held[:n_ctx]
    others = held[n_ctx : 2 * n_ctx]
    grad_rows, top, bottom = held[2 * n_ctx :]

    query_gain2 = jnp.tile(query_gain, 2)[None, :]
    key_gain2 = jnp.tile(key_gain, 2)[None, :]
    attn, stats, q_raw, k_raw, value, q_hat, k_hat, x_all = attend(
        scal, [piece for pair in zip(x_pieces, others) for piece in pair], (top, bottom), (q_cols, k_cols), cosine, sine,
        query_gain2, key_gain2,
    )
    held = tie(attn, *over_fsdp(grad_rows))
    attn = held[0]
    g_mine = jnp.stack(held[1:])
    g_other = swap_cores(g_mine)
    bits = [mask for mask in (1 << i for i in range(8)) if mask < n_fsdp]
    attn_w = jnp.stack([in_order(top, bits), in_order(bottom, bits[::-1])], axis=1).reshape(width, -1)
    out_w = attn_w[:, q_cols + 2 * k_cols :]

    branch = jnp.einsum("sth,dh->std", attn, out_w, preferred_element_type=F32)
    middle = hidden + (branch[:, :shard_rows] + swap_cores(branch[:, shard_rows:]))
    normed_two = (middle * inverse_rms(middle) * ffn_gain).astype(BF)
    x_mine = jnp.stack(over_fsdp(normed_two))
    x_other = swap_cores(x_mine)

    def flat(value):
        return value.reshape(-1, width)

    place = jnp.stack([f]).astype(jnp.int32)
    y_mine, y_other, dx_mine, dx_other, ffn_grads, ffn_gain_row = feed_forward(
        flat(x_mine), flat(x_other), flat(g_mine), flat(g_other), ffn_w, 2 * slots * shard_rows
    )

    ffn_reduced = lax.psum_scatter(
        ffn_grads.reshape(n_fsdp, n_ctx * shard, 3 * padded), "ctx", scatter_dimension=1, tiled=True
    )

    def core_sums(mine, other):
        mine = mine.reshape(n_fsdp, slots, shard_rows, width)
        other = swap_cores(other.reshape(n_fsdp, slots, shard_rows, width))
        return [mine[m].astype(F32) + other[m].astype(F32) for m in range(n_fsdp)]

    def traded(sums):
        return [sums[0]] + [fsdp_xor(sums[m].astype(BF), m) for m in range(1, n_fsdp)]

    held = tie(*traded(core_sums(dx_mine, dx_other)), *core_sums(y_mine, y_other))
    d_normed_two = sum(item.astype(F32) for item in held[:n_fsdp])
    y_sums = held[n_fsdp:]
    d_middle = grad_rows.astype(F32) + norm_back(middle, ffn_gain, d_normed_two)
    d_branch = d_middle.astype(BF)
    d_branch = jnp.concatenate([d_branch, swap_cores(d_branch)], axis=1)
    d_attn = jnp.einsum("std,dh->sth", d_branch, out_w, preferred_element_type=F32).astype(BF)
    held = tie(d_attn, *y_sums)
    d_attn = held[0]
    y_sums = held[1:]

    d_q, d_k, d_v, gq, gk = attend_back(
        scal, q_raw, k_raw, value, cosine, sine, query_gain2, key_gain2, q_hat, k_hat, attn, stats, d_attn
    )
    y_got = traded(y_sums)

    held = tie(d_q, d_k, d_v, *y_got)
    d_q, d_k, d_v = held[:3]
    result = jnp.where(valid, middle + sum(item.astype(F32) for item in held[3:]), 0.0).astype(BF)

    mine, other, attn_gain_row = input_grads(d_q, d_k, d_v, x_all, attn_w)
    mine, other, d_q, d_k, d_v, ffn_reduced = tie(mine, other, d_q, d_k, d_v, ffn_reduced)
    other = swap_cores(other)
    gains = jnp.stack([attn_gain_row[0] / attn_gain, ffn_gain_row / ffn_gain])
    heads = jnp.stack([jnp.pad(jnp.concatenate([item[0, :HEAD] + item[0, HEAD:]]), (0, HEAD)) for item in (gq, gk)])
    small = jnp.concatenate([gains, heads], axis=1)
    small = jnp.pad(small, ((0, 0), (0, 2 * q_cols + 2 * k_cols - small.shape[1])))
    grads = weight_grads(place, x_all, d_q, d_k, d_v, d_branch, attn, two_parts(small), n_fsdp)

    total = mine[n_ctx - 1] + other[n_ctx - 1].astype(F32)
    for r in range(n_ctx - 2, -1, -1):
        total = ctx_down(total.astype(BF)).astype(F32)
        if r == n_ctx - 2:
            held = tie(total, ffn_reduced, *grads)
            total, ffn_reduced = held[:2]
            grads = held[2:]
        total = mine[r] + other[r].astype(F32) + total
    attn_pieces = [grads[0]] + [fsdp_xor(grads[m], m) for m in range(1, n_fsdp)]
    ffn_parts = lax.all_to_all(ffn_reduced, "fsdp", 0, 0, tiled=True)
    depth = n_ctx * shard
    attn_part = sum(piece[:depth].astype(F32) for piece in attn_pieces)
    small = tree_sum([one_part(piece[depth:]) for piece in attn_pieces])
    total, attn_part, ffn_parts, small = tie(total, attn_part, ffn_parts, small)

    sends = attn_part.reshape(n_ctx, shard, -1)
    more = two_parts(small)
    got = [part(sends, c)]
    small = [one_part(more)]
    for k in range(1, n_ctx):
        piece = ctx_shift(jnp.concatenate([part(sends, (c + k) % n_ctx).astype(BF), more]), k)
        got.append(piece[:shard].astype(F32))
        small.append(one_part(piece[shard:]))
    gate_grad, up_grad, down_grad = finish(ffn_parts, ff_half)
    down_grad = down_grad.T
    attn_grads = sum(got)
    small = tree_sum(small)
    small = small + swap_cores(small)
    input_grad = (d_middle + norm_back(hidden, attn_gain, total)).astype(BF)
    qkv_total = attn_grads[:, : q_cols + 2 * k_cols]
    query_weight_grad = qkv_total[:, :q_cols]
    key_weight_grad = qkv_total[:, q_cols : q_cols + k_cols]
    value_weight_grad = qkv_total[:, q_cols + k_cols :]
    out_weight_grad = attn_grads[:, q_cols + 2 * k_cols :].T

    return (
        result,
        input_grad,
        small[0, :width],
        small[0, width : width + HEAD],
        small[1, width : width + HEAD],
        query_weight_grad,
        key_weight_grad,
        value_weight_grad,
        out_weight_grad,
        small[1, :width],
        gate_grad,
        up_grad,
        down_grad,
    )


def solution(mesh):
    in_specs = (
        P("fsdp", ("ctx", "tp"), None),
        P("fsdp"),
        P(),
        P(),
        P(),
        P(("fsdp", "ctx"), "tp"),
        P(("fsdp", "ctx"), "tp"),
        P(("fsdp", "ctx"), "tp"),
        P("tp", ("fsdp", "ctx")),
        P(),
        P(("fsdp", "ctx"), "tp"),
        P(("fsdp", "ctx"), "tp"),
        P("tp", ("fsdp", "ctx")),
        P("fsdp", ("ctx", "tp"), None),
    )
    out_specs = (
        P("fsdp", ("ctx", "tp"), None),
        P("fsdp", ("ctx", "tp"), None),
        P(),
        P(),
        P(),
        P(("fsdp", "ctx"), "tp"),
        P(("fsdp", "ctx"), "tp"),
        P(("fsdp", "ctx"), "tp"),
        P("tp", ("fsdp", "ctx")),
        P(),
        P(("fsdp", "ctx"), "tp"),
        P(("fsdp", "ctx"), "tp"),
        P("tp", ("fsdp", "ctx")),
    )
    return jax.shard_map(body, mesh=mesh, in_specs=in_specs, out_specs=out_specs, check_vma=False)
```

```python
import functools

import jax
import jax.numpy as jnp
import numpy as np
from jax import lax
from jax.experimental import pallas as pl
from jax.experimental.pallas import tpu as pltpu
from jax.sharding import PartitionSpec as P

HEAD = 64
TILE = 128
EPS = 1e-05
THETA = 1000000.0
SCALE = HEAD**-0.5
EXP2_SCALE = SCALE * float(np.log2(np.e))
FAR = -1e30
BF = jnp.bfloat16
F32 = jnp.float32
VMEM_LIMIT = 56 * 1024 * 1024
LATE = 12 << 30
LATER = 5 << 30


def dot(left, right, dims):
    return lax.dot_general(left, right, (dims, ((), ())), preferred_element_type=F32)


NN = ((1,), (0,))
NT = ((1,), (1,))
TN = ((0,), (0,))


def swap_cores(value):
    return lax.ppermute(value, "tp", [(0, 1), (1, 0)])


def fsdp_xor(value, mask):
    size = lax.axis_size("fsdp")
    return lax.ppermute(value, "fsdp", [(i, i ^ mask) for i in range(size)])


def ctx_up(value, step=1):
    size = lax.axis_size("ctx")
    return lax.ppermute(value, "ctx", [(i, i + step) for i in range(size - step)])


def ctx_down(value, step=1):
    size = lax.axis_size("ctx")
    return lax.ppermute(value, "ctx", [(i + step, i) for i in range(size - step)])


def ctx_shift(value, step):
    size = lax.axis_size("ctx")
    return lax.ppermute(value, "ctx", [(i, (i + step) % size) for i in range(size)])


def tree_sum(values):
    while len(values) > 1:
        half = len(values) // 2
        values = [values[i] + values[i + half] for i in range(half)]
    return values[0]


def two_parts(rows):
    first = rows.astype(BF)
    left = (rows - first.astype(F32)).astype(BF)
    return jnp.pad(jnp.concatenate([first, left]), ((0, 16 - 2 * rows.shape[0]), (0, 0)))


def one_part(rows):
    return rows[:2].astype(F32) + rows[2:4].astype(F32)


def tie(*values):
    return lax.optimization_barrier(values)


def lane_ids(rows):
    return lax.broadcasted_iota(jnp.int32, (rows, TILE), 1)


def half_swap(x):
    low = lane_ids(x.shape[0]) % HEAD < HEAD // 2
    return jnp.where(low, pltpu.roll(x, TILE - HEAD // 2, 1), pltpu.roll(x, HEAD // 2, 1))


def head_mean(x):
    first = lane_ids(x.shape[0]) < HEAD
    left = jnp.sum(jnp.where(first, x, 0.0), axis=1, keepdims=True)
    right = jnp.sum(jnp.where(first, 0.0, x), axis=1, keepdims=True)
    return jnp.where(first, left, right) * (1.0 / HEAD)


def prepare(x, gain, cosine, sine):
    scaled = x * lax.rsqrt(head_mean(x * x) + EPS) * gain
    return scaled * cosine + half_swap(scaled) * sine


def prepare_back(x, gain, cosine, sine, grad):
    grad = grad * cosine - half_swap(grad) * sine
    inverse = lax.rsqrt(head_mean(x * x) + EPS)
    normal = x * inverse
    gain_grad = jnp.sum(grad * normal, axis=0, keepdims=True)
    grad = grad * gain
    return inverse * (grad - normal * head_mean(grad * normal)), gain_grad


def key_bias(scal_ref, slot, keys, block_rows):
    c = scal_ref[0]
    core = scal_ref[1]
    length = scal_ref[3 + slot]
    half = block_rows // 2

    def places(index):
        block = index // block_rows
        side = (index // half) % 2
        return (c - block) * block_rows + (side + core - 2 * side * core) * half + index % half

    key_at = places(lax.broadcasted_iota(jnp.int32, (keys, block_rows), 0))
    query_at = places(lax.broadcasted_iota(jnp.int32, (keys, block_rows), 1))
    seen = (key_at >= 0) & (key_at <= query_at) & (key_at < length)
    return jnp.where(seen, 0.0, FAR)


def twins(x):
    first = lane_ids(x.shape[0]) < HEAD
    turned = pltpu.roll(x, HEAD, 1)
    return jnp.where(first, x, turned).astype(BF), jnp.where(first, turned, x).astype(BF)


def attend_kernel(n_pieces, n_parts, scal_ref, *refs):
    pieces = refs[:n_pieces]
    (
        tq_ref, tk_ref, tv_ref, bq_ref, bk_ref, bv_ref, cos_ref, sin_ref, qg_ref, kg_ref,
        o_ref, l_ref, qr_ref, kr_ref, v_ref, qh_ref, kh_ref, x_ref, bias_ref, wq_ref, wkv_ref,
    ) = refs[n_pieces:]
    rows = qr_ref.shape[1]
    keys = kr_ref.shape[1]
    half = rows // 2

    @pl.when(pl.program_id(1) == 0)
    def _():
        bias_ref[...] = key_bias(scal_ref, pl.program_id(0), keys, rows)
        for i, piece in enumerate(pieces):
            x_ref[0, i * half : (i + 1) * half] = piece[0]

    depth = tq_ref.shape[1]
    bits = [1 << i for i in range(8) if 1 << i < n_parts]
    for side, (query_w, key_w, value_w) in enumerate(((tq_ref, tk_ref, tv_ref), (bq_ref, bk_ref, bv_ref))):
        order = bits[::-1] if side else bits
        for i in range(n_parts):
            mask = sum(bit for j, bit in enumerate(order) if i >> j & 1)
            at = pl.ds(pl.multiple_of(((scal_ref[2] ^ mask) * 2 + side) * depth, depth), depth)
            wq_ref[at, :] = query_w[i]
            wkv_ref[at, :TILE] = key_w[i]
            wkv_ref[at, TILE:] = value_w[i]
    key_value = dot(x_ref[0], wkv_ref[...], NN)
    query_raw = dot(x_ref[0, :rows], wq_ref[...], NN)
    kr_ref[0] = key_value[:, :TILE]
    v_ref[0] = key_value[:, TILE:].astype(BF)
    qr_ref[0] = query_raw

    key = prepare(kr_ref[0], kg_ref[...], cos_ref[...], sin_ref[...]).astype(BF)
    kh_ref[0] = key
    key_twins = twins(key.astype(F32))
    value_twins = twins(v_ref[0].astype(F32))
    first = lane_ids(rows) < HEAD
    for pair in range(2):
        lanes = slice(pair * TILE, (pair + 1) * TILE)
        query = prepare(qr_ref[0, :, lanes], qg_ref[...], cos_ref[:rows], sin_ref[:rows]).astype(BF)
        qh_ref[0, :, lanes] = query
        turned_value = value_twins[pair].astype(F32).T.astype(BF)
        mixed = []
        for head in range(2):
            mine = first if head == 0 else jnp.logical_not(first)
            scores = dot(key_twins[pair], jnp.where(mine, query, jnp.zeros_like(query)), NT)
            weights = jnp.exp2(scores * EXP2_SCALE + bias_ref[...])
            inverse = 1.0 / jnp.sum(weights, axis=0, keepdims=True)
            l_ref[0, 0, pl.ds(2 * pair + head, 1), :] = inverse
            mixed.append(dot(turned_value, weights.astype(BF), NN) * inverse)
        row_first = lax.broadcasted_iota(jnp.int32, (TILE, rows), 0) < HEAD
        o_ref[0, :, lanes] = jnp.where(row_first, mixed[0], mixed[1]).T.astype(BF)


def attend_back_kernel(
    scal_ref, q_ref, k_ref, v_ref, cos_ref, sin_ref, qg_ref, kg_ref, qh_ref, kh_ref, o_ref, l_ref, d_ref,
    dq_ref, dk_ref, dv_ref, gq_ref, gk_ref, bias_ref
):
    rows = q_ref.shape[1]
    keys = k_ref.shape[1]

    @pl.when(pl.program_id(1) == 0)
    def _():
        bias_ref[...] = key_bias(scal_ref, pl.program_id(0), keys, rows)

    key_twins = twins(kh_ref[0].astype(F32))
    value_twins = twins(v_ref[0].astype(F32))
    first = lane_ids(rows) < HEAD
    key_first = lane_ids(keys) < HEAD
    row_first = lax.broadcasted_iota(jnp.int32, (TILE, rows), 0) < HEAD
    key_grads = []
    value_grads = []
    query_gain = jnp.zeros((1, TILE), F32)
    for pair in range(2):
        lanes = slice(pair * TILE, (pair + 1) * TILE)
        query = qh_ref[0, :, lanes]
        grad = d_ref[0, :, lanes]
        product = (grad.astype(F32) * o_ref[0, :, lanes].astype(F32)).T
        key_grad = jnp.zeros((keys, TILE), F32)
        value_grad = jnp.zeros((keys, TILE), F32)
        query_grads = []
        for head in range(2):
            mine = first if head == 0 else jnp.logical_not(first)
            own_query = jnp.where(mine, query, jnp.zeros_like(query))
            own_grad = jnp.where(mine, grad, jnp.zeros_like(grad))
            inner = jnp.sum(product[head * HEAD : (head + 1) * HEAD], axis=0, keepdims=True)
            inverse = l_ref[0, 0, pl.ds(2 * pair + head, 1), :]
            scores = dot(key_twins[pair], own_query, NT)
            probs = jnp.exp2(scores * EXP2_SCALE + bias_ref[...]) * inverse
            grad_probs = dot(value_twins[pair], own_grad, NT)
            grad_scores = (probs * (grad_probs - inner)).astype(BF)
            query_grads.append(dot(grad_scores, key_twins[pair], TN))
            key_grad = key_grad + dot(grad_scores, own_query, NN)
            value_grad = value_grad + dot(probs.astype(BF), own_grad, NN)
        query_rot = jnp.where(first, query_grads[0], query_grads[1]) * SCALE
        raw, gain_part = prepare_back(q_ref[0, :, lanes], qg_ref[...], cos_ref[:rows], sin_ref[:rows], query_rot)
        dq_ref[0, :, lanes] = raw.astype(BF)
        query_gain = query_gain + gain_part
        key_grads.append(key_grad + pltpu.roll(key_grad, HEAD, 1))
        value_grads.append(value_grad + pltpu.roll(value_grad, HEAD, 1))
    dv_ref[0] = jnp.where(key_first, value_grads[0], value_grads[1]).astype(BF)
    key_rot = jnp.where(key_first, key_grads[0], key_grads[1]) * SCALE
    raw, key_gain = prepare_back(k_ref[0], kg_ref[...], cos_ref[...], sin_ref[...], key_rot)
    dk_ref[0] = raw.astype(BF)

    @pl.when((pl.program_id(0) == 0) & (pl.program_id(1) == 0))
    def _():
        gq_ref[...] = jnp.zeros_like(gq_ref)
        gk_ref[...] = jnp.zeros_like(gk_ref)

    gq_ref[...] += query_gain
    gk_ref[...] += key_gain


def attention_specs(slots, rows, keys):
    smem = pl.BlockSpec(memory_space=pltpu.SMEM)
    query = pl.BlockSpec((1, rows, 2 * TILE), lambda s, p: (s, 0, p))
    key = pl.BlockSpec((1, keys, TILE), lambda s, p: (s, 0, p))
    table = pl.BlockSpec((keys, TILE), lambda s, p: (0, 0))
    gain = pl.BlockSpec((1, TILE), lambda s, p: (0, 0))
    stat = pl.BlockSpec((1, 1, 8, rows), lambda s, p: (s, p, 0, 0))
    return smem, query, key, table, gain, stat


def attend(scal, pieces, weights, widths, cosine, sine, query_gain, key_gain):
    width, kv_width = widths
    slots, half, model = pieces[0].shape
    rows = 2 * half
    keys = len(pieces) * half
    smem, query, key, table, gain, stat = attention_specs(slots, rows, keys)
    pairs = kv_width // TILE
    piece = pl.BlockSpec((1, half, model), lambda s, p: (s, 0, 0))
    parts, depth = weights[0].shape[:2]
    w_query = pl.BlockSpec((parts, depth, 2 * TILE), lambda s, p: (0, 0, p))
    w_key = pl.BlockSpec((parts, depth, TILE), lambda s, p: (0, 0, width // TILE + p))
    w_value = pl.BlockSpec((parts, depth, TILE), lambda s, p: (0, 0, (width + kv_width) // TILE + p))
    return pl.pallas_call(
        functools.partial(attend_kernel, len(pieces), parts),
        grid=(slots, pairs),
        in_specs=[smem] + [piece] * len(pieces) + [w_query, w_key, w_value] * 2 + [table, table, gain, gain],
        out_specs=[query, stat, query, key, key, query, key, pl.BlockSpec((1, keys, model), lambda s, p: (s, 0, 0))],
        out_shape=[
            jax.ShapeDtypeStruct((slots, rows, width), BF),
            jax.ShapeDtypeStruct((slots, pairs, 8, rows), F32),
            jax.ShapeDtypeStruct((slots, rows, width), F32),
            jax.ShapeDtypeStruct((slots, keys, kv_width), F32),
            jax.ShapeDtypeStruct((slots, keys, kv_width), BF),
            jax.ShapeDtypeStruct((slots, rows, width), BF),
            jax.ShapeDtypeStruct((slots, keys, kv_width), BF),
            jax.ShapeDtypeStruct((slots, keys, model), BF),
        ],
        scratch_shapes=[
            pltpu.VMEM((keys, rows), F32),
            pltpu.VMEM((model, 2 * TILE), BF),
            pltpu.VMEM((model, 2 * TILE), BF),
        ],
        compiler_params=pltpu.CompilerParams(vmem_limit_bytes=VMEM_LIMIT),
        cost_estimate=pl.CostEstimate(flops=1 << 20, bytes_accessed=1 << 20, transcendentals=0),
        name="attend",
    )(scal, *pieces, *[item for item in weights for _ in range(3)], cosine, sine, query_gain, key_gain)


def attend_back(scal, q_raw, k_raw, value, cosine, sine, query_gain, key_gain, q_hat, k_hat, out, stats, grad):
    slots, rows, width = q_raw.shape
    keys, kv_width = k_raw.shape[1:]
    smem, query, key, table, gain, stat = attention_specs(slots, rows, keys)
    pairs = kv_width // TILE
    return pl.pallas_call(
        attend_back_kernel,
        grid=(slots, pairs),
        in_specs=[smem, query, key, key, table, table, gain, gain, query, key, query, stat, query],
        out_specs=[query, key, key, gain, gain],
        out_shape=[
            jax.ShapeDtypeStruct((slots, rows, width), BF),
            jax.ShapeDtypeStruct((slots, keys, kv_width), BF),
            jax.ShapeDtypeStruct((slots, keys, kv_width), BF),
            jax.ShapeDtypeStruct((1, TILE), F32),
            jax.ShapeDtypeStruct((1, TILE), F32),
        ],
        scratch_shapes=[pltpu.VMEM((keys, rows), F32)],
        compiler_params=pltpu.CompilerParams(vmem_limit_bytes=VMEM_LIMIT),
        cost_estimate=pl.CostEstimate(
            flops=24 << 30, bytes_accessed=12 << 20, transcendentals=0
        ),
        name="attend_back",
    )(scal, q_raw, k_raw, value, cosine, sine, query_gain, key_gain, q_hat, k_hat, out, stats, grad)


def bits_of(size):
    return [1 << i for i in range(8) if 1 << i < size]


def weight_kernel(parts, at_ref, x_ref, dq_ref, dk_ref, dv_ref, b_ref, o_ref, w_ref, gain_ref, more_ref, *refs):
    top_send, top_keep, low_send, low_keep, sum_ref = refs
    slots, rows, q_cols = dq_ref.shape
    k_cols = dk_ref.shape[2]
    depth = x_ref.shape[2]
    half = depth // 2
    m = pl.program_id(0)
    query = jnp.zeros((depth, q_cols), F32)
    key = jnp.zeros((depth, k_cols), F32)
    value = jnp.zeros((depth, k_cols), F32)
    out = jnp.zeros((depth, q_cols), F32)
    for s in range(slots):
        x = x_ref[s]
        query = query + dot(x[:rows], dq_ref[s], TN)
        key = key + dot(x, dk_ref[s], TN)
        value = value + dot(x, dv_ref[s], TN)
        out = out + dot(b_ref[s], o_ref[s], TN)
    total = jnp.concatenate([query, key, value, out], axis=1)
    product = total[:, : q_cols + 2 * k_cols] * w_ref[:, : q_cols + 2 * k_cols].astype(F32)
    ones = jnp.ones((8, q_cols + 2 * k_cols), BF)
    high = product.astype(BF)
    low = (product - high.astype(F32)).astype(BF)
    place = pl.ds(pl.multiple_of((at_ref[0] ^ m) * depth, TILE), depth)
    sum_ref[:, place] = dot(ones, high, NT) + dot(ones, low, NT)
    total = total.astype(BF)
    bits = bits_of(parts)
    for bit, rows_of, send, keep in (
        (bits[0], total[:half], top_send, top_keep),
        (bits[-1], total[half:], low_send, low_keep),
    ):
        chosen = [i for i in range(parts) if i & bit]
        for i in range(parts):
            ref = send if i & bit else keep
            rank = chosen.index(i | bit)

            @pl.when(m == i)
            def _(ref=ref, rank=rank, rows_of=rows_of):
                ref[rank * half : (rank + 1) * half] = rows_of

    @pl.when(m == parts - 1)
    def _():
        width = sum_ref.shape[1]
        row = sum_ref[:1] / gain_ref[...]
        first = row.astype(BF).astype(F32)
        left = row - first
        ids = lax.broadcasted_iota(jnp.int32, (16, width), 0)
        more = more_ref[...].astype(F32)
        here = jnp.where(ids == 0, first, jnp.where(ids == 2, left, more[:, :width]))
        top_send[parts // 2 * half :, :width] = here.astype(BF)
        top_send[parts // 2 * half :, width:] = more_ref[:, width:]


def weight_grads(at, x, d_q, d_k, d_v, d_branch, attn, w, gain, more, parts):
    slots, keys, width = x.shape
    cols = 2 * d_q.shape[2] + 2 * d_k.shape[2]
    depth = width // parts
    shapes = [(width // 4 + more.shape[0], cols), (width // 4, cols), (width // 4, cols), (width // 4, cols)]
    spec = pltpu.PrefetchScalarGridSpec(
        num_scalar_prefetch=1,
        grid=(parts,),
        in_specs=[
            pl.BlockSpec((slots, keys, depth), lambda m, at: (0, 0, at[0] ^ m)),
            pl.BlockSpec(d_q.shape, lambda m, at: (0, 0, 0)),
            pl.BlockSpec(d_k.shape, lambda m, at: (0, 0, 0)),
            pl.BlockSpec(d_v.shape, lambda m, at: (0, 0, 0)),
            pl.BlockSpec(d_branch.shape[:2] + (depth,), lambda m, at: (0, 0, at[0] ^ m)),
            pl.BlockSpec(attn.shape, lambda m, at: (0, 0, 0)),
            pl.BlockSpec((depth, cols), lambda m, at: (at[0] ^ m, 0)),
            pl.BlockSpec(gain.shape, lambda m, at: (0, 0)),
            pl.BlockSpec(more.shape, lambda m, at: (0, 0)),
        ],
        out_specs=[pl.BlockSpec(shape, lambda m, at: (0, 0)) for shape in shapes],
        scratch_shapes=[pltpu.VMEM((8, width), F32)],
    )
    return pl.pallas_call(
        functools.partial(weight_kernel, parts),
        grid_spec=spec,
        out_shape=[jax.ShapeDtypeStruct(shape, BF) for shape in shapes],
        compiler_params=pltpu.CompilerParams(vmem_limit_bytes=VMEM_LIMIT),
        cost_estimate=pl.CostEstimate(flops=10 << 30, bytes_accessed=8 << 20, transcendentals=0),
        name="weight_grads",
    )(at, x, d_q, d_k, d_v, d_branch, attn, w, gain, more)


def input_kernel(with_own, dq_ref, dk_ref, dv_ref, w_ref, mine_ref, other_ref):
    slots, rows, q_cols = dq_ref.shape
    k_cols = dk_ref.shape[2]
    half = rows // 2
    for s in range(slots):
        d_x = dot(dk_ref[s], w_ref[:, q_cols : q_cols + k_cols], NT)
        d_x = d_x + dot(dv_ref[s], w_ref[:, q_cols + k_cols : q_cols + 2 * k_cols], NT)
        mine_ref[0, s] = d_x[:half]
        other_ref[0, s] = d_x[half:].astype(BF)

    @pl.when(with_own & (pl.program_id(0) == 0))
    def _():
        for s in range(slots):
            d_x = dot(dq_ref[s], w_ref[:, :q_cols], NT)
            mine_ref[0, s] += d_x[:half]
            other_ref[0, s] = (other_ref[0, s].astype(F32) + d_x[half:]).astype(BF)


def input_grads(d_q, d_k, d_v, w, first, blocks):
    slots, rows, q_cols = d_q.shape
    k_cols = d_k.shape[2]
    width = w.shape[0]
    part = pl.BlockSpec((slots, rows, k_cols), lambda r: (0, r + first, 0))
    out = pl.BlockSpec((1, slots, rows // 2, width), lambda r: (r, 0, 0, 0))
    return pl.pallas_call(
        functools.partial(input_kernel, first == 0),
        grid=(blocks,),
        in_specs=[
            pl.BlockSpec(d_q.shape, lambda r: (0, 0, 0)),
            part,
            part,
            pl.BlockSpec(w.shape, lambda r: (0, 0)),
        ],
        out_specs=[out, out],
        out_shape=[
            jax.ShapeDtypeStruct((blocks, slots, rows // 2, width), F32),
            jax.ShapeDtypeStruct((blocks, slots, rows // 2, width), BF),
        ],
        compiler_params=pltpu.CompilerParams(vmem_limit_bytes=VMEM_LIMIT),
        cost_estimate=pl.CostEstimate(flops=6 << 30, bytes_accessed=1 << 20, transcendentals=0),
        name="input_grads",
    )(d_q, d_k, d_v, w)


def in_parts(rows):
    first = rows.astype(BF).astype(F32)
    return jnp.concatenate([first, rows - first, jnp.zeros((12, rows.shape[1]), F32)]).astype(BF)


def down_kernel(*refs):
    mine_ref, other_ref, *came, out_ref = refs
    total = mine_ref[0] + other_ref[0].astype(F32)
    if came:
        total = total + came[0][...].astype(F32)
    out_ref[...] = total.astype(BF)


def down_add(mine, other, block, *came):
    shape = mine.shape[1:]
    one = pl.BlockSpec((1, 1) + shape[1:], lambda s: (block, s, 0, 0))
    here = pl.BlockSpec((1,) + shape[1:], lambda s: (s, 0, 0))
    return pl.pallas_call(
        down_kernel,
        grid=(shape[0],),
        in_specs=[one, one] + [here] * len(came),
        out_specs=here,
        out_shape=jax.ShapeDtypeStruct(shape, BF),
        cost_estimate=pl.CostEstimate(flops=LATER, bytes_accessed=0, transcendentals=0),
        name="down_add",
    )(mine, other, *came)


def half_kernel(half, sends, keeps, extra, keep_ref, came_ref, *refs):
    own_ref = refs[0] if extra else None
    send_ref, left_ref = refs[-2:]
    for ranks, ref in ((sends, send_ref), (keeps, left_ref)):
        for place, i in enumerate(ranks):
            rows = slice(i * half, (i + 1) * half)
            total = keep_ref[rows].astype(F32) + came_ref[rows].astype(F32)
            ref[place * half : (place + 1) * half] = total.astype(BF)
    if extra:
        ours, theirs = own_ref[...].astype(F32), came_ref[-16:].astype(F32)
        send_ref[len(sends) * half :] = in_parts((ours[:2] + ours[2:4]) + (theirs[:2] + theirs[2:4]))


def half_sum(keep, came, own, half, sends, keeps):
    cols = keep.shape[1]
    riding = 0 if own is None else 16
    return pl.pallas_call(
        functools.partial(half_kernel, half, sends, keeps, own is not None),
        out_shape=[
            jax.ShapeDtypeStruct((len(sends) * half + riding, cols), BF),
            jax.ShapeDtypeStruct((len(keeps) * half, cols), BF),
        ],
        compiler_params=pltpu.CompilerParams(vmem_limit_bytes=VMEM_LIMIT),
        cost_estimate=pl.CostEstimate(flops=LATE, bytes_accessed=0, transcendentals=0),
        name="half_sum",
    )(keep, came, *(() if own is None else (own,)))


def ctx_kernel(parts, at_ref, top_ref, top_came, low_ref, low_came, own_ref, mine_ref, small_ref, *refs):
    *sends, sum_ref = refs
    half = top_ref.shape[0]
    shard = mine_ref.shape[0]
    sum_ref[:half] = top_ref[...].astype(F32) + top_came[:half].astype(F32)
    sum_ref[half:] = low_ref[...].astype(F32) + low_came[...].astype(F32)
    ours, theirs = own_ref[...].astype(F32), top_came[half:].astype(F32)
    small = in_parts((ours[:2] + ours[2:4]) + (theirs[:2] + theirs[2:4]))
    small_ref[...] = small

    def rows(k):
        return sum_ref[pl.ds(pl.multiple_of(((at_ref[1] + k) % parts) * shard, 8), shard)]

    mine_ref[...] = rows(0)
    for k, ref in enumerate(sends, 1):
        ref[:shard] = rows(k).astype(BF)
        ref[shard:] = small


def to_ctx(at, top, top_came, low, low_came, own, parts):
    half, cols = top.shape
    shard = 2 * half // parts
    vmem = pl.BlockSpec(memory_space=pltpu.VMEM)
    message = jax.ShapeDtypeStruct((shard + 16, cols), BF)
    return pl.pallas_call(
        functools.partial(ctx_kernel, parts),
        in_specs=[pl.BlockSpec(memory_space=pltpu.SMEM)] + [vmem] * 5,
        out_shape=[jax.ShapeDtypeStruct((shard, cols), F32), jax.ShapeDtypeStruct((16, cols), BF)] + [message] * (parts - 1),
        scratch_shapes=[pltpu.VMEM((2 * half, cols), F32)],
        compiler_params=pltpu.CompilerParams(vmem_limit_bytes=VMEM_LIMIT),
        cost_estimate=pl.CostEstimate(flops=LATE, bytes_accessed=0, transcendentals=0),
        name="to_ctx",
    )(at, top, top_came, low, low_came, own)


def ffn_kernel(xo_ref, xm_ref, go_ref, gm_ref, w_ref, yo_ref, ym_ref, do_ref, dm_ref, inner_ref, gain_ref):
    units = w_ref.shape[1] // 3
    step = pl.program_id(0)
    early = step < pl.num_programs(0) // 2
    x = jnp.where(early, xo_ref[...], xm_ref[...])
    g = jnp.where(early, go_ref[...], gm_ref[...])
    raised = dot(x, w_ref[:, : 2 * units], NN)
    gate = raised[:, :units]
    upper = raised[:, units:]
    sig = 1.0 / (1.0 + jnp.exp(-gate))
    silu = gate * sig
    act = (silu * upper).astype(BF)
    y = dot(act, w_ref[:, 2 * units :], NT).astype(BF)
    d_act = dot(g, w_ref[:, 2 * units :], NN)
    d_gate = (d_act * upper * (sig + silu * (1.0 - sig))).astype(BF)
    d_up = (d_act * silu).astype(BF)
    inner_ref[:, :units] = d_gate
    inner_ref[:, units : 2 * units] = d_up
    inner_ref[:, 2 * units :] = act
    d_x = dot(inner_ref[:, : 2 * units], w_ref[:, : 2 * units], NT)
    gain_row = jnp.sum(d_x * x.astype(F32), axis=0, keepdims=True)
    dx = d_x.astype(BF)

    @pl.when(early)
    def _():
        yo_ref[...] = y
        do_ref[...] = dx

    @pl.when(jnp.logical_not(early))
    def _():
        ym_ref[...] = y
        dm_ref[...] = dx

    @pl.when(step == 0)
    def _():
        gain_ref[...] = gain_row

    @pl.when(step > 0)
    def _():
        gain_ref[...] += gain_row


def ffn_weight_kernel(xo_ref, xm_ref, go_ref, gm_ref, inner_ref, grad_ref, sum_ref):
    units = inner_ref.shape[1] // 3
    step = pl.program_id(0)
    early = step < pl.num_programs(0) // 2
    x = jnp.where(early, xo_ref[...], xm_ref[...])
    g = jnp.where(early, go_ref[...], gm_ref[...])
    left = dot(x, inner_ref[:, : 2 * units], TN)
    right = dot(g, inner_ref[:, 2 * units :], TN)

    @pl.when(step == 0)
    def _():
        sum_ref[:, : 2 * units] = left
        sum_ref[:, 2 * units :] = right

    @pl.when((step > 0) & (step < pl.num_programs(0) - 1))
    def _():
        sum_ref[:, : 2 * units] += left
        sum_ref[:, 2 * units :] += right

    @pl.when(step == pl.num_programs(0) - 1)
    def _():
        grad_ref[:, : 2 * units] = (sum_ref[:, : 2 * units] + left).astype(BF)
        grad_ref[:, 2 * units :] = (sum_ref[:, 2 * units :] + right).astype(BF)


def ffn_specs(tokens, width, units3, rows):
    steps = tokens // rows
    other = pl.BlockSpec((rows, width), lambda i: (jnp.minimum(i, steps - 1), 0))
    mine = pl.BlockSpec((rows, width), lambda i: (jnp.maximum(i - steps, 0), 0))
    whole = pl.BlockSpec((width, units3), lambda i: (0, 0))
    inner = pl.BlockSpec((rows, units3), lambda i: (i, 0))
    return 2 * steps, other, mine, whole, inner


def feed_forward(x_mine, x_other, g_mine, g_other, w, rows):
    tokens, width = x_mine.shape
    units3 = w.shape[1]
    grid, other, mine, whole, inner = ffn_specs(tokens, width, units3, rows)
    part = jax.ShapeDtypeStruct((tokens, width), BF)
    y_other, y_mine, dx_other, dx_mine, inside, gain_row = pl.pallas_call(
        ffn_kernel,
        grid=(grid,),
        in_specs=[other, mine, other, mine, whole],
        out_specs=[other, mine, other, mine, inner, pl.BlockSpec((1, width), lambda i: (0, 0))],
        out_shape=[
            part, part, part, part,
            jax.ShapeDtypeStruct((2 * tokens, units3), BF), jax.ShapeDtypeStruct((1, width), F32),
        ],
        compiler_params=pltpu.CompilerParams(vmem_limit_bytes=VMEM_LIMIT),
        cost_estimate=pl.CostEstimate(
            flops=8 * tokens * width * units3, bytes_accessed=24 << 20, transcendentals=2 * tokens * units3 // 3
        ),
        name="feed_forward",
    )(x_other, x_mine, g_other, g_mine, w)
    return y_mine, y_other, dx_mine, dx_other, inside, gain_row[0]


def ffn_weight_grads(x_mine, x_other, g_mine, g_other, inside, rows):
    tokens, width = x_mine.shape
    units3 = inside.shape[1]
    grid, other, mine, whole, inner = ffn_specs(tokens, width, units3, rows)
    return pl.pallas_call(
        ffn_weight_kernel,
        grid=(grid,),
        in_specs=[other, mine, other, mine, inner],
        out_specs=whole,
        out_shape=jax.ShapeDtypeStruct((width, units3), BF),
        scratch_shapes=[pltpu.VMEM((width, units3), F32)],
        compiler_params=pltpu.CompilerParams(vmem_limit_bytes=VMEM_LIMIT),
        cost_estimate=pl.CostEstimate(flops=16 << 30, bytes_accessed=24 << 20, transcendentals=0),
        name="ffn_weight_grads",
    )(x_other, x_mine, g_other, g_mine, inside)


def same_kernel(in_ref, out_ref):
    pass


def same(value, flops):
    return pl.pallas_call(
        same_kernel,
        in_specs=[pl.BlockSpec(memory_space=pl.ANY)],
        out_specs=pl.BlockSpec(memory_space=pl.ANY),
        out_shape=jax.ShapeDtypeStruct(value.shape, value.dtype),
        input_output_aliases={0: 0},
        cost_estimate=pl.CostEstimate(flops=flops, bytes_accessed=0, transcendentals=0),
        name="same",
    )(value)


def pack_kernel(gate_ref, up_ref, down_ref, out_ref):
    parts, shard, units3 = out_ref.shape
    units = units3 // 3
    have = gate_ref.shape[1]
    for t in range(parts):
        for j, ref in enumerate((gate_ref, up_ref, down_ref)):
            first = min(t * units, have)
            count = min((t + 1) * units, have) - first
            if count:
                out_ref[t, :, j * units : j * units + count] = ref[:, first : first + count]
            if count < units:
                out_ref[t, :, j * units + count : (j + 1) * units] = jnp.zeros((shard, units - count), BF)


def pack(gate, up, down, parts, units):
    shard = gate.shape[0]
    return pl.pallas_call(
        pack_kernel,
        out_shape=jax.ShapeDtypeStruct((parts, shard, 3 * units), BF),
        compiler_params=pltpu.CompilerParams(vmem_limit_bytes=VMEM_LIMIT),
        name="pack",
    )(gate, up, down)


def finish_kernel(parts_ref, gate_ref, up_ref, down_ref):
    parts, shard, units3 = parts_ref.shape
    units = units3 // 3
    have = gate_ref.shape[1]
    for t in range(parts):
        for j, ref in enumerate((gate_ref, up_ref, down_ref)):
            first = min(t * units, have)
            count = min((t + 1) * units, have) - first
            if count:
                ref[:, first : first + count] = parts_ref[t, :, j * units : j * units + count].astype(F32)


def finish(parts, columns):
    whole = jax.ShapeDtypeStruct((parts.shape[1], columns), F32)
    return pl.pallas_call(
        finish_kernel,
        out_shape=[whole, whole, whole],
        compiler_params=pltpu.CompilerParams(vmem_limit_bytes=VMEM_LIMIT),
        name="finish",
    )(parts)


def inverse_rms(values):
    return lax.rsqrt(jnp.mean(values * values, axis=-1, keepdims=True) + EPS)


def norm_back(values, gain, grad):
    inverse = inverse_rms(values)
    normal = values * inverse
    scaled = grad * gain
    return inverse * (scaled - normal * jnp.mean(scaled * normal, axis=-1, keepdims=True))


def body(
    hidden_in,
    seq_lengths,
    attn_gain,
    query_gain,
    key_gain,
    query_weight,
    key_projection,
    value_projection,
    out_weight,
    ffn_gain,
    gate_weight,
    up_weight,
    down_weight,
    cotangent,
):
    slots, shard_rows, width = hidden_in.shape
    n_fsdp = lax.axis_size("fsdp")
    n_ctx = lax.axis_size("ctx")
    f = lax.axis_index("fsdp")
    c = lax.axis_index("ctx")
    core = lax.axis_index("tp")
    rows = 2 * shard_rows
    keys = n_ctx * rows
    q_cols = query_weight.shape[1]
    k_cols = key_projection.shape[1]
    shard = query_weight.shape[0]
    ff_half = gate_weight.shape[1]
    units = ff_half // n_fsdp
    padded = -(-units // TILE) * TILE

    at = jnp.arange(keys)
    places = (c - at // rows) * rows + ((at // shard_rows) % 2 ^ core) * shard_rows + at % shard_rows
    lanes = jnp.arange(TILE)
    freqs = THETA ** (-((lanes % (HEAD // 2)).astype(F32) * 2.0 / HEAD))
    angles = places.astype(F32)[:, None] * freqs[None, :]
    cosine = jnp.cos(angles)
    sine = jnp.sin(angles) * jnp.where(lanes % HEAD < HEAD // 2, -1.0, 1.0)[None, :]
    scal = jnp.concatenate([jnp.stack([c, core, f]).astype(jnp.int32), seq_lengths])
    own_places = places[:shard_rows]
    valid = own_places[None, :, None] < seq_lengths[:, None, None]

    hidden = hidden_in.astype(F32)
    inverse_one = inverse_rms(hidden)
    normed = (hidden * inverse_one * attn_gain).astype(BF)

    def ctx_stack(pieces):
        stack = jnp.zeros((n_ctx,) + pieces[0].shape, pieces[0].dtype)
        for k, piece in enumerate(pieces):
            stack = lax.dynamic_update_index_in_dim(stack, piece, (c - k) % n_ctx, 0)
        return stack

    def fsdp_stack(pieces):
        stack = jnp.zeros((n_fsdp,) + pieces[0].shape, pieces[0].dtype)
        for m, piece in enumerate(pieces):
            stack = lax.dynamic_update_index_in_dim(stack, piece, f ^ m, 0)
        return stack

    def spread_halves(value):
        masks = [1 << i for i in range(8) if 1 << i < n_fsdp]
        halves = []
        for half, order in zip(jnp.split(value, 2), (masks, masks[::-1])):
            half = half[None]
            for mask in order:
                half = jnp.concatenate([half, fsdp_xor(half, mask)])
            halves.append(half)
        return halves

    def in_order(half, order):
        got = jnp.zeros_like(half)
        for i in range(n_fsdp):
            mask = sum(bit for j, bit in enumerate(order) if i >> j & 1)
            got = lax.dynamic_update_index_in_dim(got, half[i], f ^ mask, 0)
        return got

    def over_ctx(value):
        return [value] + [ctx_shift(value, k) for k in range(1, n_ctx)]

    def over_fsdp(value):
        return [value] + [fsdp_xor(value, m) for m in range(1, n_fsdp)]

    def part(array, index):
        return lax.dynamic_index_in_dim(array, index, 0, keepdims=False)

    def trade_parts(parts):
        return [part(parts, f)] + [fsdp_xor(part(parts, f ^ m), m) for m in range(1, n_fsdp)]

    ffn_packed = pack(gate_weight, up_weight, down_weight.T, n_fsdp, padded)
    packed = jnp.concatenate([query_weight, key_projection, value_projection, out_weight.T], axis=1)
    grad_rows = jnp.where(valid, cotangent, jnp.zeros_like(cotangent))
    x_pieces = [normed, ctx_up(normed)]
    ffn_rows = lax.all_to_all(ffn_packed, "fsdp", 0, 0, tiled=True)
    held = tie(*x_pieces, *over_ctx(packed))
    x_pieces = list(held[:2])
    stack = ctx_stack(held[2:]).reshape(n_ctx * shard, -1)

    top, bottom = spread_halves(stack)
    others = [swap_cores(piece) for piece in x_pieces]
    while len(x_pieces) < n_ctx:
        x_pieces.append(ctx_up(x_pieces[-1]))
        if len(x_pieces) == 3:
            ffn_rows, x_pieces[-1] = tie(ffn_rows, x_pieces[-1])
        others.append(swap_cores(x_pieces[-1]))
    ffn_w = lax.all_gather(ffn_rows, "ctx", axis=1, tiled=True).reshape(width, 3 * padded)
    ffn_w = same(ffn_w, 20 << 30)
    held = tie(*x_pieces, *others, grad_rows, top, bottom)
    x_pieces = held[:n_ctx]
    others = held[n_ctx : 2 * n_ctx]
    grad_rows, top, bottom = held[2 * n_ctx :]

    query_gain2 = jnp.tile(query_gain, 2)[None, :]
    key_gain2 = jnp.tile(key_gain, 2)[None, :]
    attn, stats, q_raw, k_raw, value, q_hat, k_hat, x_all = attend(
        scal, [piece for pair in zip(x_pieces, others) for piece in pair], (top, bottom), (q_cols, k_cols), cosine, sine,
        query_gain2, key_gain2,
    )
    held = tie(attn, *over_fsdp(grad_rows))
    attn = held[0]
    g_mine = jnp.stack(held[1:])
    g_other = swap_cores(g_mine)
    bits = [mask for mask in (1 << i for i in range(8)) if mask < n_fsdp]
    attn_w = jnp.stack([in_order(top, bits), in_order(bottom, bits[::-1])], axis=1).reshape(width, -1)
    out_w = attn_w[:, q_cols + 2 * k_cols :]

    branch = jnp.einsum("sth,dh->std", attn, out_w, preferred_element_type=F32)
    middle = hidden + (branch[:, :shard_rows] + swap_cores(branch[:, shard_rows:]))
    normed_two = (middle * inverse_rms(middle) * ffn_gain).astype(BF)
    x_mine = jnp.stack(over_fsdp(normed_two))
    x_other = swap_cores(x_mine)

    def flat(value):
        return value.reshape(-1, width)

    place = jnp.stack([f]).astype(jnp.int32)
    y_mine, y_other, dx_mine, dx_other, inside, ffn_gain_row = feed_forward(
        flat(x_mine), flat(x_other), flat(g_mine), flat(g_other), ffn_w, 2 * slots * shard_rows
    )

    def core_sums(mine, other):
        mine = mine.reshape(n_fsdp, slots, shard_rows, width)
        other = swap_cores(other.reshape(n_fsdp, slots, shard_rows, width))
        return [mine[m].astype(F32) + other[m].astype(F32) for m in range(n_fsdp)]

    def traded(sums):
        return [sums[0]] + [fsdp_xor(sums[m], m) for m in range(1, n_fsdp)]

    dx_sums = core_sums(dx_mine, dx_other)
    inside, *dx_sums = tie(inside, dx_sums[0], *[item.astype(BF) for item in dx_sums[1:]])
    y_sums = core_sums(y_mine, y_other)
    inside, *y_sums = tie(inside, y_sums[0], *[item.astype(BF) for item in y_sums[1:]])
    ffn_grads = ffn_weight_grads(
        flat(x_mine), flat(x_other), flat(g_mine), flat(g_other), inside, 2 * slots * shard_rows
    )
    ffn_grads, *held = tie(ffn_grads, *traded(dx_sums))
    ffn_reduced = lax.psum_scatter(
        ffn_grads.reshape(n_fsdp, n_ctx * shard, 3 * padded), "ctx", scatter_dimension=1, tiled=True
    )
    d_normed_two = sum(item.astype(F32) for item in held)
    d_middle = grad_rows.astype(F32) + norm_back(middle, ffn_gain, d_normed_two)
    d_branch = d_middle.astype(BF)
    d_branch = jnp.concatenate([d_branch, swap_cores(d_branch)], axis=1)
    d_attn = jnp.einsum("std,dh->sth", d_branch, out_w, preferred_element_type=F32).astype(BF)
    held = tie(d_attn, *y_sums)
    d_attn = held[0]
    y_sums = held[1:]

    d_q, d_k, d_v, gq, gk = attend_back(
        scal, q_raw, k_raw, value, cosine, sine, query_gain2, key_gain2, q_hat, k_hat, attn, stats, d_attn
    )
    y_got = traded(y_sums)

    held = tie(d_q, d_k, d_v, gq, gk, d_branch, ffn_gain_row, *y_got)
    d_q, d_k, d_v, gq, gk, d_branch, ffn_gain_row = held[:7]
    result = jnp.where(valid, middle + sum(item.astype(F32) for item in held[7:]), 0.0).astype(BF)

    heads = jnp.stack([jnp.pad(item[0, :HEAD] + item[0, HEAD:], (0, HEAD)) for item in (gq, gk)])
    small = jnp.stack([jnp.zeros_like(ffn_gain), ffn_gain_row / ffn_gain])
    small = jnp.concatenate([small, heads], axis=1)
    small = jnp.pad(small, ((0, 0), (0, 2 * q_cols + 2 * k_cols - small.shape[1])))
    top_send, top, low_send, low = weight_grads(
        place, x_all, d_q, d_k, d_v, d_branch, attn, attn_w, attn_gain[None, :], two_parts(small), n_fsdp
    )
    top_send, top, low_send, low, d_q, d_k, d_v = tie(top_send, top, low_send, low, d_q, d_k, d_v)

    half = n_ctx * shard // 2
    bits = bits_of(n_fsdp)
    own = top_send[n_fsdp // 2 * half :]
    came = [fsdp_xor(top_send, bits[0]), fsdp_xor(low_send, bits[-1])]
    mine, other = input_grads(d_q, d_k, d_v, attn_w, 0, n_ctx)
    mine, other, *came = tie(mine, other, *came)
    other = swap_cores(other)
    block = n_ctx - 1
    total = None
    for step in range(1, len(bits)):
        count = n_fsdp >> step
        sent = []
        kept = []
        for side, keep in enumerate((top, low)):
            order = bits if side == 0 else bits[::-1]
            masks = sorted(sum(bit for j, bit in enumerate(order[step:]) if i >> j & 1) for i in range(count))
            sends = [i for i, mask in enumerate(masks) if mask & order[step]]
            keeps = [i for i, mask in enumerate(masks) if not mask & order[step]]
            send, keep = half_sum(keep, came[side], own if side == 0 else None, half, sends, keeps)
            sent.append(send)
            kept.append(keep)
        if step == 1:
            other, mine, *held = tie(other, mine, *sent, *kept)
            sent, kept = held[:2], held[2:]
        top, low = kept
        own = sent[0][count // 2 * half :]
        came = [fsdp_xor(sent[0], bits[step]), fsdp_xor(sent[1], bits[-1 - step])]
        if block > 0:
            total = ctx_down(down_add(mine, other, block, *(() if total is None else (total,))))
            block -= 1
            total, *came = tie(total, *came)
    ctx_place = jnp.stack([f, c]).astype(jnp.int32)
    mine_rows, small, *messages = to_ctx(ctx_place, top, came[0], low, came[1], own, n_ctx)
    got = [ctx_shift(message, k) for k, message in enumerate(messages, 1)]
    ffn_parts = lax.all_to_all(ffn_reduced, "fsdp", 0, 0, tiled=True)
    if block > 0:
        total = ctx_down(down_add(mine, other, block, total))
        block -= 1
        total, ffn_parts, *got = tie(total, ffn_parts, *got)
    while block > 0:
        total = ctx_down(down_add(mine, other, block, total))
        block -= 1
    total = mine[0] + other[0].astype(F32) + total.astype(F32)

    small = [one_part(small)] + [one_part(piece[shard:]) for piece in got]
    got = [mine_rows] + [piece[:shard].astype(F32) for piece in got]
    gate_grad, up_grad, down_grad = finish(ffn_parts, ff_half)
    down_grad = down_grad.T
    attn_grads = sum(got)
    small = tree_sum(small)
    small = small + swap_cores(small)
    input_grad = (d_middle + norm_back(hidden, attn_gain, total)).astype(BF)
    qkv_total = attn_grads[:, : q_cols + 2 * k_cols]
    query_weight_grad = qkv_total[:, :q_cols]
    key_weight_grad = qkv_total[:, q_cols : q_cols + k_cols]
    value_weight_grad = qkv_total[:, q_cols + k_cols :]
    out_weight_grad = attn_grads[:, q_cols + 2 * k_cols :].T

    return (
        result,
        input_grad,
        small[0, :width],
        small[0, width : width + HEAD],
        small[1, width : width + HEAD],
        query_weight_grad,
        key_weight_grad,
        value_weight_grad,
        out_weight_grad,
        small[1, :width],
        gate_grad,
        up_grad,
        down_grad,
    )


def solution(mesh):
    in_specs = (
        P("fsdp", ("ctx", "tp"), None),
        P("fsdp"),
        P(),
        P(),
        P(),
        P(("fsdp", "ctx"), "tp"),
        P(("fsdp", "ctx"), "tp"),
        P(("fsdp", "ctx"), "tp"),
        P("tp", ("fsdp", "ctx")),
        P(),
        P(("fsdp", "ctx"), "tp"),
        P(("fsdp", "ctx"), "tp"),
        P("tp", ("fsdp", "ctx")),
        P("fsdp", ("ctx", "tp"), None),
    )
    out_specs = (
        P("fsdp", ("ctx", "tp"), None),
        P("fsdp", ("ctx", "tp"), None),
        P(),
        P(),
        P(),
        P(("fsdp", "ctx"), "tp"),
        P(("fsdp", "ctx"), "tp"),
        P(("fsdp", "ctx"), "tp"),
        P("tp", ("fsdp", "ctx")),
        P(),
        P(("fsdp", "ctx"), "tp"),
        P(("fsdp", "ctx"), "tp"),
        P("tp", ("fsdp", "ctx")),
    )
    return jax.shard_map(body, mesh=mesh, in_specs=in_specs, out_specs=out_specs, check_vma=False)
```

```python
import functools

import jax
import jax.numpy as jnp
import numpy as np
from jax import lax
from jax.experimental import pallas as pl
from jax.experimental.pallas import tpu as pltpu
from jax.sharding import PartitionSpec as P

HEAD = 64
TILE = 128
EPS = 1e-05
THETA = 1000000.0
SCALE = HEAD**-0.5
EXP2_SCALE = SCALE * float(np.log2(np.e))
FAR = -1e30
BF = jnp.bfloat16
F32 = jnp.float32
VMEM_LIMIT = 56 * 1024 * 1024
LATE = 12 << 30
LATER = 5 << 30


def dot(left, right, dims):
    return lax.dot_general(left, right, (dims, ((), ())), preferred_element_type=F32)


NN = ((1,), (0,))
NT = ((1,), (1,))
TN = ((0,), (0,))


def swap_cores(value):
    return lax.ppermute(value, "tp", [(0, 1), (1, 0)])


def fsdp_xor(value, mask):
    size = lax.axis_size("fsdp")
    return lax.ppermute(value, "fsdp", [(i, i ^ mask) for i in range(size)])


def ctx_up(value, step=1):
    size = lax.axis_size("ctx")
    return lax.ppermute(value, "ctx", [(i, i + step) for i in range(size - step)])


def ctx_down(value, step=1):
    size = lax.axis_size("ctx")
    return lax.ppermute(value, "ctx", [(i + step, i) for i in range(size - step)])


def ctx_shift(value, step):
    size = lax.axis_size("ctx")
    return lax.ppermute(value, "ctx", [(i, (i + step) % size) for i in range(size)])


def tree_sum(values):
    while len(values) > 1:
        half = len(values) // 2
        values = [values[i] + values[i + half] for i in range(half)]
    return values[0]


def two_parts(rows):
    first = rows.astype(BF)
    left = (rows - first.astype(F32)).astype(BF)
    return jnp.pad(jnp.concatenate([first, left]), ((0, 16 - 2 * rows.shape[0]), (0, 0)))


def one_part(rows):
    return rows[:2].astype(F32) + rows[2:4].astype(F32)


def tie(*values):
    return lax.optimization_barrier(values)


def lane_ids(rows):
    return lax.broadcasted_iota(jnp.int32, (rows, TILE), 1)


def half_swap(x):
    low = lane_ids(x.shape[0]) % HEAD < HEAD // 2
    return jnp.where(low, pltpu.roll(x, TILE - HEAD // 2, 1), pltpu.roll(x, HEAD // 2, 1))


def head_mean(x):
    first = lane_ids(x.shape[0]) < HEAD
    left = jnp.sum(jnp.where(first, x, 0.0), axis=1, keepdims=True)
    right = jnp.sum(jnp.where(first, 0.0, x), axis=1, keepdims=True)
    return jnp.where(first, left, right) * (1.0 / HEAD)


def prepare(x, gain, cosine, sine):
    scaled = x * lax.rsqrt(head_mean(x * x) + EPS) * gain
    return scaled * cosine + half_swap(scaled) * sine


def prepare_back(x, gain, cosine, sine, grad):
    grad = grad * cosine - half_swap(grad) * sine
    inverse = lax.rsqrt(head_mean(x * x) + EPS)
    normal = x * inverse
    gain_grad = jnp.sum(grad * normal, axis=0, keepdims=True)
    grad = grad * gain
    return inverse * (grad - normal * head_mean(grad * normal)), gain_grad


def key_bias(scal_ref, slot, keys, block_rows):
    c = scal_ref[0]
    core = scal_ref[1]
    length = scal_ref[3 + slot]
    half = block_rows // 2

    def places(index):
        block = index // block_rows
        side = (index // half) % 2
        return (c - block) * block_rows + (side + core - 2 * side * core) * half + index % half

    key_at = places(lax.broadcasted_iota(jnp.int32, (keys, block_rows), 0))
    query_at = places(lax.broadcasted_iota(jnp.int32, (keys, block_rows), 1))
    seen = (key_at >= 0) & (key_at <= query_at) & (key_at < length)
    return jnp.where(seen, 0.0, FAR)


def twins(x):
    first = lane_ids(x.shape[0]) < HEAD
    turned = pltpu.roll(x, HEAD, 1)
    return jnp.where(first, x, turned).astype(BF), jnp.where(first, turned, x).astype(BF)


def attend_kernel(n_pieces, n_parts, scal_ref, *refs):
    pieces = refs[:n_pieces]
    (
        tq_ref, tk_ref, tv_ref, bq_ref, bk_ref, bv_ref, cos_ref, sin_ref, qg_ref, kg_ref,
        o_ref, l_ref, qr_ref, kr_ref, v_ref, qh_ref, kh_ref, x_ref, bias_ref, wq_ref, wkv_ref,
    ) = refs[n_pieces:]
    rows = qr_ref.shape[1]
    keys = kr_ref.shape[1]
    half = rows // 2

    @pl.when(pl.program_id(1) == 0)
    def _():
        bias_ref[...] = key_bias(scal_ref, pl.program_id(0), keys, rows)
        for i, piece in enumerate(pieces):
            x_ref[0, i * half : (i + 1) * half] = piece[0]

    depth = tq_ref.shape[1]
    bits = [1 << i for i in range(8) if 1 << i < n_parts]
    for side, (query_w, key_w, value_w) in enumerate(((tq_ref, tk_ref, tv_ref), (bq_ref, bk_ref, bv_ref))):
        order = bits[::-1] if side else bits
        for i in range(n_parts):
            mask = sum(bit for j, bit in enumerate(order) if i >> j & 1)
            at = pl.ds(pl.multiple_of(((scal_ref[2] ^ mask) * 2 + side) * depth, depth), depth)
            wq_ref[at, :] = query_w[i]
            wkv_ref[at, :TILE] = key_w[i]
            wkv_ref[at, TILE:] = value_w[i]
    key_value = dot(x_ref[0], wkv_ref[...], NN)
    query_raw = dot(x_ref[0, :rows], wq_ref[...], NN)
    kr_ref[0] = key_value[:, :TILE]
    v_ref[0] = key_value[:, TILE:].astype(BF)
    qr_ref[0] = query_raw

    key = prepare(kr_ref[0], kg_ref[...], cos_ref[...], sin_ref[...]).astype(BF)
    kh_ref[0] = key
    key_twins = twins(key.astype(F32))
    value_twins = twins(v_ref[0].astype(F32))
    first = lane_ids(rows) < HEAD
    for pair in range(2):
        lanes = slice(pair * TILE, (pair + 1) * TILE)
        query = prepare(qr_ref[0, :, lanes], qg_ref[...], cos_ref[:rows], sin_ref[:rows]).astype(BF)
        qh_ref[0, :, lanes] = query
        turned_value = value_twins[pair].astype(F32).T.astype(BF)
        mixed = []
        for head in range(2):
            mine = first if head == 0 else jnp.logical_not(first)
            scores = dot(key_twins[pair], jnp.where(mine, query, jnp.zeros_like(query)), NT)
            weights = jnp.exp2(scores * EXP2_SCALE + bias_ref[...])
            inverse = 1.0 / jnp.sum(weights, axis=0, keepdims=True)
            l_ref[0, 0, pl.ds(2 * pair + head, 1), :] = inverse
            mixed.append(dot(turned_value, weights.astype(BF), NN) * inverse)
        row_first = lax.broadcasted_iota(jnp.int32, (TILE, rows), 0) < HEAD
        o_ref[0, :, lanes] = jnp.where(row_first, mixed[0], mixed[1]).T.astype(BF)


def attend_back_kernel(
    scal_ref, q_ref, k_ref, v_ref, cos_ref, sin_ref, qg_ref, kg_ref, qh_ref, kh_ref, o_ref, l_ref, d_ref,
    dq_ref, dk_ref, dv_ref, gq_ref, gk_ref, bias_ref
):
    rows = q_ref.shape[1]
    keys = k_ref.shape[1]

    @pl.when(pl.program_id(1) == 0)
    def _():
        bias_ref[...] = key_bias(scal_ref, pl.program_id(0), keys, rows)

    key_twins = twins(kh_ref[0].astype(F32))
    value_twins = twins(v_ref[0].astype(F32))
    first = lane_ids(rows) < HEAD
    key_first = lane_ids(keys) < HEAD
    row_first = lax.broadcasted_iota(jnp.int32, (TILE, rows), 0) < HEAD
    key_grads = []
    value_grads = []
    query_gain = jnp.zeros((1, TILE), F32)
    for pair in range(2):
        lanes = slice(pair * TILE, (pair + 1) * TILE)
        query = qh_ref[0, :, lanes]
        grad = d_ref[0, :, lanes]
        product = (grad.astype(F32) * o_ref[0, :, lanes].astype(F32)).T
        key_grad = jnp.zeros((keys, TILE), F32)
        value_grad = jnp.zeros((keys, TILE), F32)
        query_grads = []
        for head in range(2):
            mine = first if head == 0 else jnp.logical_not(first)
            own_query = jnp.where(mine, query, jnp.zeros_like(query))
            own_grad = jnp.where(mine, grad, jnp.zeros_like(grad))
            inner = jnp.sum(product[head * HEAD : (head + 1) * HEAD], axis=0, keepdims=True)
            inverse = l_ref[0, 0, pl.ds(2 * pair + head, 1), :]
            scores = dot(key_twins[pair], own_query, NT)
            probs = jnp.exp2(scores * EXP2_SCALE + bias_ref[...]) * inverse
            grad_probs = dot(value_twins[pair], own_grad, NT)
            grad_scores = (probs * (grad_probs - inner)).astype(BF)
            query_grads.append(dot(grad_scores, key_twins[pair], TN))
            key_grad = key_grad + dot(grad_scores, own_query, NN)
            value_grad = value_grad + dot(probs.astype(BF), own_grad, NN)
        query_rot = jnp.where(first, query_grads[0], query_grads[1]) * SCALE
        raw, gain_part = prepare_back(q_ref[0, :, lanes], qg_ref[...], cos_ref[:rows], sin_ref[:rows], query_rot)
        dq_ref[0, :, lanes] = raw.astype(BF)
        query_gain = query_gain + gain_part
        key_grads.append(key_grad + pltpu.roll(key_grad, HEAD, 1))
        value_grads.append(value_grad + pltpu.roll(value_grad, HEAD, 1))
    dv_ref[0] = jnp.where(key_first, value_grads[0], value_grads[1]).astype(BF)
    key_rot = jnp.where(key_first, key_grads[0], key_grads[1]) * SCALE
    raw, key_gain = prepare_back(k_ref[0], kg_ref[...], cos_ref[...], sin_ref[...], key_rot)
    dk_ref[0] = raw.astype(BF)

    @pl.when((pl.program_id(0) == 0) & (pl.program_id(1) == 0))
    def _():
        gq_ref[...] = jnp.zeros_like(gq_ref)
        gk_ref[...] = jnp.zeros_like(gk_ref)

    gq_ref[...] += query_gain
    gk_ref[...] += key_gain


def attention_specs(slots, rows, keys):
    smem = pl.BlockSpec(memory_space=pltpu.SMEM)
    query = pl.BlockSpec((1, rows, 2 * TILE), lambda s, p: (s, 0, p))
    key = pl.BlockSpec((1, keys, TILE), lambda s, p: (s, 0, p))
    table = pl.BlockSpec((keys, TILE), lambda s, p: (0, 0))
    gain = pl.BlockSpec((1, TILE), lambda s, p: (0, 0))
    stat = pl.BlockSpec((1, 1, 8, rows), lambda s, p: (s, p, 0, 0))
    return smem, query, key, table, gain, stat


def attend(scal, pieces, weights, widths, cosine, sine, query_gain, key_gain):
    width, kv_width = widths
    slots, half, model = pieces[0].shape
    rows = 2 * half
    keys = len(pieces) * half
    smem, query, key, table, gain, stat = attention_specs(slots, rows, keys)
    pairs = kv_width // TILE
    piece = pl.BlockSpec((1, half, model), lambda s, p: (s, 0, 0))
    parts, depth = weights[0].shape[:2]
    w_query = pl.BlockSpec((parts, depth, 2 * TILE), lambda s, p: (0, 0, p))
    w_key = pl.BlockSpec((parts, depth, TILE), lambda s, p: (0, 0, width // TILE + p))
    w_value = pl.BlockSpec((parts, depth, TILE), lambda s, p: (0, 0, (width + kv_width) // TILE + p))
    return pl.pallas_call(
        functools.partial(attend_kernel, len(pieces), parts),
        grid=(slots, pairs),
        in_specs=[smem] + [piece] * len(pieces) + [w_query, w_key, w_value] * 2 + [table, table, gain, gain],
        out_specs=[
            query, stat, query, key, key, query, key, pl.BlockSpec((1, keys, model), lambda s, p: (s, 0, 0)),
        ],
        out_shape=[
            jax.ShapeDtypeStruct((slots, rows, width), BF),
            jax.ShapeDtypeStruct((slots, pairs, 8, rows), F32),
            jax.ShapeDtypeStruct((slots, rows, width), F32),
            jax.ShapeDtypeStruct((slots, keys, kv_width), F32),
            jax.ShapeDtypeStruct((slots, keys, kv_width), BF),
            jax.ShapeDtypeStruct((slots, rows, width), BF),
            jax.ShapeDtypeStruct((slots, keys, kv_width), BF),
            jax.ShapeDtypeStruct((slots, keys, model), BF),
        ],
        scratch_shapes=[
            pltpu.VMEM((keys, rows), F32),
            pltpu.VMEM((model, 2 * TILE), BF),
            pltpu.VMEM((model, 2 * TILE), BF),
        ],
        compiler_params=pltpu.CompilerParams(vmem_limit_bytes=VMEM_LIMIT),
        cost_estimate=pl.CostEstimate(flops=1 << 20, bytes_accessed=1 << 20, transcendentals=0),
        name="attend",
    )(scal, *pieces, *[item for item in weights for _ in range(3)], cosine, sine, query_gain, key_gain)


def attend_back(scal, q_raw, k_raw, value, cosine, sine, query_gain, key_gain, q_hat, k_hat, out, stats, grad):
    slots, rows, width = q_raw.shape
    keys, kv_width = k_raw.shape[1:]
    smem, query, key, table, gain, stat = attention_specs(slots, rows, keys)
    pairs = kv_width // TILE
    return pl.pallas_call(
        attend_back_kernel,
        grid=(slots, pairs),
        in_specs=[smem, query, key, key, table, table, gain, gain, query, key, query, stat, query],
        out_specs=[query, key, key, gain, gain],
        out_shape=[
            jax.ShapeDtypeStruct((slots, rows, width), BF),
            jax.ShapeDtypeStruct((slots, keys, kv_width), BF),
            jax.ShapeDtypeStruct((slots, keys, kv_width), BF),
            jax.ShapeDtypeStruct((1, TILE), F32),
            jax.ShapeDtypeStruct((1, TILE), F32),
        ],
        scratch_shapes=[pltpu.VMEM((keys, rows), F32)],
        compiler_params=pltpu.CompilerParams(vmem_limit_bytes=VMEM_LIMIT),
        cost_estimate=pl.CostEstimate(
            flops=24 << 30, bytes_accessed=12 << 20, transcendentals=0
        ),
        name="attend_back",
    )(scal, q_raw, k_raw, value, cosine, sine, query_gain, key_gain, q_hat, k_hat, out, stats, grad)


def bits_of(size):
    return [1 << i for i in range(8) if 1 << i < size]


def weight_kernel(parts, at_ref, x_ref, dq_ref, dk_ref, dv_ref, bm_ref, bo_ref, o_ref, w_ref, gain_ref, more_ref, *refs):
    top_send, top_keep, low_send, low_keep, sum_ref = refs
    slots, rows, q_cols = dq_ref.shape
    k_cols = dk_ref.shape[2]
    depth = x_ref.shape[2]
    half = depth // 2
    m = pl.program_id(0)
    query = jnp.zeros((depth, q_cols), F32)
    key = jnp.zeros((depth, k_cols), F32)
    value = jnp.zeros((depth, k_cols), F32)
    out = jnp.zeros((depth, q_cols), F32)
    for s in range(slots):
        x = x_ref[s]
        query = query + dot(x[:rows], dq_ref[s], TN)
        key = key + dot(x, dk_ref[s], TN)
        value = value + dot(x, dv_ref[s], TN)
        out = out + dot(jnp.concatenate([bm_ref[s], bo_ref[s]]), o_ref[s], TN)
    total = jnp.concatenate([query, key, value, out], axis=1)
    product = total[:, : q_cols + 2 * k_cols] * w_ref[:, : q_cols + 2 * k_cols].astype(F32)
    ones = jnp.ones((8, q_cols + 2 * k_cols), BF)
    high = product.astype(BF)
    low = (product - high.astype(F32)).astype(BF)
    place = pl.ds(pl.multiple_of((at_ref[0] ^ m) * depth, TILE), depth)
    sum_ref[:, place] = dot(ones, high, NT) + dot(ones, low, NT)
    total = total.astype(BF)
    bits = bits_of(parts)
    for bit, rows_of, send, keep in (
        (bits[0], total[:half], top_send, top_keep),
        (bits[-1], total[half:], low_send, low_keep),
    ):
        chosen = [i for i in range(parts) if i & bit]
        for i in range(parts):
            ref = send if i & bit else keep
            rank = chosen.index(i | bit)

            @pl.when(m == i)
            def _(ref=ref, rank=rank, rows_of=rows_of):
                ref[rank * half : (rank + 1) * half] = rows_of

    @pl.when(m == parts - 1)
    def _():
        width = sum_ref.shape[1]
        row = sum_ref[:1] / gain_ref[...]
        first = row.astype(BF).astype(F32)
        left = row - first
        ids = lax.broadcasted_iota(jnp.int32, (16, width), 0)
        more = more_ref[...].astype(F32)
        here = jnp.where(ids == 0, first, jnp.where(ids == 2, left, more[:, :width]))
        top_send[parts // 2 * half :, :width] = here.astype(BF)
        top_send[parts // 2 * half :, width:] = more_ref[:, width:]


def weight_grads(at, x, d_q, d_k, d_v, d_mine, d_other, attn, w, gain, more, parts):
    slots, keys, width = x.shape
    cols = 2 * d_q.shape[2] + 2 * d_k.shape[2]
    depth = width // parts
    shapes = [(width // 4 + more.shape[0], cols), (width // 4, cols), (width // 4, cols), (width // 4, cols)]
    spec = pltpu.PrefetchScalarGridSpec(
        num_scalar_prefetch=1,
        grid=(parts,),
        in_specs=[
            pl.BlockSpec((slots, keys, depth), lambda m, at: (0, 0, at[0] ^ m)),
            pl.BlockSpec(d_q.shape, lambda m, at: (0, 0, 0)),
            pl.BlockSpec(d_k.shape, lambda m, at: (0, 0, 0)),
            pl.BlockSpec(d_v.shape, lambda m, at: (0, 0, 0)),
            pl.BlockSpec(d_mine.shape[:2] + (depth,), lambda m, at: (0, 0, at[0] ^ m)),
            pl.BlockSpec(d_mine.shape[:2] + (depth,), lambda m, at: (0, 0, at[0] ^ m)),
            pl.BlockSpec(attn.shape, lambda m, at: (0, 0, 0)),
            pl.BlockSpec((depth, cols), lambda m, at: (at[0] ^ m, 0)),
            pl.BlockSpec(gain.shape, lambda m, at: (0, 0)),
            pl.BlockSpec(more.shape, lambda m, at: (0, 0)),
        ],
        out_specs=[pl.BlockSpec(shape, lambda m, at: (0, 0)) for shape in shapes],
        scratch_shapes=[pltpu.VMEM((8, width), F32)],
    )
    return pl.pallas_call(
        functools.partial(weight_kernel, parts),
        grid_spec=spec,
        out_shape=[jax.ShapeDtypeStruct(shape, BF) for shape in shapes],
        compiler_params=pltpu.CompilerParams(vmem_limit_bytes=VMEM_LIMIT),
        cost_estimate=pl.CostEstimate(flops=10 << 30, bytes_accessed=8 << 20, transcendentals=0),
        name="weight_grads",
    )(at, x, d_q, d_k, d_v, d_mine, d_other, attn, w, gain, more)


def input_kernel(with_own, dq_ref, dk_ref, dv_ref, w_ref, mine_ref, other_ref):
    slots, rows, q_cols = dq_ref.shape
    k_cols = dk_ref.shape[2]
    half = rows // 2
    for s in range(slots):
        d_x = dot(dk_ref[s], w_ref[:, q_cols : q_cols + k_cols], NT)
        d_x = d_x + dot(dv_ref[s], w_ref[:, q_cols + k_cols : q_cols + 2 * k_cols], NT)
        mine_ref[0, s] = d_x[:half]
        other_ref[0, s] = d_x[half:].astype(BF)

    @pl.when(with_own & (pl.program_id(0) == 0))
    def _():
        for s in range(slots):
            d_x = dot(dq_ref[s], w_ref[:, :q_cols], NT)
            mine_ref[0, s] += d_x[:half]
            other_ref[0, s] = (other_ref[0, s].astype(F32) + d_x[half:]).astype(BF)


def input_grads(d_q, d_k, d_v, w, first, blocks):
    slots, rows, q_cols = d_q.shape
    k_cols = d_k.shape[2]
    width = w.shape[0]
    part = pl.BlockSpec((slots, rows, k_cols), lambda r: (0, r + first, 0))
    out = pl.BlockSpec((1, slots, rows // 2, width), lambda r: (r, 0, 0, 0))
    return pl.pallas_call(
        functools.partial(input_kernel, first == 0),
        grid=(blocks,),
        in_specs=[
            pl.BlockSpec(d_q.shape, lambda r: (0, 0, 0)),
            part,
            part,
            pl.BlockSpec(w.shape, lambda r: (0, 0)),
        ],
        out_specs=[out, out],
        out_shape=[
            jax.ShapeDtypeStruct((blocks, slots, rows // 2, width), F32),
            jax.ShapeDtypeStruct((blocks, slots, rows // 2, width), BF),
        ],
        compiler_params=pltpu.CompilerParams(vmem_limit_bytes=VMEM_LIMIT),
        cost_estimate=pl.CostEstimate(flops=6 << 30, bytes_accessed=1 << 20, transcendentals=0),
        name="input_grads",
    )(d_q, d_k, d_v, w)


def in_parts(rows):
    first = rows.astype(BF).astype(F32)
    return jnp.concatenate([first, rows - first, jnp.zeros((12, rows.shape[1]), F32)]).astype(BF)


def down_kernel(*refs):
    mine_ref, other_ref, *came, out_ref = refs
    total = mine_ref[0] + other_ref[0].astype(F32)
    if came:
        total = total + came[0][...].astype(F32)
    out_ref[...] = total.astype(BF)


def down_add(mine, other, block, *came):
    shape = mine.shape[1:]
    one = pl.BlockSpec((1, 1) + shape[1:], lambda s: (block, s, 0, 0))
    here = pl.BlockSpec((1,) + shape[1:], lambda s: (s, 0, 0))
    return pl.pallas_call(
        down_kernel,
        grid=(shape[0],),
        in_specs=[one, one] + [here] * len(came),
        out_specs=here,
        out_shape=jax.ShapeDtypeStruct(shape, BF),
        cost_estimate=pl.CostEstimate(flops=LATER, bytes_accessed=0, transcendentals=0),
        name="down_add",
    )(mine, other, *came)


def half_kernel(half, sends, keeps, extra, keep_ref, came_ref, *refs):
    own_ref = refs[0] if extra else None
    send_ref, left_ref = refs[-2:]
    for ranks, ref in ((sends, send_ref), (keeps, left_ref)):
        for place, i in enumerate(ranks):
            rows = slice(i * half, (i + 1) * half)
            total = keep_ref[rows].astype(F32) + came_ref[rows].astype(F32)
            ref[place * half : (place + 1) * half] = total.astype(BF)
    if extra:
        ours, theirs = own_ref[...].astype(F32), came_ref[-16:].astype(F32)
        send_ref[len(sends) * half :] = in_parts((ours[:2] + ours[2:4]) + (theirs[:2] + theirs[2:4]))


def half_sum(keep, came, own, half, sends, keeps):
    cols = keep.shape[1]
    riding = 0 if own is None else 16
    return pl.pallas_call(
        functools.partial(half_kernel, half, sends, keeps, own is not None),
        out_shape=[
            jax.ShapeDtypeStruct((len(sends) * half + riding, cols), BF),
            jax.ShapeDtypeStruct((len(keeps) * half, cols), BF),
        ],
        compiler_params=pltpu.CompilerParams(vmem_limit_bytes=VMEM_LIMIT),
        cost_estimate=pl.CostEstimate(flops=LATE, bytes_accessed=0, transcendentals=0),
        name="half_sum",
    )(keep, came, *(() if own is None else (own,)))


def ctx_kernel(parts, at_ref, top_ref, top_came, low_ref, low_came, own_ref, mine_ref, small_ref, *refs):
    *sends, sum_ref = refs
    half = top_ref.shape[0]
    shard = mine_ref.shape[0]
    sum_ref[:half] = top_ref[...].astype(F32) + top_came[:half].astype(F32)
    sum_ref[half:] = low_ref[...].astype(F32) + low_came[...].astype(F32)
    ours, theirs = own_ref[...].astype(F32), top_came[half:].astype(F32)
    small = in_parts((ours[:2] + ours[2:4]) + (theirs[:2] + theirs[2:4]))
    small_ref[...] = small

    def rows(k):
        return sum_ref[pl.ds(pl.multiple_of(((at_ref[1] + k) % parts) * shard, 8), shard)]

    mine_ref[...] = rows(0)
    for k, ref in enumerate(sends, 1):
        ref[:shard] = rows(k).astype(BF)
        ref[shard:] = small


def to_ctx(at, top, top_came, low, low_came, own, parts):
    half, cols = top.shape
    shard = 2 * half // parts
    vmem = pl.BlockSpec(memory_space=pltpu.VMEM)
    message = jax.ShapeDtypeStruct((shard + 16, cols), BF)
    return pl.pallas_call(
        functools.partial(ctx_kernel, parts),
        in_specs=[pl.BlockSpec(memory_space=pltpu.SMEM)] + [vmem] * 5,
        out_shape=[jax.ShapeDtypeStruct((shard, cols), F32), jax.ShapeDtypeStruct((16, cols), BF)] + [message] * (parts - 1),
        scratch_shapes=[pltpu.VMEM((2 * half, cols), F32)],
        compiler_params=pltpu.CompilerParams(vmem_limit_bytes=VMEM_LIMIT),
        cost_estimate=pl.CostEstimate(flops=LATE, bytes_accessed=0, transcendentals=0),
        name="to_ctx",
    )(at, top, top_came, low, low_came, own)


def ffn_kernel(xo_ref, xm_ref, go_ref, gm_ref, w_ref, yo_ref, ym_ref, do_ref, dm_ref, inner_ref, gain_ref):
    units = w_ref.shape[1] // 3
    step = pl.program_id(0)
    early = step < pl.num_programs(0) // 2
    x = jnp.where(early, xo_ref[...], xm_ref[...])
    g = jnp.where(early, go_ref[...], gm_ref[...])
    raised = dot(x, w_ref[:, : 2 * units], NN)
    gate = raised[:, :units]
    upper = raised[:, units:]
    sig = 1.0 / (1.0 + jnp.exp(-gate))
    silu = gate * sig
    act = (silu * upper).astype(BF)
    y = dot(act, w_ref[:, 2 * units :], NT).astype(BF)
    d_act = dot(g, w_ref[:, 2 * units :], NN)
    d_gate = (d_act * upper * (sig + silu * (1.0 - sig))).astype(BF)
    d_up = (d_act * silu).astype(BF)
    inner_ref[:, :units] = d_gate
    inner_ref[:, units : 2 * units] = d_up
    inner_ref[:, 2 * units :] = act
    d_x = dot(inner_ref[:, : 2 * units], w_ref[:, : 2 * units], NT)
    gain_row = jnp.sum(d_x * x.astype(F32), axis=0, keepdims=True)
    dx = d_x.astype(BF)

    @pl.when(early)
    def _():
        yo_ref[...] = y
        do_ref[...] = dx

    @pl.when(jnp.logical_not(early))
    def _():
        ym_ref[...] = y
        dm_ref[...] = dx

    @pl.when(step == 0)
    def _():
        gain_ref[...] = gain_row

    @pl.when(step > 0)
    def _():
        gain_ref[...] += gain_row


def ffn_weight_kernel(xo_ref, xm_ref, go_ref, gm_ref, inner_ref, grad_ref, sum_ref):
    units = inner_ref.shape[1] // 3
    step = pl.program_id(0)
    early = step < pl.num_programs(0) // 2
    x = jnp.where(early, xo_ref[...], xm_ref[...])
    g = jnp.where(early, go_ref[...], gm_ref[...])
    left = dot(x, inner_ref[:, : 2 * units], TN)
    right = dot(g, inner_ref[:, 2 * units :], TN)

    @pl.when(step == 0)
    def _():
        sum_ref[:, : 2 * units] = left
        sum_ref[:, 2 * units :] = right

    @pl.when((step > 0) & (step < pl.num_programs(0) - 1))
    def _():
        sum_ref[:, : 2 * units] += left
        sum_ref[:, 2 * units :] += right

    @pl.when(step == pl.num_programs(0) - 1)
    def _():
        grad_ref[:, : 2 * units] = (sum_ref[:, : 2 * units] + left).astype(BF)
        grad_ref[:, 2 * units :] = (sum_ref[:, 2 * units :] + right).astype(BF)


def ffn_specs(tokens, width, units3, rows):
    steps = tokens // rows
    other = pl.BlockSpec((rows, width), lambda i: (jnp.minimum(i, steps - 1), 0))
    mine = pl.BlockSpec((rows, width), lambda i: (jnp.maximum(i - steps, 0), 0))
    whole = pl.BlockSpec((width, units3), lambda i: (0, 0))
    inner = pl.BlockSpec((rows, units3), lambda i: (i, 0))
    return 2 * steps, other, mine, whole, inner


def feed_forward(x_mine, x_other, g_mine, g_other, w, rows):
    tokens, width = x_mine.shape
    units3 = w.shape[1]
    grid, other, mine, whole, inner = ffn_specs(tokens, width, units3, rows)
    part = jax.ShapeDtypeStruct((tokens, width), BF)
    y_other, y_mine, dx_other, dx_mine, inside, gain_row = pl.pallas_call(
        ffn_kernel,
        grid=(grid,),
        in_specs=[other, mine, other, mine, whole],
        out_specs=[other, mine, other, mine, inner, pl.BlockSpec((1, width), lambda i: (0, 0))],
        out_shape=[
            part, part, part, part,
            jax.ShapeDtypeStruct((2 * tokens, units3), BF), jax.ShapeDtypeStruct((1, width), F32),
        ],
        compiler_params=pltpu.CompilerParams(vmem_limit_bytes=VMEM_LIMIT),
        cost_estimate=pl.CostEstimate(
            flops=8 * tokens * width * units3, bytes_accessed=24 << 20, transcendentals=2 * tokens * units3 // 3
        ),
        name="feed_forward",
    )(x_other, x_mine, g_other, g_mine, w)
    return y_mine, y_other, dx_mine, dx_other, inside, gain_row[0]


def ffn_weight_grads(x_mine, x_other, g_mine, g_other, inside, rows):
    tokens, width = x_mine.shape
    units3 = inside.shape[1]
    grid, other, mine, whole, inner = ffn_specs(tokens, width, units3, rows)
    return pl.pallas_call(
        ffn_weight_kernel,
        grid=(grid,),
        in_specs=[other, mine, other, mine, inner],
        out_specs=whole,
        out_shape=jax.ShapeDtypeStruct((width, units3), BF),
        scratch_shapes=[pltpu.VMEM((width, units3), F32)],
        compiler_params=pltpu.CompilerParams(vmem_limit_bytes=VMEM_LIMIT),
        cost_estimate=pl.CostEstimate(flops=16 << 30, bytes_accessed=24 << 20, transcendentals=0),
        name="ffn_weight_grads",
    )(x_other, x_mine, g_other, g_mine, inside)


def same_kernel(in_ref, out_ref):
    pass


def same(value, flops):
    return pl.pallas_call(
        same_kernel,
        in_specs=[pl.BlockSpec(memory_space=pl.ANY)],
        out_specs=pl.BlockSpec(memory_space=pl.ANY),
        out_shape=jax.ShapeDtypeStruct(value.shape, value.dtype),
        input_output_aliases={0: 0},
        cost_estimate=pl.CostEstimate(flops=flops, bytes_accessed=0, transcendentals=0),
        name="same",
    )(value)


def pack_kernel(gate_ref, up_ref, down_ref, out_ref):
    parts, shard, units3 = out_ref.shape
    units = units3 // 3
    have = gate_ref.shape[1]
    for t in range(parts):
        for j, ref in enumerate((gate_ref, up_ref, down_ref)):
            first = min(t * units, have)
            count = min((t + 1) * units, have) - first
            if count:
                out_ref[t, :, j * units : j * units + count] = ref[:, first : first + count]
            if count < units:
                out_ref[t, :, j * units + count : (j + 1) * units] = jnp.zeros((shard, units - count), BF)


def pack(gate, up, down, parts, units):
    shard = gate.shape[0]
    return pl.pallas_call(
        pack_kernel,
        out_shape=jax.ShapeDtypeStruct((parts, shard, 3 * units), BF),
        compiler_params=pltpu.CompilerParams(vmem_limit_bytes=VMEM_LIMIT),
        name="pack",
    )(gate, up, down)


def finish_kernel(parts_ref, gate_ref, up_ref, down_ref):
    parts, shard, units3 = parts_ref.shape
    units = units3 // 3
    have = gate_ref.shape[1]
    for t in range(parts):
        for j, ref in enumerate((gate_ref, up_ref, down_ref)):
            first = min(t * units, have)
            count = min((t + 1) * units, have) - first
            if count:
                ref[:, first : first + count] = parts_ref[t, :, j * units : j * units + count].astype(F32)


def finish(parts, columns):
    whole = jax.ShapeDtypeStruct((parts.shape[1], columns), F32)
    return pl.pallas_call(
        finish_kernel,
        out_shape=[whole, whole, whole],
        compiler_params=pltpu.CompilerParams(vmem_limit_bytes=VMEM_LIMIT),
        name="finish",
    )(parts)


def inverse_rms(values):
    return lax.rsqrt(jnp.mean(values * values, axis=-1, keepdims=True) + EPS)


def norm_back(values, gain, grad):
    inverse = inverse_rms(values)
    normal = values * inverse
    scaled = grad * gain
    return inverse * (scaled - normal * jnp.mean(scaled * normal, axis=-1, keepdims=True))


def body(
    hidden_in,
    seq_lengths,
    attn_gain,
    query_gain,
    key_gain,
    query_weight,
    key_projection,
    value_projection,
    out_weight,
    ffn_gain,
    gate_weight,
    up_weight,
    down_weight,
    cotangent,
):
    slots, shard_rows, width = hidden_in.shape
    n_fsdp = lax.axis_size("fsdp")
    n_ctx = lax.axis_size("ctx")
    f = lax.axis_index("fsdp")
    c = lax.axis_index("ctx")
    core = lax.axis_index("tp")
    rows = 2 * shard_rows
    keys = n_ctx * rows
    q_cols = query_weight.shape[1]
    k_cols = key_projection.shape[1]
    shard = query_weight.shape[0]
    ff_half = gate_weight.shape[1]
    units = ff_half // n_fsdp
    padded = -(-units // TILE) * TILE

    at = jnp.arange(keys)
    places = (c - at // rows) * rows + ((at // shard_rows) % 2 ^ core) * shard_rows + at % shard_rows
    lanes = jnp.arange(TILE)
    freqs = THETA ** (-((lanes % (HEAD // 2)).astype(F32) * 2.0 / HEAD))
    angles = places.astype(F32)[:, None] * freqs[None, :]
    cosine = jnp.cos(angles)
    sine = jnp.sin(angles) * jnp.where(lanes % HEAD < HEAD // 2, -1.0, 1.0)[None, :]
    scal = jnp.concatenate([jnp.stack([c, core, f]).astype(jnp.int32), seq_lengths])
    own_places = places[:shard_rows]
    valid = own_places[None, :, None] < seq_lengths[:, None, None]

    hidden = hidden_in.astype(F32)
    inverse_one = inverse_rms(hidden)
    normed = (hidden * inverse_one * attn_gain).astype(BF)

    def ctx_stack(pieces):
        stack = jnp.zeros((n_ctx,) + pieces[0].shape, pieces[0].dtype)
        for k, piece in enumerate(pieces):
            stack = lax.dynamic_update_index_in_dim(stack, piece, (c - k) % n_ctx, 0)
        return stack

    def fsdp_stack(pieces):
        stack = jnp.zeros((n_fsdp,) + pieces[0].shape, pieces[0].dtype)
        for m, piece in enumerate(pieces):
            stack = lax.dynamic_update_index_in_dim(stack, piece, f ^ m, 0)
        return stack

    def spread_halves(value):
        masks = [1 << i for i in range(8) if 1 << i < n_fsdp]
        halves = []
        for half, order in zip(jnp.split(value, 2), (masks, masks[::-1])):
            half = half[None]
            for mask in order:
                half = jnp.concatenate([half, fsdp_xor(half, mask)])
            halves.append(half)
        return halves

    def in_order(half, order):
        got = jnp.zeros_like(half)
        for i in range(n_fsdp):
            mask = sum(bit for j, bit in enumerate(order) if i >> j & 1)
            got = lax.dynamic_update_index_in_dim(got, half[i], f ^ mask, 0)
        return got

    def over_ctx(value):
        return [value] + [ctx_shift(value, k) for k in range(1, n_ctx)]

    def over_fsdp(value):
        return [value] + [fsdp_xor(value, m) for m in range(1, n_fsdp)]

    def part(array, index):
        return lax.dynamic_index_in_dim(array, index, 0, keepdims=False)

    def trade_parts(parts):
        return [part(parts, f)] + [fsdp_xor(part(parts, f ^ m), m) for m in range(1, n_fsdp)]

    ffn_packed = pack(gate_weight, up_weight, down_weight.T, n_fsdp, padded)
    packed = jnp.concatenate([query_weight, key_projection, value_projection, out_weight.T], axis=1)
    grad_rows = jnp.where(valid, cotangent, jnp.zeros_like(cotangent))
    x_pieces = [normed, ctx_up(normed)]
    ffn_rows = lax.all_to_all(ffn_packed, "fsdp", 0, 0, tiled=True)
    held = tie(*x_pieces, *over_ctx(packed))
    x_pieces = list(held[:2])
    stack = ctx_stack(held[2:]).reshape(n_ctx * shard, -1)

    top, bottom = spread_halves(stack)
    others = [swap_cores(piece) for piece in x_pieces]
    while len(x_pieces) < n_ctx:
        x_pieces.append(ctx_up(x_pieces[-1]))
        if len(x_pieces) == 3:
            ffn_rows, x_pieces[-1] = tie(ffn_rows, x_pieces[-1])
        others.append(swap_cores(x_pieces[-1]))
    ffn_w = lax.all_gather(ffn_rows, "ctx", axis=1, tiled=True).reshape(width, 3 * padded)
    ffn_w = same(ffn_w, 20 << 30)
    held = tie(*x_pieces, *others, grad_rows, top, bottom)
    x_pieces = held[:n_ctx]
    others = held[n_ctx : 2 * n_ctx]
    grad_rows, top, bottom = held[2 * n_ctx :]

    query_gain2 = jnp.tile(query_gain, 2)[None, :]
    key_gain2 = jnp.tile(key_gain, 2)[None, :]
    attn, stats, q_raw, k_raw, value, q_hat, k_hat, x_all = attend(
        scal, [piece for pair in zip(x_pieces, others) for piece in pair], (top, bottom), (q_cols, k_cols), cosine, sine,
        query_gain2, key_gain2,
    )
    held = tie(attn, *over_fsdp(grad_rows))
    attn = held[0]
    g_mine = jnp.stack(held[1:])
    g_other = swap_cores(g_mine)
    bits = [mask for mask in (1 << i for i in range(8)) if mask < n_fsdp]
    attn_w = jnp.stack([in_order(top, bits), in_order(bottom, bits[::-1])], axis=1).reshape(width, -1)
    out_w = attn_w[:, q_cols + 2 * k_cols :]

    branch = jnp.einsum("sth,dh->std", attn, out_w, preferred_element_type=F32)
    middle = hidden + (branch[:, :shard_rows] + swap_cores(branch[:, shard_rows:]))
    normed_two = (middle * inverse_rms(middle) * ffn_gain).astype(BF)
    x_mine = jnp.stack(over_fsdp(normed_two))
    x_other = swap_cores(x_mine)

    def flat(value):
        return value.reshape(-1, width)

    place = jnp.stack([f]).astype(jnp.int32)
    y_mine, y_other, dx_mine, dx_other, inside, ffn_gain_row = feed_forward(
        flat(x_mine), flat(x_other), flat(g_mine), flat(g_other), ffn_w, 2 * slots * shard_rows
    )

    def core_sums(mine, other):
        mine = mine.reshape(n_fsdp, slots, shard_rows, width)
        other = swap_cores(other.reshape(n_fsdp, slots, shard_rows, width))
        return [mine[m].astype(F32) + other[m].astype(F32) for m in range(n_fsdp)]

    def traded(sums):
        return [sums[0]] + [fsdp_xor(sums[m], m) for m in range(1, n_fsdp)]

    dx_sums = core_sums(dx_mine, dx_other)
    inside, *dx_sums = tie(inside, dx_sums[0], *[item.astype(BF) for item in dx_sums[1:]])
    y_sums = core_sums(y_mine, y_other)
    inside, *y_sums = tie(inside, y_sums[0], *[item.astype(BF) for item in y_sums[1:]])
    ffn_grads = ffn_weight_grads(
        flat(x_mine), flat(x_other), flat(g_mine), flat(g_other), inside, 2 * slots * shard_rows
    )
    ffn_grads, *held = tie(ffn_grads, *traded(dx_sums))
    ffn_reduced = lax.psum_scatter(
        ffn_grads.reshape(n_fsdp, n_ctx * shard, 3 * padded), "ctx", scatter_dimension=1, tiled=True
    )
    d_normed_two = sum(item.astype(F32) for item in held)
    d_middle = grad_rows.astype(F32) + norm_back(middle, ffn_gain, d_normed_two)
    d_mine = d_middle.astype(BF)
    d_other = swap_cores(d_mine)
    d_branch = jnp.concatenate([d_mine, d_other], axis=1)
    d_attn = jnp.einsum("std,dh->sth", d_branch, out_w, preferred_element_type=F32).astype(BF)
    held = tie(d_attn, *y_sums)
    d_attn = held[0]
    y_sums = held[1:]

    d_q, d_k, d_v, gq, gk = attend_back(
        scal, q_raw, k_raw, value, cosine, sine, query_gain2, key_gain2, q_hat, k_hat, attn, stats, d_attn
    )
    y_got = traded(y_sums)

    held = tie(d_q, d_k, d_v, gq, gk, ffn_gain_row, *y_got)
    d_q, d_k, d_v, gq, gk, ffn_gain_row = held[:6]
    result = jnp.where(valid, middle + sum(item.astype(F32) for item in held[6:]), 0.0).astype(BF)

    heads = jnp.stack([jnp.pad(item[0, :HEAD] + item[0, HEAD:], (0, HEAD)) for item in (gq, gk)])
    small = jnp.stack([jnp.zeros_like(ffn_gain), ffn_gain_row / ffn_gain])
    small = jnp.concatenate([small, heads], axis=1)
    small = jnp.pad(small, ((0, 0), (0, 2 * q_cols + 2 * k_cols - small.shape[1])))
    top_send, top, low_send, low = weight_grads(
        place, x_all, d_q, d_k, d_v, d_mine, d_other, attn, attn_w, attn_gain[None, :], two_parts(small), n_fsdp
    )
    top_send, top, low_send, low, d_q, d_k, d_v = tie(top_send, top, low_send, low, d_q, d_k, d_v)

    half = n_ctx * shard // 2
    bits = bits_of(n_fsdp)
    own = top_send[n_fsdp // 2 * half :]
    came = [fsdp_xor(top_send, bits[0]), fsdp_xor(low_send, bits[-1])]
    last_mine, last_other = input_grads(d_q, d_k, d_v, attn_w, n_ctx - 1, 1)
    last_other = swap_cores(last_other)
    mine, other = input_grads(d_q, d_k, d_v, attn_w, 0, n_ctx - 1)
    mine, other, last_other, *came = tie(mine, other, last_other, *came)
    other = swap_cores(other)
    total = ctx_down(down_add(last_mine, last_other, 0))
    block = n_ctx - 2
    for step in range(1, len(bits)):
        count = n_fsdp >> step
        sent = []
        kept = []
        for side, keep in enumerate((top, low)):
            order = bits if side == 0 else bits[::-1]
            masks = sorted(sum(bit for j, bit in enumerate(order[step:]) if i >> j & 1) for i in range(count))
            sends = [i for i, mask in enumerate(masks) if mask & order[step]]
            keeps = [i for i, mask in enumerate(masks) if not mask & order[step]]
            send, keep = half_sum(keep, came[side], own if side == 0 else None, half, sends, keeps)
            sent.append(send)
            kept.append(keep)
        if step == 1:
            total, other, mine, ffn_reduced, *held = tie(total, other, mine, ffn_reduced, *sent, *kept)
            sent, kept = held[:2], held[2:]
        top, low = kept
        own = sent[0][count // 2 * half :]
        came = [fsdp_xor(sent[0], bits[step]), fsdp_xor(sent[1], bits[-1 - step])]
        if block > 0:
            total = ctx_down(down_add(mine, other, block, total))
            block -= 1
            total, *came = tie(total, *came)
    ctx_place = jnp.stack([f, c]).astype(jnp.int32)
    mine_rows, small, *messages = to_ctx(ctx_place, top, came[0], low, came[1], own, n_ctx)
    while block > 0:
        total = ctx_down(down_add(mine, other, block, total))
        block -= 1
    got = [ctx_shift(message, k) for k, message in enumerate(messages, 1)]
    ffn_parts = lax.all_to_all(ffn_reduced, "fsdp", 0, 0, tiled=True)
    total = mine[0] + other[0].astype(F32) + total.astype(F32)

    small = [one_part(small)] + [one_part(piece[shard:]) for piece in got]
    got = [mine_rows] + [piece[:shard].astype(F32) for piece in got]
    gate_grad, up_grad, down_grad = finish(ffn_parts, ff_half)
    down_grad = down_grad.T
    attn_grads = sum(got)
    small = tree_sum(small)
    small = small + swap_cores(small)
    input_grad = (d_middle + norm_back(hidden, attn_gain, total)).astype(BF)
    qkv_total = attn_grads[:, : q_cols + 2 * k_cols]
    query_weight_grad = qkv_total[:, :q_cols]
    key_weight_grad = qkv_total[:, q_cols : q_cols + k_cols]
    value_weight_grad = qkv_total[:, q_cols + k_cols :]
    out_weight_grad = attn_grads[:, q_cols + 2 * k_cols :].T

    return (
        result,
        input_grad,
        small[0, :width],
        small[0, width : width + HEAD],
        small[1, width : width + HEAD],
        query_weight_grad,
        key_weight_grad,
        value_weight_grad,
        out_weight_grad,
        small[1, :width],
        gate_grad,
        up_grad,
        down_grad,
    )


def solution(mesh):
    in_specs = (
        P("fsdp", ("ctx", "tp"), None),
        P("fsdp"),
        P(),
        P(),
        P(),
        P(("fsdp", "ctx"), "tp"),
        P(("fsdp", "ctx"), "tp"),
        P(("fsdp", "ctx"), "tp"),
        P("tp", ("fsdp", "ctx")),
        P(),
        P(("fsdp", "ctx"), "tp"),
        P(("fsdp", "ctx"), "tp"),
        P("tp", ("fsdp", "ctx")),
        P("fsdp", ("ctx", "tp"), None),
    )
    out_specs = (
        P("fsdp", ("ctx", "tp"), None),
        P("fsdp", ("ctx", "tp"), None),
        P(),
        P(),
        P(),
        P(("fsdp", "ctx"), "tp"),
        P(("fsdp", "ctx"), "tp"),
        P(("fsdp", "ctx"), "tp"),
        P("tp", ("fsdp", "ctx")),
        P(),
        P(("fsdp", "ctx"), "tp"),
        P(("fsdp", "ctx"), "tp"),
        P("tp", ("fsdp", "ctx")),
    )
    return jax.shard_map(body, mesh=mesh, in_specs=in_specs, out_specs=out_specs, check_vma=False)
```

```python
import functools

import jax
import jax.numpy as jnp
import numpy as np
from jax import lax
from jax.experimental import pallas as pl
from jax.experimental.pallas import tpu as pltpu
from jax.sharding import PartitionSpec as P

HEAD = 64
TILE = 128
EPS = 1e-05
THETA = 1000000.0
SCALE = HEAD**-0.5
EXP2_SCALE = SCALE * float(np.log2(np.e))
FAR = -1e30
BF = jnp.bfloat16
F32 = jnp.float32
VMEM_LIMIT = 56 * 1024 * 1024
LATE = 12 << 30
LATER = 5 << 30


def dot(left, right, dims):
    return lax.dot_general(left, right, (dims, ((), ())), preferred_element_type=F32)


NN = ((1,), (0,))
NT = ((1,), (1,))
TN = ((0,), (0,))


def swap_cores(value):
    return lax.ppermute(value, "tp", [(0, 1), (1, 0)])


def fsdp_xor(value, mask):
    size = lax.axis_size("fsdp")
    return lax.ppermute(value, "fsdp", [(i, i ^ mask) for i in range(size)])


def ctx_up(value, step=1):
    size = lax.axis_size("ctx")
    return lax.ppermute(value, "ctx", [(i, i + step) for i in range(size - step)])


def ctx_down(value, step=1):
    size = lax.axis_size("ctx")
    return lax.ppermute(value, "ctx", [(i + step, i) for i in range(size - step)])


def ctx_shift(value, step):
    size = lax.axis_size("ctx")
    return lax.ppermute(value, "ctx", [(i, (i + step) % size) for i in range(size)])


def tree_sum(values):
    while len(values) > 1:
        half = len(values) // 2
        values = [values[i] + values[i + half] for i in range(half)]
    return values[0]


def two_parts(rows):
    first = rows.astype(BF)
    left = (rows - first.astype(F32)).astype(BF)
    return jnp.pad(jnp.concatenate([first, left]), ((0, 16 - 2 * rows.shape[0]), (0, 0)))


def one_part(rows):
    return rows[:2].astype(F32) + rows[2:4].astype(F32)


def tie(*values):
    return lax.optimization_barrier(values)


def lane_ids(rows):
    return lax.broadcasted_iota(jnp.int32, (rows, TILE), 1)


def half_swap(x):
    low = lane_ids(x.shape[0]) % HEAD < HEAD // 2
    return jnp.where(low, pltpu.roll(x, TILE - HEAD // 2, 1), pltpu.roll(x, HEAD // 2, 1))


def head_mean(x):
    first = lane_ids(x.shape[0]) < HEAD
    left = jnp.sum(jnp.where(first, x, 0.0), axis=1, keepdims=True)
    right = jnp.sum(jnp.where(first, 0.0, x), axis=1, keepdims=True)
    return jnp.where(first, left, right) * (1.0 / HEAD)


def prepare(x, gain, cosine, sine):
    scaled = x * lax.rsqrt(head_mean(x * x) + EPS) * gain
    return scaled * cosine + half_swap(scaled) * sine


def prepare_back(x, gain, cosine, sine, grad):
    grad = grad * cosine - half_swap(grad) * sine
    inverse = lax.rsqrt(head_mean(x * x) + EPS)
    normal = x * inverse
    gain_grad = jnp.sum(grad * normal, axis=0, keepdims=True)
    grad = grad * gain
    return inverse * (grad - normal * head_mean(grad * normal)), gain_grad


def key_bias(scal_ref, slot, keys, block_rows):
    c = scal_ref[0]
    core = scal_ref[1]
    length = scal_ref[3 + slot]
    half = block_rows // 2

    def places(index):
        block = index // block_rows
        side = (index // half) % 2
        return (c - block) * block_rows + (side + core - 2 * side * core) * half + index % half

    key_at = places(lax.broadcasted_iota(jnp.int32, (keys, block_rows), 0))
    query_at = places(lax.broadcasted_iota(jnp.int32, (keys, block_rows), 1))
    seen = (key_at >= 0) & (key_at <= query_at) & (key_at < length)
    return jnp.where(seen, 0.0, FAR)


def twins(x):
    first = lane_ids(x.shape[0]) < HEAD
    turned = pltpu.roll(x, HEAD, 1)
    return jnp.where(first, x, turned).astype(BF), jnp.where(first, turned, x).astype(BF)


def by_head(x):
    first = lane_ids(x.shape[0]) < HEAD
    none = jnp.zeros_like(x)
    return jnp.concatenate([jnp.where(first, x, none), jnp.where(first, none, x)])


def attend_kernel(n_pieces, n_parts, scal_ref, *refs):
    pieces = refs[:n_pieces]
    (
        tq_ref, tk_ref, tv_ref, bq_ref, bk_ref, bv_ref, cos_ref, sin_ref, qg_ref, kg_ref,
        o_ref, l_ref, qr_ref, kr_ref, v_ref, qh_ref, kh_ref, x_ref, bias_ref, wq_ref, wkv_ref,
    ) = refs[n_pieces:]
    rows = qr_ref.shape[1]
    keys = kr_ref.shape[1]
    half = rows // 2

    @pl.when(pl.program_id(1) == 0)
    def _():
        bias_ref[...] = key_bias(scal_ref, pl.program_id(0), keys, rows)
        for i, piece in enumerate(pieces):
            x_ref[0, i * half : (i + 1) * half] = piece[0]

    depth = tq_ref.shape[1]
    bits = [1 << i for i in range(8) if 1 << i < n_parts]
    for side, (query_w, key_w, value_w) in enumerate(((tq_ref, tk_ref, tv_ref), (bq_ref, bk_ref, bv_ref))):
        order = bits[::-1] if side else bits
        for i in range(n_parts):
            mask = sum(bit for j, bit in enumerate(order) if i >> j & 1)
            at = pl.ds(pl.multiple_of(((scal_ref[2] ^ mask) * 2 + side) * depth, depth), depth)
            wq_ref[at, :] = query_w[i]
            wkv_ref[at, :TILE] = key_w[i]
            wkv_ref[at, TILE:] = value_w[i]
    key_value = dot(x_ref[0], wkv_ref[...], NN)
    query_raw = dot(x_ref[0, :rows], wq_ref[...], NN)
    kr_ref[0] = key_value[:, :TILE]
    v_ref[0] = key_value[:, TILE:].astype(BF)
    qr_ref[0] = query_raw

    key = prepare(kr_ref[0], kg_ref[...], cos_ref[...], sin_ref[...]).astype(BF)
    kh_ref[0] = key
    key_twins = twins(key.astype(F32))
    value_twins = twins(v_ref[0].astype(F32))
    first = lane_ids(rows) < HEAD
    for pair in range(2):
        lanes = slice(pair * TILE, (pair + 1) * TILE)
        query = prepare(qr_ref[0, :, lanes], qg_ref[...], cos_ref[:rows], sin_ref[:rows]).astype(BF)
        qh_ref[0, :, lanes] = query
        scores = dot(key_twins[pair], by_head(query), NT)
        weights = jnp.exp2(scores * EXP2_SCALE + jnp.concatenate([bias_ref[...]] * 2, axis=1))
        inverse = 1.0 / jnp.sum(weights, axis=0, keepdims=True)
        l_ref[0, 0, pl.ds(2 * pair, 1), :] = inverse[:, :rows]
        l_ref[0, 0, pl.ds(2 * pair + 1, 1), :] = inverse[:, rows:]
        mixed = dot(weights.astype(BF), value_twins[pair], TN) * jnp.broadcast_to(inverse, (TILE, 2 * rows)).T
        o_ref[0, :, lanes] = jnp.where(first, mixed[:rows], mixed[rows:]).astype(BF)


def attend_back_kernel(
    scal_ref, q_ref, k_ref, v_ref, cos_ref, sin_ref, qg_ref, kg_ref, qh_ref, kh_ref, o_ref, l_ref, d_ref,
    dq_ref, dk_ref, dv_ref, gq_ref, gk_ref, bias_ref
):
    rows = q_ref.shape[1]
    keys = k_ref.shape[1]

    @pl.when(pl.program_id(1) == 0)
    def _():
        bias_ref[...] = key_bias(scal_ref, pl.program_id(0), keys, rows)

    key_twins = twins(kh_ref[0].astype(F32))
    value_twins = twins(v_ref[0].astype(F32))
    first = lane_ids(rows) < HEAD
    key_first = lane_ids(keys) < HEAD
    row_first = lax.broadcasted_iota(jnp.int32, (TILE, rows), 0) < HEAD
    key_grads = []
    value_grads = []
    query_gain = jnp.zeros((1, TILE), F32)
    for pair in range(2):
        lanes = slice(pair * TILE, (pair + 1) * TILE)
        query = qh_ref[0, :, lanes]
        grad = d_ref[0, :, lanes]
        product = (grad.astype(F32) * o_ref[0, :, lanes].astype(F32)).T
        key_grad = jnp.zeros((keys, TILE), F32)
        value_grad = jnp.zeros((keys, TILE), F32)
        query_grads = []
        for head in range(2):
            mine = first if head == 0 else jnp.logical_not(first)
            own_query = jnp.where(mine, query, jnp.zeros_like(query))
            own_grad = jnp.where(mine, grad, jnp.zeros_like(grad))
            inner = jnp.sum(product[head * HEAD : (head + 1) * HEAD], axis=0, keepdims=True)
            inverse = l_ref[0, 0, pl.ds(2 * pair + head, 1), :]
            scores = dot(key_twins[pair], own_query, NT)
            probs = jnp.exp2(scores * EXP2_SCALE + bias_ref[...]) * inverse
            grad_probs = dot(value_twins[pair], own_grad, NT)
            grad_scores = (probs * (grad_probs - inner)).astype(BF)
            query_grads.append(dot(grad_scores, key_twins[pair], TN))
            key_grad = key_grad + dot(grad_scores, own_query, NN)
            value_grad = value_grad + dot(probs.astype(BF), own_grad, NN)
        query_rot = jnp.where(first, query_grads[0], query_grads[1]) * SCALE
        raw, gain_part = prepare_back(q_ref[0, :, lanes], qg_ref[...], cos_ref[:rows], sin_ref[:rows], query_rot)
        dq_ref[0, :, lanes] = raw.astype(BF)
        query_gain = query_gain + gain_part
        key_grads.append(key_grad + pltpu.roll(key_grad, HEAD, 1))
        value_grads.append(value_grad + pltpu.roll(value_grad, HEAD, 1))
    dv_ref[0] = jnp.where(key_first, value_grads[0], value_grads[1]).astype(BF)
    key_rot = jnp.where(key_first, key_grads[0], key_grads[1]) * SCALE
    raw, key_gain = prepare_back(k_ref[0], kg_ref[...], cos_ref[...], sin_ref[...], key_rot)
    dk_ref[0] = raw.astype(BF)

    @pl.when((pl.program_id(0) == 0) & (pl.program_id(1) == 0))
    def _():
        gq_ref[...] = jnp.zeros_like(gq_ref)
        gk_ref[...] = jnp.zeros_like(gk_ref)

    gq_ref[...] += query_gain + pltpu.roll(query_gain, HEAD, 1)
    gk_ref[...] += key_gain + pltpu.roll(key_gain, HEAD, 1)


def attention_specs(slots, rows, keys):
    smem = pl.BlockSpec(memory_space=pltpu.SMEM)
    query = pl.BlockSpec((1, rows, 2 * TILE), lambda s, p: (s, 0, p))
    key = pl.BlockSpec((1, keys, TILE), lambda s, p: (s, 0, p))
    table = pl.BlockSpec((keys, TILE), lambda s, p: (0, 0))
    gain = pl.BlockSpec((1, TILE), lambda s, p: (0, 0))
    stat = pl.BlockSpec((1, 1, 8, rows), lambda s, p: (s, p, 0, 0))
    return smem, query, key, table, gain, stat


def attend(scal, pieces, weights, widths, cosine, sine, query_gain, key_gain):
    width, kv_width = widths
    slots, half, model = pieces[0].shape
    rows = 2 * half
    keys = len(pieces) * half
    smem, query, key, table, gain, stat = attention_specs(slots, rows, keys)
    pairs = kv_width // TILE
    piece = pl.BlockSpec((1, half, model), lambda s, p: (s, 0, 0))
    parts, depth = weights[0].shape[:2]
    w_query = pl.BlockSpec((parts, depth, 2 * TILE), lambda s, p: (0, 0, p))
    w_key = pl.BlockSpec((parts, depth, TILE), lambda s, p: (0, 0, width // TILE + p))
    w_value = pl.BlockSpec((parts, depth, TILE), lambda s, p: (0, 0, (width + kv_width) // TILE + p))
    return pl.pallas_call(
        functools.partial(attend_kernel, len(pieces), parts),
        grid=(slots, pairs),
        in_specs=[smem] + [piece] * len(pieces) + [w_query, w_key, w_value] * 2 + [table, table, gain, gain],
        out_specs=[
            query, stat, query, key, key, query, key, pl.BlockSpec((1, keys, model), lambda s, p: (s, 0, 0)),
        ],
        out_shape=[
            jax.ShapeDtypeStruct((slots, rows, width), BF),
            jax.ShapeDtypeStruct((slots, pairs, 8, rows), F32),
            jax.ShapeDtypeStruct((slots, rows, width), F32),
            jax.ShapeDtypeStruct((slots, keys, kv_width), F32),
            jax.ShapeDtypeStruct((slots, keys, kv_width), BF),
            jax.ShapeDtypeStruct((slots, rows, width), BF),
            jax.ShapeDtypeStruct((slots, keys, kv_width), BF),
            jax.ShapeDtypeStruct((slots, keys, model), BF),
        ],
        scratch_shapes=[
            pltpu.VMEM((keys, rows), F32),
            pltpu.VMEM((model, 2 * TILE), BF),
            pltpu.VMEM((model, 2 * TILE), BF),
        ],
        compiler_params=pltpu.CompilerParams(vmem_limit_bytes=VMEM_LIMIT),
        cost_estimate=pl.CostEstimate(flops=1 << 20, bytes_accessed=1 << 20, transcendentals=0),
        name="attend",
    )(scal, *pieces, *[item for item in weights for _ in range(3)], cosine, sine, query_gain, key_gain)


def attend_back(scal, q_raw, k_raw, value, cosine, sine, query_gain, key_gain, q_hat, k_hat, out, stats, grad):
    slots, rows, width = q_raw.shape
    keys, kv_width = k_raw.shape[1:]
    smem, query, key, table, gain, stat = attention_specs(slots, rows, keys)
    pairs = kv_width // TILE
    return pl.pallas_call(
        attend_back_kernel,
        grid=(slots, pairs),
        in_specs=[smem, query, key, key, table, table, gain, gain, query, key, query, stat, query],
        out_specs=[query, key, key, gain, gain],
        out_shape=[
            jax.ShapeDtypeStruct((slots, rows, width), BF),
            jax.ShapeDtypeStruct((slots, keys, kv_width), BF),
            jax.ShapeDtypeStruct((slots, keys, kv_width), BF),
            jax.ShapeDtypeStruct((1, TILE), F32),
            jax.ShapeDtypeStruct((1, TILE), F32),
        ],
        scratch_shapes=[pltpu.VMEM((keys, rows), F32)],
        compiler_params=pltpu.CompilerParams(vmem_limit_bytes=VMEM_LIMIT),
        cost_estimate=pl.CostEstimate(
            flops=24 << 30, bytes_accessed=12 << 20, transcendentals=0
        ),
        name="attend_back",
    )(scal, q_raw, k_raw, value, cosine, sine, query_gain, key_gain, q_hat, k_hat, out, stats, grad)


def bits_of(size):
    return [1 << i for i in range(8) if 1 << i < size]


def weight_kernel(parts, at_ref, x_ref, dq_ref, dk_ref, dv_ref, bm_ref, bo_ref, o_ref, w_ref, gain_ref, more_ref, *refs):
    top_send, top_keep, low_send, low_keep, own_ref, sum_ref = refs
    slots, rows, q_cols = dq_ref.shape
    k_cols = dk_ref.shape[2]
    depth = x_ref.shape[2]
    half = depth // 2
    m = pl.program_id(0)
    query = jnp.zeros((depth, q_cols), F32)
    key = jnp.zeros((depth, k_cols), F32)
    value = jnp.zeros((depth, k_cols), F32)
    out = jnp.zeros((depth, q_cols), F32)
    for s in range(slots):
        x = x_ref[s]
        query = query + dot(x[:rows], dq_ref[s], TN)
        key = key + dot(x, dk_ref[s], TN)
        value = value + dot(x, dv_ref[s], TN)
        out = out + dot(jnp.concatenate([bm_ref[s], bo_ref[s]]), o_ref[s], TN)
    total = jnp.concatenate([query, key, value, out], axis=1)
    product = total[:, : q_cols + 2 * k_cols] * w_ref[:, : q_cols + 2 * k_cols].astype(F32)
    ones = jnp.ones((8, q_cols + 2 * k_cols), BF)
    high = product.astype(BF)
    low = (product - high.astype(F32)).astype(BF)
    place = pl.ds(pl.multiple_of((at_ref[0] ^ m) * depth, TILE), depth)
    sum_ref[:, place] = dot(ones, high, NT) + dot(ones, low, NT)
    total = total.astype(BF)
    bits = bits_of(parts)
    for bit, rows_of, send, keep in (
        (bits[0], total[:half], top_send, top_keep),
        (bits[-1], total[half:], low_send, low_keep),
    ):
        chosen = [i for i in range(parts) if i & bit]
        for i in range(parts):
            ref = send if i & bit else keep
            rank = chosen.index(i | bit)

            @pl.when(m == i)
            def _(ref=ref, rank=rank, rows_of=rows_of):
                ref[rank * half : (rank + 1) * half] = rows_of

    @pl.when(m == parts - 1)
    def _():
        width = sum_ref.shape[1]
        row = sum_ref[:1] / gain_ref[...]
        first = row.astype(BF).astype(F32)
        left = row - first
        ids = lax.broadcasted_iota(jnp.int32, (16, width), 0)
        more = more_ref[...].astype(F32)
        here = jnp.where(ids == 0, first, jnp.where(ids == 2, left, more[:, :width]))
        for ref, rows_at in ((top_send, slice(parts // 2 * half, parts // 2 * half + 16)), (own_ref, slice(0, 16))):
            ref[rows_at, :width] = here.astype(BF)
            ref[rows_at, width:] = more_ref[:, width:]


def weight_grads(at, x, d_q, d_k, d_v, d_mine, d_other, attn, w, gain, more, parts):
    slots, keys, width = x.shape
    cols = 2 * d_q.shape[2] + 2 * d_k.shape[2]
    depth = width // parts
    rows = parts // 2 * (depth // 2)
    shapes = [(rows + more.shape[0], cols), (rows, cols), (rows, cols), (rows, cols), more.shape]
    spec = pltpu.PrefetchScalarGridSpec(
        num_scalar_prefetch=1,
        grid=(parts,),
        in_specs=[
            pl.BlockSpec((slots, keys, depth), lambda m, at: (0, 0, at[0] ^ m)),
            pl.BlockSpec(d_q.shape, lambda m, at: (0, 0, 0)),
            pl.BlockSpec(d_k.shape, lambda m, at: (0, 0, 0)),
            pl.BlockSpec(d_v.shape, lambda m, at: (0, 0, 0)),
            pl.BlockSpec(d_mine.shape[:2] + (depth,), lambda m, at: (0, 0, at[0] ^ m)),
            pl.BlockSpec(d_mine.shape[:2] + (depth,), lambda m, at: (0, 0, at[0] ^ m)),
            pl.BlockSpec(attn.shape, lambda m, at: (0, 0, 0)),
            pl.BlockSpec((depth, cols), lambda m, at: (at[0] ^ m, 0)),
            pl.BlockSpec(gain.shape, lambda m, at: (0, 0)),
            pl.BlockSpec(more.shape, lambda m, at: (0, 0)),
        ],
        out_specs=[pl.BlockSpec(shape, lambda m, at: (0, 0)) for shape in shapes],
        scratch_shapes=[pltpu.VMEM((8, width), F32)],
    )
    return pl.pallas_call(
        functools.partial(weight_kernel, parts),
        grid_spec=spec,
        out_shape=[jax.ShapeDtypeStruct(shape, BF) for shape in shapes],
        compiler_params=pltpu.CompilerParams(vmem_limit_bytes=VMEM_LIMIT),
        cost_estimate=pl.CostEstimate(flops=10 << 30, bytes_accessed=8 << 20, transcendentals=0),
        name="weight_grads",
    )(at, x, d_q, d_k, d_v, d_mine, d_other, attn, w, gain, more)


def input_kernel(with_own, dq_ref, dk_ref, dv_ref, w_ref, mine_ref, other_ref):
    slots, rows, q_cols = dq_ref.shape
    k_cols = dk_ref.shape[2]
    half = rows // 2
    for s in range(slots):
        d_x = dot(dk_ref[s], w_ref[:, q_cols : q_cols + k_cols], NT)
        d_x = d_x + dot(dv_ref[s], w_ref[:, q_cols + k_cols : q_cols + 2 * k_cols], NT)
        mine_ref[0, s] = d_x[:half]
        other_ref[0, s] = d_x[half:].astype(BF)

    @pl.when(with_own & (pl.program_id(0) == 0))
    def _():
        for s in range(slots):
            d_x = dot(dq_ref[s], w_ref[:, :q_cols], NT)
            mine_ref[0, s] += d_x[:half]
            other_ref[0, s] = (other_ref[0, s].astype(F32) + d_x[half:]).astype(BF)


def input_grads(d_q, d_k, d_v, w, first, blocks):
    slots, rows, q_cols = d_q.shape
    k_cols = d_k.shape[2]
    width = w.shape[0]
    part = pl.BlockSpec((slots, rows, k_cols), lambda r: (0, r + first, 0))
    out = pl.BlockSpec((1, slots, rows // 2, width), lambda r: (r, 0, 0, 0))
    return pl.pallas_call(
        functools.partial(input_kernel, first == 0),
        grid=(blocks,),
        in_specs=[
            pl.BlockSpec(d_q.shape, lambda r: (0, 0, 0)),
            part,
            part,
            pl.BlockSpec(w.shape, lambda r: (0, 0)),
        ],
        out_specs=[out, out],
        out_shape=[
            jax.ShapeDtypeStruct((blocks, slots, rows // 2, width), F32),
            jax.ShapeDtypeStruct((blocks, slots, rows // 2, width), BF),
        ],
        compiler_params=pltpu.CompilerParams(vmem_limit_bytes=VMEM_LIMIT),
        cost_estimate=pl.CostEstimate(flops=6 << 30, bytes_accessed=1 << 20, transcendentals=0),
        name="input_grads",
    )(d_q, d_k, d_v, w)


def in_parts(rows):
    first = rows.astype(BF).astype(F32)
    return jnp.concatenate([first, rows - first, jnp.zeros((12, rows.shape[1]), F32)]).astype(BF)


def down_kernel(*refs):
    mine_ref, other_ref, *came, out_ref = refs
    total = mine_ref[0] + other_ref[0].astype(F32)
    if came:
        total = total + came[0][...].astype(F32)
    out_ref[...] = total.astype(BF)


def down_add(mine, other, block, *came):
    shape = mine.shape[1:]
    one = pl.BlockSpec((1, 1) + shape[1:], lambda s: (block, s, 0, 0))
    here = pl.BlockSpec((1,) + shape[1:], lambda s: (s, 0, 0))
    return pl.pallas_call(
        down_kernel,
        grid=(shape[0],),
        in_specs=[one, one] + [here] * len(came),
        out_specs=here,
        out_shape=jax.ShapeDtypeStruct(shape, BF),
        cost_estimate=pl.CostEstimate(flops=LATER, bytes_accessed=0, transcendentals=0),
        name="down_add",
    )(mine, other, *came)


def last_kernel(mine_ref, other_ref, came_ref, middle_ref, hidden_ref, gain_ref, out_ref):
    grad = (mine_ref[0, 0] + other_ref[0, 0].astype(F32) + came_ref[0].astype(F32)) * gain_ref[...]
    values = hidden_ref[0].astype(F32)
    inverse = lax.rsqrt(jnp.mean(values * values, axis=1, keepdims=True) + EPS)
    normal = values * inverse
    back = inverse * (grad - normal * jnp.mean(grad * normal, axis=1, keepdims=True))
    out_ref[0] = (middle_ref[0] + back).astype(BF)


def last_step(mine, other, came, d_middle, hidden, gain):
    slots, rows, width = hidden.shape
    block = pl.BlockSpec((1, 1, rows, width), lambda s: (0, s, 0, 0))
    here = pl.BlockSpec((1, rows, width), lambda s: (s, 0, 0))
    return pl.pallas_call(
        last_kernel,
        grid=(slots,),
        in_specs=[block, block, here, here, here, pl.BlockSpec((1, width), lambda s: (0, 0))],
        out_specs=here,
        out_shape=jax.ShapeDtypeStruct((slots, rows, width), BF),
        cost_estimate=pl.CostEstimate(flops=2 << 30, bytes_accessed=0, transcendentals=0),
        name="last_step",
    )(mine, other, came, d_middle, hidden, gain)


def half_kernel(half, sends, keeps, extra, keep_ref, came_ref, *refs):
    own_ref = refs[0] if extra else None
    send_ref, left_ref = refs[-2:]
    for ranks, ref in ((sends, send_ref), (keeps, left_ref)):
        for place, i in enumerate(ranks):
            rows = slice(i * half, (i + 1) * half)
            total = keep_ref[rows].astype(F32) + came_ref[rows].astype(F32)
            ref[place * half : (place + 1) * half] = total.astype(BF)
    if extra:
        ours, theirs = own_ref[...].astype(F32), came_ref[-16:].astype(F32)
        send_ref[len(sends) * half :] = in_parts((ours[:2] + ours[2:4]) + (theirs[:2] + theirs[2:4]))


def half_sum(keep, came, own, half, sends, keeps):
    cols = keep.shape[1]
    riding = 0 if own is None else 16
    return pl.pallas_call(
        functools.partial(half_kernel, half, sends, keeps, own is not None),
        out_shape=[
            jax.ShapeDtypeStruct((len(sends) * half + riding, cols), BF),
            jax.ShapeDtypeStruct((len(keeps) * half, cols), BF),
        ],
        compiler_params=pltpu.CompilerParams(vmem_limit_bytes=VMEM_LIMIT),
        cost_estimate=pl.CostEstimate(flops=LATE, bytes_accessed=0, transcendentals=0),
        name="half_sum",
    )(keep, came, *(() if own is None else (own,)))


def ctx_kernel(parts, at_ref, top_ref, top_came, low_ref, low_came, own_ref, mine_ref, small_ref, *refs):
    *sends, sum_ref = refs
    half = top_ref.shape[0]
    shard = mine_ref.shape[0]
    sum_ref[:half] = top_ref[...].astype(F32) + top_came[:half].astype(F32)
    sum_ref[half:] = low_ref[...].astype(F32) + low_came[...].astype(F32)
    ours, theirs = own_ref[...].astype(F32), top_came[half:].astype(F32)
    small = in_parts((ours[:2] + ours[2:4]) + (theirs[:2] + theirs[2:4]))
    small_ref[...] = small

    def rows(k):
        return sum_ref[pl.ds(pl.multiple_of(((at_ref[1] + k) % parts) * shard, 8), shard)]

    mine_ref[...] = rows(0)
    for k, ref in enumerate(sends, 1):
        ref[:shard] = rows(k).astype(BF)
        ref[shard:] = small


def to_ctx(at, top, top_came, low, low_came, own, parts):
    half, cols = top.shape
    shard = 2 * half // parts
    vmem = pl.BlockSpec(memory_space=pltpu.VMEM)
    message = jax.ShapeDtypeStruct((shard + 16, cols), BF)
    return pl.pallas_call(
        functools.partial(ctx_kernel, parts),
        in_specs=[pl.BlockSpec(memory_space=pltpu.SMEM)] + [vmem] * 5,
        out_shape=[jax.ShapeDtypeStruct((shard, cols), F32), jax.ShapeDtypeStruct((16, cols), BF)] + [message] * (parts - 1),
        scratch_shapes=[pltpu.VMEM((2 * half, cols), F32)],
        compiler_params=pltpu.CompilerParams(vmem_limit_bytes=VMEM_LIMIT),
        cost_estimate=pl.CostEstimate(flops=LATE, bytes_accessed=0, transcendentals=0),
        name="to_ctx",
    )(at, top, top_came, low, low_came, own)


def ffn_block(x, g, w_ref, inner_ref):
    units = w_ref.shape[1] // 3
    raised = dot(x, w_ref[:, : 2 * units], NN)
    gate = raised[:, :units]
    upper = raised[:, units:]
    sig = 1.0 / (1.0 + jnp.exp(-gate))
    silu = gate * sig
    act = (silu * upper).astype(BF)
    y = dot(act, w_ref[:, 2 * units :], NT).astype(BF)
    d_act = dot(g, w_ref[:, 2 * units :], NN)
    inner_ref[:, :units] = (d_act * upper * (sig + silu * (1.0 - sig))).astype(BF)
    inner_ref[:, units : 2 * units] = (d_act * silu).astype(BF)
    inner_ref[:, 2 * units :] = act
    d_x = dot(inner_ref[:, : 2 * units], w_ref[:, : 2 * units], NT)
    return y, d_x.astype(BF), jnp.sum(d_x * x.astype(F32), axis=0, keepdims=True)


def ffn_kernel(xm_ref, xo_ref, gm_ref, go_ref, w_ref, ym_ref, yo_ref, dm_ref, do_ref, inner_ref, gain_ref):
    half = xm_ref.shape[0]
    x = jnp.concatenate([xm_ref[...], xo_ref[...]])
    g = jnp.concatenate([gm_ref[...], go_ref[...]])
    y, d_x, gain_row = ffn_block(x, g, w_ref, inner_ref)
    ym_ref[...] = y[:half]
    yo_ref[...] = y[half:]
    dm_ref[...] = d_x[:half]
    do_ref[...] = d_x[half:]

    @pl.when(pl.program_id(0) == 0)
    def _():
        gain_ref[...] = gain_row

    @pl.when(pl.program_id(0) > 0)
    def _():
        gain_ref[...] += gain_row


def ffn_rest_kernel(
    xm_ref, xo_ref, gm_ref, go_ref, w_ref, inside_ref, ym_ref, yo_ref, dm_ref, do_ref, gain_ref, grad_ref, inner_ref, sum_ref
):
    units = w_ref.shape[1] // 3
    half = xm_ref.shape[0]
    step = pl.program_id(0)
    x = jnp.concatenate([xm_ref[...], xo_ref[...]])
    g = jnp.concatenate([gm_ref[...], go_ref[...]])

    @pl.when(step == 0)
    def _():
        y, d_x, gain_row = ffn_block(x, g, w_ref, inner_ref)
        ym_ref[...] = y[:half]
        yo_ref[...] = y[half:]
        dm_ref[...] = d_x[:half]
        do_ref[...] = d_x[half:]
        gain_ref[...] = gain_row

    @pl.when(step > 0)
    def _():
        inner_ref[...] = inside_ref[...]

    left = dot(x, inner_ref[:, : 2 * units], TN)
    right = dot(g, inner_ref[:, 2 * units :], TN)

    @pl.when(step == 0)
    def _():
        sum_ref[:, : 2 * units] = left
        sum_ref[:, 2 * units :] = right

    @pl.when((step > 0) & (step < pl.num_programs(0) - 1))
    def _():
        sum_ref[:, : 2 * units] += left
        sum_ref[:, 2 * units :] += right

    @pl.when(step == pl.num_programs(0) - 1)
    def _():
        grad_ref[:, : 2 * units] = (sum_ref[:, : 2 * units] + left).astype(BF)
        grad_ref[:, 2 * units :] = (sum_ref[:, 2 * units :] + right).astype(BF)


def feed_forward(x_mine, x_other, g_mine, g_other, w, parts):
    tokens, width = x_mine.shape
    rows = tokens // parts
    units3 = w.shape[1]
    block = pl.BlockSpec((rows, width), lambda i: (i + 1, 0))
    out = pl.BlockSpec((rows, width), lambda i: (i, 0))
    part = jax.ShapeDtypeStruct((tokens - rows, width), BF)
    return pl.pallas_call(
        ffn_kernel,
        grid=(parts - 1,),
        in_specs=[block] * 4 + [pl.BlockSpec((width, units3), lambda i: (0, 0))],
        out_specs=[out] * 4 + [pl.BlockSpec((2 * rows, units3), lambda i: (i, 0)), pl.BlockSpec((1, width), lambda i: (0, 0))],
        out_shape=[part] * 4
        + [jax.ShapeDtypeStruct((2 * (tokens - rows), units3), BF), jax.ShapeDtypeStruct((1, width), F32)],
        compiler_params=pltpu.CompilerParams(vmem_limit_bytes=VMEM_LIMIT),
        cost_estimate=pl.CostEstimate(flops=8 * tokens * width * units3, bytes_accessed=24 << 20, transcendentals=0),
        name="feed_forward",
    )(x_mine, x_other, g_mine, g_other, w)


def ffn_rest(x_mine, x_other, g_mine, g_other, w, inside, parts):
    tokens, width = x_mine.shape
    rows = tokens // parts
    units3 = w.shape[1]
    block = pl.BlockSpec((rows, width), lambda i: (i, 0))
    whole = pl.BlockSpec((width, units3), lambda i: (0, 0))
    own = pl.BlockSpec((rows, width), lambda i: (0, 0))
    part = jax.ShapeDtypeStruct((rows, width), BF)
    return pl.pallas_call(
        ffn_rest_kernel,
        grid=(parts,),
        in_specs=[block] * 4 + [whole, pl.BlockSpec((2 * rows, units3), lambda i: (jnp.maximum(i - 1, 0), 0))],
        out_specs=[own] * 4 + [pl.BlockSpec((1, width), lambda i: (0, 0)), whole],
        out_shape=[part] * 4
        + [jax.ShapeDtypeStruct((1, width), F32), jax.ShapeDtypeStruct((width, units3), BF)],
        scratch_shapes=[pltpu.VMEM((2 * rows, units3), BF), pltpu.VMEM((width, units3), F32)],
        compiler_params=pltpu.CompilerParams(vmem_limit_bytes=VMEM_LIMIT),
        cost_estimate=pl.CostEstimate(flops=24 << 30, bytes_accessed=24 << 20, transcendentals=0),
        name="ffn_rest",
    )(x_mine, x_other, g_mine, g_other, w, inside)


def same_kernel(in_ref, out_ref):
    pass


def same(value, flops):
    return pl.pallas_call(
        same_kernel,
        in_specs=[pl.BlockSpec(memory_space=pl.ANY)],
        out_specs=pl.BlockSpec(memory_space=pl.ANY),
        out_shape=jax.ShapeDtypeStruct(value.shape, value.dtype),
        input_output_aliases={0: 0},
        cost_estimate=pl.CostEstimate(flops=flops, bytes_accessed=0, transcendentals=0),
        name="same",
    )(value)


def pack_kernel(gate_ref, up_ref, down_ref, out_ref):
    parts, shard, units3 = out_ref.shape
    units = units3 // 3
    have = gate_ref.shape[1]
    for t in range(parts):
        for j, ref in enumerate((gate_ref, up_ref, down_ref)):
            first = min(t * units, have)
            count = min((t + 1) * units, have) - first
            if count:
                out_ref[t, :, j * units : j * units + count] = ref[:, first : first + count]
            if count < units:
                out_ref[t, :, j * units + count : (j + 1) * units] = jnp.zeros((shard, units - count), BF)


def pack(gate, up, down, parts, units):
    shard = gate.shape[0]
    return pl.pallas_call(
        pack_kernel,
        out_shape=jax.ShapeDtypeStruct((parts, shard, 3 * units), BF),
        compiler_params=pltpu.CompilerParams(vmem_limit_bytes=VMEM_LIMIT),
        name="pack",
    )(gate, up, down)


def finish_kernel(parts_ref, gate_ref, up_ref, down_ref):
    parts, shard, units3 = parts_ref.shape
    units = units3 // 3
    have = gate_ref.shape[1]
    for t in range(parts):
        for j, ref in enumerate((gate_ref, up_ref, down_ref)):
            first = min(t * units, have)
            count = min((t + 1) * units, have) - first
            if count:
                ref[:, first : first + count] = parts_ref[t, :, j * units : j * units + count].astype(F32)


def finish(parts, columns):
    whole = jax.ShapeDtypeStruct((parts.shape[1], columns), F32)
    return pl.pallas_call(
        finish_kernel,
        out_shape=[whole, whole, whole],
        compiler_params=pltpu.CompilerParams(vmem_limit_bytes=VMEM_LIMIT),
        name="finish",
    )(parts)


def inverse_rms(values):
    return lax.rsqrt(jnp.mean(values * values, axis=-1, keepdims=True) + EPS)


def norm_back(values, gain, grad):
    inverse = inverse_rms(values)
    normal = values * inverse
    scaled = grad * gain
    return inverse * (scaled - normal * jnp.mean(scaled * normal, axis=-1, keepdims=True))


def body(
    hidden_in,
    seq_lengths,
    attn_gain,
    query_gain,
    key_gain,
    query_weight,
    key_projection,
    value_projection,
    out_weight,
    ffn_gain,
    gate_weight,
    up_weight,
    down_weight,
    cotangent,
):
    slots, shard_rows, width = hidden_in.shape
    n_fsdp = lax.axis_size("fsdp")
    n_ctx = lax.axis_size("ctx")
    f = lax.axis_index("fsdp")
    c = lax.axis_index("ctx")
    core = lax.axis_index("tp")
    rows = 2 * shard_rows
    keys = n_ctx * rows
    q_cols = query_weight.shape[1]
    k_cols = key_projection.shape[1]
    shard = query_weight.shape[0]
    ff_half = gate_weight.shape[1]
    units = ff_half // n_fsdp
    padded = -(-units // TILE) * TILE

    at = jnp.arange(keys)
    places = (c - at // rows) * rows + ((at // shard_rows) % 2 ^ core) * shard_rows + at % shard_rows
    lanes = jnp.arange(TILE)
    freqs = THETA ** (-((lanes % (HEAD // 2)).astype(F32) * 2.0 / HEAD))
    angles = places.astype(F32)[:, None] * freqs[None, :]
    cosine = jnp.cos(angles)
    sine = jnp.sin(angles) * jnp.where(lanes % HEAD < HEAD // 2, -1.0, 1.0)[None, :]
    scal = jnp.concatenate([jnp.stack([c, core, f]).astype(jnp.int32), seq_lengths])
    own_places = places[:shard_rows]
    valid = own_places[None, :, None] < seq_lengths[:, None, None]

    hidden = hidden_in.astype(F32)
    inverse_one = inverse_rms(hidden)
    normed = (hidden * inverse_one * attn_gain).astype(BF)

    def ctx_stack(pieces):
        stack = jnp.zeros((n_ctx,) + pieces[0].shape, pieces[0].dtype)
        for k, piece in enumerate(pieces):
            stack = lax.dynamic_update_index_in_dim(stack, piece, (c - k) % n_ctx, 0)
        return stack

    def fsdp_stack(pieces):
        stack = jnp.zeros((n_fsdp,) + pieces[0].shape, pieces[0].dtype)
        for m, piece in enumerate(pieces):
            stack = lax.dynamic_update_index_in_dim(stack, piece, f ^ m, 0)
        return stack

    def spread_halves(value):
        masks = [1 << i for i in range(8) if 1 << i < n_fsdp]
        halves = []
        for half, order in zip(jnp.split(value, 2), (masks, masks[::-1])):
            half = half[None]
            for mask in order:
                half = jnp.concatenate([half, fsdp_xor(half, mask)])
            halves.append(half)
        return halves

    def in_order(half, order):
        got = jnp.zeros_like(half)
        for i in range(n_fsdp):
            mask = sum(bit for j, bit in enumerate(order) if i >> j & 1)
            got = lax.dynamic_update_index_in_dim(got, half[i], f ^ mask, 0)
        return got

    def over_ctx(value):
        return [value] + [ctx_shift(value, k) for k in range(1, n_ctx)]

    def over_fsdp(value):
        return [value] + [fsdp_xor(value, m) for m in range(1, n_fsdp)]

    def part(array, index):
        return lax.dynamic_index_in_dim(array, index, 0, keepdims=False)

    def trade_parts(parts):
        return [part(parts, f)] + [fsdp_xor(part(parts, f ^ m), m) for m in range(1, n_fsdp)]

    ffn_packed = pack(gate_weight, up_weight, down_weight.T, n_fsdp, padded)
    packed = jnp.concatenate([query_weight, key_projection, value_projection, out_weight.T], axis=1)
    grad_rows = jnp.where(valid, cotangent, jnp.zeros_like(cotangent))
    x_pieces = [normed, ctx_up(normed)]
    ffn_rows = lax.all_to_all(ffn_packed, "fsdp", 0, 0, tiled=True)
    held = tie(*x_pieces, *over_ctx(packed))
    x_pieces = list(held[:2])
    stack = ctx_stack(held[2:]).reshape(n_ctx * shard, -1)

    top, bottom = spread_halves(stack)
    others = [swap_cores(piece) for piece in x_pieces]
    while len(x_pieces) < n_ctx:
        x_pieces.append(ctx_up(x_pieces[-1]))
        if len(x_pieces) == 3:
            ffn_rows, x_pieces[-1] = tie(ffn_rows, x_pieces[-1])
        others.append(swap_cores(x_pieces[-1]))
    ffn_w = lax.all_gather(ffn_rows, "ctx", axis=1, tiled=True).reshape(width, 3 * padded)
    ffn_w = same(ffn_w, 60 << 30)
    held = tie(*x_pieces, *others, grad_rows, top, bottom)
    x_pieces = held[:n_ctx]
    others = held[n_ctx : 2 * n_ctx]
    grad_rows, top, bottom = held[2 * n_ctx :]

    query_gain2 = jnp.tile(query_gain, 2)[None, :]
    key_gain2 = jnp.tile(key_gain, 2)[None, :]
    attn, stats, q_raw, k_raw, value, q_hat, k_hat, x_all = attend(
        scal, [piece for pair in zip(x_pieces, others) for piece in pair], (top, bottom), (q_cols, k_cols), cosine, sine,
        query_gain2, key_gain2,
    )
    held = tie(attn, *over_fsdp(grad_rows))
    attn = held[0]
    g_mine = jnp.stack(held[1:])
    g_other = swap_cores(g_mine)
    bits = [mask for mask in (1 << i for i in range(8)) if mask < n_fsdp]
    attn_w = jnp.stack([in_order(top, bits), in_order(bottom, bits[::-1])], axis=1).reshape(width, -1)
    out_w = attn_w[:, q_cols + 2 * k_cols :]

    branch = jnp.einsum("sth,dh->std", attn, out_w, preferred_element_type=F32)
    middle = hidden + (branch[:, :shard_rows] + swap_cores(branch[:, shard_rows:]))
    normed_two = (middle * inverse_rms(middle) * ffn_gain).astype(BF)
    x_mine = jnp.stack(over_fsdp(normed_two))
    x_other = swap_cores(x_mine)

    def flat(value):
        return value.reshape(-1, width)

    place = jnp.stack([f]).astype(jnp.int32)

    tokens = (flat(x_mine), flat(x_other), flat(g_mine), flat(g_other))
    y_mine, y_other, dx_mine, dx_other, inside, gain_row = feed_forward(*tokens, ffn_w, n_fsdp)

    def core_sums(mine, other):
        mine = mine.reshape(n_fsdp - 1, slots, shard_rows, width)
        other = swap_cores(other.reshape(n_fsdp - 1, slots, shard_rows, width))
        return [(mine[m].astype(F32) + other[m].astype(F32)).astype(BF) for m in range(n_fsdp - 1)]

    def traded(sums):
        return [fsdp_xor(item, m) for m, item in enumerate(sums, 1)]

    def own(value):
        return value.reshape(slots, shard_rows, width)

    inside, *dx_sums = tie(inside, *core_sums(dx_mine, dx_other))
    inside, *y_sums = tie(inside, *core_sums(y_mine, y_other))
    y_mine, y_other, dx_mine, dx_other, own_gain_row, ffn_grads = ffn_rest(*tokens, ffn_w, inside, n_fsdp)
    ffn_gain_row = (gain_row + own_gain_row)[0]
    ffn_grads, dx_mine, dx_other, *held = tie(ffn_grads, dx_mine, dx_other, *traded(dx_sums))
    ffn_reduced = lax.psum_scatter(
        ffn_grads.reshape(n_fsdp, n_ctx * shard, 3 * padded), "ctx", scatter_dimension=1, tiled=True
    )
    d_normed_two = own(dx_mine).astype(F32) + swap_cores(own(dx_other)).astype(F32)
    d_normed_two = d_normed_two + sum(item.astype(F32) for item in held)
    d_middle = grad_rows.astype(F32) + norm_back(middle, ffn_gain, d_normed_two)
    d_mine = d_middle.astype(BF)
    d_other = swap_cores(d_mine)
    d_branch = jnp.concatenate([d_mine, d_other], axis=1)
    d_attn = jnp.einsum("std,dh->sth", d_branch, out_w, preferred_element_type=F32).astype(BF)
    held = tie(d_attn, *y_sums)
    d_attn = held[0]
    y_sums = held[1:]

    d_q, d_k, d_v, gq, gk = attend_back(
        scal, q_raw, k_raw, value, cosine, sine, query_gain2, key_gain2, q_hat, k_hat, attn, stats, d_attn
    )
    y_got = [own(y_mine), swap_cores(own(y_other))] + traded(y_sums)

    held = tie(d_q, d_k, d_v, gq, gk, ffn_gain_row, *y_got)
    d_q, d_k, d_v, gq, gk, ffn_gain_row = held[:6]
    result = jnp.where(valid, middle + sum(item.astype(F32) for item in held[6:]), 0.0).astype(BF)

    heads = jnp.concatenate([gq, gk])
    small = jnp.stack([jnp.zeros_like(ffn_gain), ffn_gain_row / ffn_gain])
    small = jnp.concatenate([small, heads], axis=1)
    small = jnp.pad(small, ((0, 0), (0, 2 * q_cols + 2 * k_cols - small.shape[1])))
    top_send, top, low_send, low, own = weight_grads(
        place, x_all, d_q, d_k, d_v, d_mine, d_other, attn, attn_w, attn_gain[None, :], two_parts(small), n_fsdp
    )
    top_send, top, low_send, low, own, d_q, d_k, d_v = tie(top_send, top, low_send, low, own, d_q, d_k, d_v)

    half = n_ctx * shard // 2
    bits = bits_of(n_fsdp)
    came = [fsdp_xor(top_send, bits[0]), fsdp_xor(low_send, bits[-1])]
    last_mine, last_other = input_grads(d_q, d_k, d_v, attn_w, n_ctx - 1, 1)
    last_other = swap_cores(last_other)
    mine, other = input_grads(d_q, d_k, d_v, attn_w, 0, n_ctx - 1)
    mine, other, last_other, result, *came = tie(mine, other, last_other, result, *came)
    other = swap_cores(other)
    total = ctx_down(down_add(last_mine, last_other, 0))
    block = n_ctx - 2
    for step in range(1, len(bits)):
        count = n_fsdp >> step
        sent = []
        kept = []
        for side, keep in enumerate((top, low)):
            order = bits if side == 0 else bits[::-1]
            masks = sorted(sum(bit for j, bit in enumerate(order[step:]) if i >> j & 1) for i in range(count))
            sends = [i for i, mask in enumerate(masks) if mask & order[step]]
            keeps = [i for i, mask in enumerate(masks) if not mask & order[step]]
            send, keep = half_sum(keep, came[side], own if side == 0 else None, half, sends, keeps)
            sent.append(send)
            kept.append(keep)
        if step == 1:
            total, other, mine, ffn_reduced, *held = tie(total, other, mine, ffn_reduced, *sent, *kept)
            sent, kept = held[:2], held[2:]
        top, low = kept
        own = sent[0][count // 2 * half :]
        came = [fsdp_xor(sent[0], bits[step]), fsdp_xor(sent[1], bits[-1 - step])]
        if block > 0:
            total = ctx_down(down_add(mine, other, block, total))
            block -= 1
            total, ffn_reduced, *came = tie(total, ffn_reduced, *came)
    ctx_place = jnp.stack([f, c]).astype(jnp.int32)
    mine_rows, small, *messages = to_ctx(ctx_place, top, came[0], low, came[1], own, n_ctx)
    while block > 0:
        total = ctx_down(down_add(mine, other, block, total))
        block -= 1
    got = [ctx_shift(message, k) for k, message in enumerate(messages, 1)]
    ffn_parts = lax.all_to_all(ffn_reduced, "fsdp", 0, 0, tiled=True)
    gate_grad, up_grad, down_grad = finish(ffn_parts, ff_half)
    total, gate_grad, up_grad, down_grad = tie(total, gate_grad, up_grad, down_grad)
    small = [one_part(small)] + [one_part(piece[shard:]) for piece in got]
    got = [mine_rows] + [piece[:shard].astype(F32) for piece in got]
    down_grad = down_grad.T
    attn_grads = sum(got)
    small = tree_sum(small)
    small = small + swap_cores(small)
    input_grad = last_step(mine, other, total, d_middle, hidden_in, attn_gain[None, :])
    qkv_total = attn_grads[:, : q_cols + 2 * k_cols]
    query_weight_grad = qkv_total[:, :q_cols]
    key_weight_grad = qkv_total[:, q_cols : q_cols + k_cols]
    value_weight_grad = qkv_total[:, q_cols + k_cols :]
    out_weight_grad = attn_grads[:, q_cols + 2 * k_cols :].T

    return (
        result,
        input_grad,
        small[0, :width],
        small[0, width : width + HEAD],
        small[1, width : width + HEAD],
        query_weight_grad,
        key_weight_grad,
        value_weight_grad,
        out_weight_grad,
        small[1, :width],
        gate_grad,
        up_grad,
        down_grad,
    )


def solution(mesh):
    in_specs = (
        P("fsdp", ("ctx", "tp"), None),
        P("fsdp"),
        P(),
        P(),
        P(),
        P(("fsdp", "ctx"), "tp"),
        P(("fsdp", "ctx"), "tp"),
        P(("fsdp", "ctx"), "tp"),
        P("tp", ("fsdp", "ctx")),
        P(),
        P(("fsdp", "ctx"), "tp"),
        P(("fsdp", "ctx"), "tp"),
        P("tp", ("fsdp", "ctx")),
        P("fsdp", ("ctx", "tp"), None),
    )
    out_specs = (
        P("fsdp", ("ctx", "tp"), None),
        P("fsdp", ("ctx", "tp"), None),
        P(),
        P(),
        P(),
        P(("fsdp", "ctx"), "tp"),
        P(("fsdp", "ctx"), "tp"),
        P(("fsdp", "ctx"), "tp"),
        P("tp", ("fsdp", "ctx")),
        P(),
        P(("fsdp", "ctx"), "tp"),
        P(("fsdp", "ctx"), "tp"),
        P("tp", ("fsdp", "ctx")),
    )
    return jax.shard_map(body, mesh=mesh, in_specs=in_specs, out_specs=out_specs, check_vma=False)
```

```python
import functools

import jax
import jax.numpy as jnp
import numpy as np
from jax import lax
from jax.experimental import pallas as pl
from jax.experimental.pallas import tpu as pltpu
from jax.sharding import PartitionSpec as P

HEAD = 64
TILE = 128
EPS = 1e-05
THETA = 1000000.0
SCALE = HEAD**-0.5
EXP2_SCALE = SCALE * float(np.log2(np.e))
FAR = -1e30
BF = jnp.bfloat16
F32 = jnp.float32
VMEM_LIMIT = 56 * 1024 * 1024
LATE = 12 << 30
LATER = 5 << 30


def dot(left, right, dims):
    return lax.dot_general(left, right, (dims, ((), ())), preferred_element_type=F32)


NN = ((1,), (0,))
NT = ((1,), (1,))
TN = ((0,), (0,))


def swap_cores(value):
    return lax.ppermute(value, "tp", [(0, 1), (1, 0)])


def fsdp_xor(value, mask):
    size = lax.axis_size("fsdp")
    return lax.ppermute(value, "fsdp", [(i, i ^ mask) for i in range(size)])


def ctx_up(value, step=1):
    size = lax.axis_size("ctx")
    return lax.ppermute(value, "ctx", [(i, i + step) for i in range(size - step)])


def ctx_down(value, step=1):
    size = lax.axis_size("ctx")
    return lax.ppermute(value, "ctx", [(i + step, i) for i in range(size - step)])


def ctx_round(value):
    return ctx_shift(value, lax.axis_size("ctx") - 1)


def ctx_shift(value, step):
    size = lax.axis_size("ctx")
    return lax.ppermute(value, "ctx", [(i, (i + step) % size) for i in range(size)])


def tree_sum(values):
    while len(values) > 1:
        half = len(values) // 2
        values = [values[i] + values[i + half] for i in range(half)]
    return values[0]


def two_parts(rows):
    first = rows.astype(BF)
    left = (rows - first.astype(F32)).astype(BF)
    return jnp.pad(jnp.concatenate([first, left]), ((0, 16 - 2 * rows.shape[0]), (0, 0)))


def one_part(rows):
    return rows[:2].astype(F32) + rows[2:4].astype(F32)


def tie(*values):
    return lax.optimization_barrier(values)


def lane_ids(rows):
    return lax.broadcasted_iota(jnp.int32, (rows, TILE), 1)


def half_swap(x):
    low = lane_ids(x.shape[0]) % HEAD < HEAD // 2
    return jnp.where(low, pltpu.roll(x, TILE - HEAD // 2, 1), pltpu.roll(x, HEAD // 2, 1))


def head_mean(x):
    first = lane_ids(x.shape[0]) < HEAD
    left = jnp.sum(jnp.where(first, x, 0.0), axis=1, keepdims=True)
    right = jnp.sum(jnp.where(first, 0.0, x), axis=1, keepdims=True)
    return jnp.where(first, left, right) * (1.0 / HEAD)


def prepare(x, gain, cosine, sine):
    scaled = x * lax.rsqrt(head_mean(x * x) + EPS) * gain
    return scaled * cosine + half_swap(scaled) * sine


def prepare_back(x, gain, cosine, sine, grad):
    grad = grad * cosine - half_swap(grad) * sine
    inverse = lax.rsqrt(head_mean(x * x) + EPS)
    normal = x * inverse
    gain_grad = jnp.sum(grad * normal, axis=0, keepdims=True)
    grad = grad * gain
    return inverse * (grad - normal * head_mean(grad * normal)), gain_grad


def key_bias(scal_ref, slot, keys, block_rows):
    c = scal_ref[0]
    core = scal_ref[1]
    length = scal_ref[3 + slot]
    half = block_rows // 2

    def places(index):
        block = index // block_rows
        side = (index // half) % 2
        return (c - block) * block_rows + (side + core - 2 * side * core) * half + index % half

    key_at = places(lax.broadcasted_iota(jnp.int32, (keys, block_rows), 0))
    query_at = places(lax.broadcasted_iota(jnp.int32, (keys, block_rows), 1))
    seen = (key_at >= 0) & (key_at <= query_at) & (key_at < length)
    return jnp.where(seen, 0.0, FAR)


def twins(x):
    first = lane_ids(x.shape[0]) < HEAD
    turned = pltpu.roll(x, HEAD, 1)
    return jnp.where(first, x, turned).astype(BF), jnp.where(first, turned, x).astype(BF)


def by_head(x):
    first = lane_ids(x.shape[0]) < HEAD
    none = jnp.zeros_like(x)
    return jnp.concatenate([jnp.where(first, x, none), jnp.where(first, none, x)])


def attend_kernel(n_pieces, n_parts, scal_ref, *refs):
    pieces = refs[:n_pieces]
    (
        tq_ref, tk_ref, tv_ref, bq_ref, bk_ref, bv_ref, cos_ref, sin_ref, qg_ref, kg_ref,
        o_ref, l_ref, qr_ref, kr_ref, v_ref, qh_ref, kh_ref, x_ref, bias_ref, wq_ref, wkv_ref,
    ) = refs[n_pieces:]
    rows = qr_ref.shape[1]
    keys = kr_ref.shape[1]
    half = rows // 2

    @pl.when(pl.program_id(1) == 0)
    def _():
        bias_ref[...] = key_bias(scal_ref, pl.program_id(0), keys, rows)
        for i, piece in enumerate(pieces):
            x_ref[0, i * half : (i + 1) * half] = piece[0]

    depth = tq_ref.shape[1]
    bits = [1 << i for i in range(8) if 1 << i < n_parts]
    for side, (query_w, key_w, value_w) in enumerate(((tq_ref, tk_ref, tv_ref), (bq_ref, bk_ref, bv_ref))):
        order = bits[::-1] if side else bits
        for i in range(n_parts):
            mask = sum(bit for j, bit in enumerate(order) if i >> j & 1)
            at = pl.ds(pl.multiple_of(((scal_ref[2] ^ mask) * 2 + side) * depth, depth), depth)
            wq_ref[at, :] = query_w[i]
            wkv_ref[at, :TILE] = key_w[i]
            wkv_ref[at, TILE:] = value_w[i]
    key_value = dot(x_ref[0], wkv_ref[...], NN)
    query_raw = dot(x_ref[0, :rows], wq_ref[...], NN)
    kr_ref[0] = key_value[:, :TILE]
    v_ref[0] = key_value[:, TILE:].astype(BF)
    qr_ref[0] = query_raw

    key = prepare(kr_ref[0], kg_ref[...], cos_ref[...], sin_ref[...]).astype(BF)
    kh_ref[0] = key
    key_twins = twins(key.astype(F32))
    value_twins = twins(v_ref[0].astype(F32))
    first = lane_ids(rows) < HEAD
    for pair in range(2):
        lanes = slice(pair * TILE, (pair + 1) * TILE)
        query = prepare(qr_ref[0, :, lanes], qg_ref[...], cos_ref[:rows], sin_ref[:rows]).astype(BF)
        qh_ref[0, :, lanes] = query
        scores = dot(key_twins[pair], by_head(query), NT)
        weights = jnp.exp2(scores * EXP2_SCALE + jnp.concatenate([bias_ref[...]] * 2, axis=1))
        inverse = 1.0 / jnp.sum(weights, axis=0, keepdims=True)
        l_ref[0, 0, pl.ds(2 * pair, 1), :] = inverse[:, :rows]
        l_ref[0, 0, pl.ds(2 * pair + 1, 1), :] = inverse[:, rows:]
        mixed = dot(weights.astype(BF), value_twins[pair], TN) * jnp.broadcast_to(inverse, (TILE, 2 * rows)).T
        o_ref[0, :, lanes] = jnp.where(first, mixed[:rows], mixed[rows:]).astype(BF)


def attend_back_kernel(
    scal_ref, q_ref, k_ref, v_ref, cos_ref, sin_ref, qg_ref, kg_ref, qh_ref, kh_ref, o_ref, l_ref, d_ref,
    dq_ref, dk_ref, dv_ref, gq_ref, gk_ref, bias_ref
):
    rows = q_ref.shape[1]
    keys = k_ref.shape[1]

    @pl.when(pl.program_id(1) == 0)
    def _():
        bias_ref[...] = key_bias(scal_ref, pl.program_id(0), keys, rows)

    key_twins = twins(kh_ref[0].astype(F32))
    value_twins = twins(v_ref[0].astype(F32))
    first = lane_ids(rows) < HEAD
    key_first = lane_ids(keys) < HEAD
    row_first = lax.broadcasted_iota(jnp.int32, (TILE, rows), 0) < HEAD
    key_grads = []
    value_grads = []
    query_gain = jnp.zeros((1, TILE), F32)
    for pair in range(2):
        lanes = slice(pair * TILE, (pair + 1) * TILE)
        query = qh_ref[0, :, lanes]
        grad = d_ref[0, :, lanes]
        product = (grad.astype(F32) * o_ref[0, :, lanes].astype(F32)).T
        key_grad = jnp.zeros((keys, TILE), F32)
        value_grad = jnp.zeros((keys, TILE), F32)
        query_grads = []
        for head in range(2):
            mine = first if head == 0 else jnp.logical_not(first)
            own_query = jnp.where(mine, query, jnp.zeros_like(query))
            own_grad = jnp.where(mine, grad, jnp.zeros_like(grad))
            inner = jnp.sum(product[head * HEAD : (head + 1) * HEAD], axis=0, keepdims=True)
            inverse = l_ref[0, 0, pl.ds(2 * pair + head, 1), :]
            scores = dot(key_twins[pair], own_query, NT)
            probs = jnp.exp2(scores * EXP2_SCALE + bias_ref[...]) * inverse
            grad_probs = dot(value_twins[pair], own_grad, NT)
            grad_scores = (probs * (grad_probs - inner)).astype(BF)
            query_grads.append(dot(grad_scores, key_twins[pair], TN))
            key_grad = key_grad + dot(grad_scores, own_query, NN)
            value_grad = value_grad + dot(probs.astype(BF), own_grad, NN)
        query_rot = jnp.where(first, query_grads[0], query_grads[1]) * SCALE
        raw, gain_part = prepare_back(q_ref[0, :, lanes], qg_ref[...], cos_ref[:rows], sin_ref[:rows], query_rot)
        dq_ref[0, :, lanes] = raw.astype(BF)
        query_gain = query_gain + gain_part
        key_grads.append(key_grad + pltpu.roll(key_grad, HEAD, 1))
        value_grads.append(value_grad + pltpu.roll(value_grad, HEAD, 1))
    dv_ref[0] = jnp.where(key_first, value_grads[0], value_grads[1]).astype(BF)
    key_rot = jnp.where(key_first, key_grads[0], key_grads[1]) * SCALE
    raw, key_gain = prepare_back(k_ref[0], kg_ref[...], cos_ref[...], sin_ref[...], key_rot)
    dk_ref[0] = raw.astype(BF)

    @pl.when((pl.program_id(0) == 0) & (pl.program_id(1) == 0))
    def _():
        gq_ref[...] = jnp.zeros_like(gq_ref)
        gk_ref[...] = jnp.zeros_like(gk_ref)

    gq_ref[...] += query_gain + pltpu.roll(query_gain, HEAD, 1)
    gk_ref[...] += key_gain + pltpu.roll(key_gain, HEAD, 1)


def attention_specs(slots, rows, keys):
    smem = pl.BlockSpec(memory_space=pltpu.SMEM)
    query = pl.BlockSpec((1, rows, 2 * TILE), lambda s, p: (s, 0, p))
    key = pl.BlockSpec((1, keys, TILE), lambda s, p: (s, 0, p))
    table = pl.BlockSpec((keys, TILE), lambda s, p: (0, 0))
    gain = pl.BlockSpec((1, TILE), lambda s, p: (0, 0))
    stat = pl.BlockSpec((1, 1, 8, rows), lambda s, p: (s, p, 0, 0))
    return smem, query, key, table, gain, stat


def attend(scal, pieces, weights, widths, cosine, sine, query_gain, key_gain):
    width, kv_width = widths
    slots, half, model = pieces[0].shape
    rows = 2 * half
    keys = len(pieces) * half
    smem, query, key, table, gain, stat = attention_specs(slots, rows, keys)
    pairs = kv_width // TILE
    piece = pl.BlockSpec((1, half, model), lambda s, p: (s, 0, 0))
    parts, depth = weights[0].shape[:2]
    w_query = pl.BlockSpec((parts, depth, 2 * TILE), lambda s, p: (0, 0, p))
    w_key = pl.BlockSpec((parts, depth, TILE), lambda s, p: (0, 0, width // TILE + p))
    w_value = pl.BlockSpec((parts, depth, TILE), lambda s, p: (0, 0, (width + kv_width) // TILE + p))
    return pl.pallas_call(
        functools.partial(attend_kernel, len(pieces), parts),
        grid=(slots, pairs),
        in_specs=[smem] + [piece] * len(pieces) + [w_query, w_key, w_value] * 2 + [table, table, gain, gain],
        out_specs=[
            query, stat, query, key, key, query, key, pl.BlockSpec((1, keys, model), lambda s, p: (s, 0, 0)),
        ],
        out_shape=[
            jax.ShapeDtypeStruct((slots, rows, width), BF),
            jax.ShapeDtypeStruct((slots, pairs, 8, rows), F32),
            jax.ShapeDtypeStruct((slots, rows, width), F32),
            jax.ShapeDtypeStruct((slots, keys, kv_width), F32),
            jax.ShapeDtypeStruct((slots, keys, kv_width), BF),
            jax.ShapeDtypeStruct((slots, rows, width), BF),
            jax.ShapeDtypeStruct((slots, keys, kv_width), BF),
            jax.ShapeDtypeStruct((slots, keys, model), BF),
        ],
        scratch_shapes=[
            pltpu.VMEM((keys, rows), F32),
            pltpu.VMEM((model, 2 * TILE), BF),
            pltpu.VMEM((model, 2 * TILE), BF),
        ],
        compiler_params=pltpu.CompilerParams(vmem_limit_bytes=VMEM_LIMIT),
        cost_estimate=pl.CostEstimate(flops=1 << 20, bytes_accessed=1 << 20, transcendentals=0),
        name="attend",
    )(scal, *pieces, *[item for item in weights for _ in range(3)], cosine, sine, query_gain, key_gain)


def attend_back(scal, q_raw, k_raw, value, cosine, sine, query_gain, key_gain, q_hat, k_hat, out, stats, grad):
    slots, rows, width = q_raw.shape
    keys, kv_width = k_raw.shape[1:]
    smem, query, key, table, gain, stat = attention_specs(slots, rows, keys)
    pairs = kv_width // TILE
    return pl.pallas_call(
        attend_back_kernel,
        grid=(slots, pairs),
        in_specs=[smem, query, key, key, table, table, gain, gain, query, key, query, stat, query],
        out_specs=[query, key, key, gain, gain],
        out_shape=[
            jax.ShapeDtypeStruct((slots, rows, width), BF),
            jax.ShapeDtypeStruct((slots, keys, kv_width), BF),
            jax.ShapeDtypeStruct((slots, keys, kv_width), BF),
            jax.ShapeDtypeStruct((1, TILE), F32),
            jax.ShapeDtypeStruct((1, TILE), F32),
        ],
        scratch_shapes=[pltpu.VMEM((keys, rows), F32)],
        compiler_params=pltpu.CompilerParams(vmem_limit_bytes=VMEM_LIMIT),
        cost_estimate=pl.CostEstimate(
            flops=24 << 30, bytes_accessed=12 << 20, transcendentals=0
        ),
        name="attend_back",
    )(scal, q_raw, k_raw, value, cosine, sine, query_gain, key_gain, q_hat, k_hat, out, stats, grad)


def bits_of(size):
    return [1 << i for i in range(8) if 1 << i < size]


def weight_kernel(parts, at_ref, x_ref, dq_ref, dk_ref, dv_ref, bm_ref, bo_ref, o_ref, w_ref, gain_ref, more_ref, *refs):
    top_send, top_keep, low_send, low_keep, own_ref, sum_ref = refs
    slots, rows, q_cols = dq_ref.shape
    k_cols = dk_ref.shape[2]
    depth = x_ref.shape[2]
    half = depth // 2
    m = pl.program_id(0)
    query = jnp.zeros((depth, q_cols), F32)
    key = jnp.zeros((depth, k_cols), F32)
    value = jnp.zeros((depth, k_cols), F32)
    out = jnp.zeros((depth, q_cols), F32)
    for s in range(slots):
        x = x_ref[s]
        query = query + dot(x[:rows], dq_ref[s], TN)
        key = key + dot(x, dk_ref[s], TN)
        value = value + dot(x, dv_ref[s], TN)
        out = out + dot(jnp.concatenate([bm_ref[s], bo_ref[s]]), o_ref[s], TN)
    total = jnp.concatenate([query, key, value, out], axis=1)
    product = total[:, : q_cols + 2 * k_cols] * w_ref[:, : q_cols + 2 * k_cols].astype(F32)
    ones = jnp.ones((8, q_cols + 2 * k_cols), BF)
    high = product.astype(BF)
    low = (product - high.astype(F32)).astype(BF)
    place = pl.ds(pl.multiple_of((at_ref[0] ^ m) * depth, TILE), depth)
    sum_ref[:, place] = dot(ones, high, NT) + dot(ones, low, NT)
    total = total.astype(BF)
    bits = bits_of(parts)
    for bit, rows_of, send, keep in (
        (bits[0], total[:half], top_send, top_keep),
        (bits[-1], total[half:], low_send, low_keep),
    ):
        chosen = [i for i in range(parts) if i & bit]
        for i in range(parts):
            ref = send if i & bit else keep
            rank = chosen.index(i | bit)

            @pl.when(m == i)
            def _(ref=ref, rank=rank, rows_of=rows_of):
                ref[rank * half : (rank + 1) * half] = rows_of

    @pl.when(m == parts - 1)
    def _():
        width = sum_ref.shape[1]
        row = sum_ref[:1] / gain_ref[...]
        first = row.astype(BF).astype(F32)
        left = row - first
        ids = lax.broadcasted_iota(jnp.int32, (16, width), 0)
        more = more_ref[...].astype(F32)
        here = jnp.where(ids == 0, first, jnp.where(ids == 2, left, more[:, :width]))
        for ref, rows_at in ((top_send, slice(parts // 2 * half, parts // 2 * half + 16)), (own_ref, slice(0, 16))):
            ref[rows_at, :width] = here.astype(BF)
            ref[rows_at, width:] = more_ref[:, width:]


def weight_grads(at, x, d_q, d_k, d_v, d_mine, d_other, attn, w, gain, more, parts):
    slots, keys, width = x.shape
    cols = 2 * d_q.shape[2] + 2 * d_k.shape[2]
    depth = width // parts
    rows = parts // 2 * (depth // 2)
    shapes = [(rows + more.shape[0], cols), (rows, cols), (rows, cols), (rows, cols), more.shape]
    spec = pltpu.PrefetchScalarGridSpec(
        num_scalar_prefetch=1,
        grid=(parts,),
        in_specs=[
            pl.BlockSpec((slots, keys, depth), lambda m, at: (0, 0, at[0] ^ m)),
            pl.BlockSpec(d_q.shape, lambda m, at: (0, 0, 0)),
            pl.BlockSpec(d_k.shape, lambda m, at: (0, 0, 0)),
            pl.BlockSpec(d_v.shape, lambda m, at: (0, 0, 0)),
            pl.BlockSpec(d_mine.shape[:2] + (depth,), lambda m, at: (0, 0, at[0] ^ m)),
            pl.BlockSpec(d_mine.shape[:2] + (depth,), lambda m, at: (0, 0, at[0] ^ m)),
            pl.BlockSpec(attn.shape, lambda m, at: (0, 0, 0)),
            pl.BlockSpec((depth, cols), lambda m, at: (at[0] ^ m, 0)),
            pl.BlockSpec(gain.shape, lambda m, at: (0, 0)),
            pl.BlockSpec(more.shape, lambda m, at: (0, 0)),
        ],
        out_specs=[pl.BlockSpec(shape, lambda m, at: (0, 0)) for shape in shapes],
        scratch_shapes=[pltpu.VMEM((8, width), F32)],
    )
    return pl.pallas_call(
        functools.partial(weight_kernel, parts),
        grid_spec=spec,
        out_shape=[jax.ShapeDtypeStruct(shape, BF) for shape in shapes],
        compiler_params=pltpu.CompilerParams(vmem_limit_bytes=VMEM_LIMIT),
        cost_estimate=pl.CostEstimate(flops=10 << 30, bytes_accessed=8 << 20, transcendentals=0),
        name="weight_grads",
    )(at, x, d_q, d_k, d_v, d_mine, d_other, attn, w, gain, more)


def input_kernel(with_own, dq_ref, dk_ref, dv_ref, w_ref, mine_ref, other_ref):
    slots, rows, q_cols = dq_ref.shape
    k_cols = dk_ref.shape[2]
    half = rows // 2
    for s in range(slots):
        d_x = dot(dk_ref[s], w_ref[:, q_cols : q_cols + k_cols], NT)
        d_x = d_x + dot(dv_ref[s], w_ref[:, q_cols + k_cols : q_cols + 2 * k_cols], NT)
        mine_ref[0, s] = d_x[:half]
        other_ref[0, s] = d_x[half:].astype(BF)

    @pl.when(with_own & (pl.program_id(0) == 0))
    def _():
        for s in range(slots):
            d_x = dot(dq_ref[s], w_ref[:, :q_cols], NT)
            mine_ref[0, s] += d_x[:half]
            other_ref[0, s] = (other_ref[0, s].astype(F32) + d_x[half:]).astype(BF)


def input_grads(d_q, d_k, d_v, w, first, blocks):
    slots, rows, q_cols = d_q.shape
    k_cols = d_k.shape[2]
    width = w.shape[0]
    part = pl.BlockSpec((slots, rows, k_cols), lambda r: (0, r + first, 0))
    out = pl.BlockSpec((1, slots, rows // 2, width), lambda r: (r, 0, 0, 0))
    return pl.pallas_call(
        functools.partial(input_kernel, first == 0),
        grid=(blocks,),
        in_specs=[
            pl.BlockSpec(d_q.shape, lambda r: (0, 0, 0)),
            part,
            part,
            pl.BlockSpec(w.shape, lambda r: (0, 0)),
        ],
        out_specs=[out, out],
        out_shape=[
            jax.ShapeDtypeStruct((blocks, slots, rows // 2, width), F32),
            jax.ShapeDtypeStruct((blocks, slots, rows // 2, width), BF),
        ],
        compiler_params=pltpu.CompilerParams(vmem_limit_bytes=VMEM_LIMIT),
        cost_estimate=pl.CostEstimate(flops=6 << 30, bytes_accessed=1 << 20, transcendentals=0),
        name="input_grads",
    )(d_q, d_k, d_v, w)


def in_parts(rows):
    first = rows.astype(BF).astype(F32)
    return jnp.concatenate([first, rows - first, jnp.zeros((12, rows.shape[1]), F32)]).astype(BF)


def down_kernel(*refs):
    mine_ref, other_ref, *came, out_ref = refs
    total = mine_ref[0] + other_ref[0].astype(F32)
    if came:
        total = total + came[0][...].astype(F32)
    out_ref[...] = total.astype(BF)


def down_add(mine, other, block, *came):
    shape = mine.shape[1:]
    one = pl.BlockSpec((1, 1) + shape[1:], lambda s: (block, s, 0, 0))
    here = pl.BlockSpec((1,) + shape[1:], lambda s: (s, 0, 0))
    return pl.pallas_call(
        down_kernel,
        grid=(shape[0],),
        in_specs=[one, one] + [here] * len(came),
        out_specs=here,
        out_shape=jax.ShapeDtypeStruct(shape, BF),
        cost_estimate=pl.CostEstimate(flops=LATER, bytes_accessed=0, transcendentals=0),
        name="down_add",
    )(mine, other, *came)


def last_kernel(mine_ref, other_ref, came_ref, middle_ref, hidden_ref, gain_ref, out_ref):
    grad = (mine_ref[0, 0] + other_ref[0, 0].astype(F32) + came_ref[0].astype(F32)) * gain_ref[...]
    values = hidden_ref[0].astype(F32)
    inverse = lax.rsqrt(jnp.mean(values * values, axis=1, keepdims=True) + EPS)
    normal = values * inverse
    back = inverse * (grad - normal * jnp.mean(grad * normal, axis=1, keepdims=True))
    out_ref[0] = (middle_ref[0] + back).astype(BF)


def last_step(mine, other, came, d_middle, hidden, gain):
    slots, rows, width = hidden.shape
    block = pl.BlockSpec((1, 1, rows, width), lambda s: (0, s, 0, 0))
    here = pl.BlockSpec((1, rows, width), lambda s: (s, 0, 0))
    return pl.pallas_call(
        last_kernel,
        grid=(slots,),
        in_specs=[block, block, here, here, here, pl.BlockSpec((1, width), lambda s: (0, 0))],
        out_specs=here,
        out_shape=jax.ShapeDtypeStruct((slots, rows, width), BF),
        cost_estimate=pl.CostEstimate(flops=2 << 30, bytes_accessed=0, transcendentals=0),
        name="last_step",
    )(mine, other, came, d_middle, hidden, gain)


def half_kernel(half, sends, keeps, extra, keep_ref, came_ref, *refs):
    own_ref = refs[0] if extra else None
    send_ref, left_ref = refs[-2:]
    for ranks, ref in ((sends, send_ref), (keeps, left_ref)):
        for place, i in enumerate(ranks):
            rows = slice(i * half, (i + 1) * half)
            total = keep_ref[rows].astype(F32) + came_ref[rows].astype(F32)
            ref[place * half : (place + 1) * half] = total.astype(BF)
    if extra:
        ours, theirs = own_ref[...].astype(F32), came_ref[-16:].astype(F32)
        send_ref[len(sends) * half :] = in_parts((ours[:2] + ours[2:4]) + (theirs[:2] + theirs[2:4]))


def half_sum(keep, came, own, half, sends, keeps):
    cols = keep.shape[1]
    riding = 0 if own is None else 16
    return pl.pallas_call(
        functools.partial(half_kernel, half, sends, keeps, own is not None),
        out_shape=[
            jax.ShapeDtypeStruct((len(sends) * half + riding, cols), BF),
            jax.ShapeDtypeStruct((len(keeps) * half, cols), BF),
        ],
        compiler_params=pltpu.CompilerParams(vmem_limit_bytes=VMEM_LIMIT),
        cost_estimate=pl.CostEstimate(flops=LATE, bytes_accessed=0, transcendentals=0),
        name="half_sum",
    )(keep, came, *(() if own is None else (own,)))


def ctx_kernel(parts, at_ref, top_ref, top_came, low_ref, low_came, own_ref, mine_ref, small_ref, *refs):
    *sends, sum_ref = refs
    half = top_ref.shape[0]
    shard = mine_ref.shape[0]
    sum_ref[:half] = top_ref[...].astype(F32) + top_came[:half].astype(F32)
    sum_ref[half:] = low_ref[...].astype(F32) + low_came[...].astype(F32)
    ours, theirs = own_ref[...].astype(F32), top_came[half:].astype(F32)
    small = in_parts((ours[:2] + ours[2:4]) + (theirs[:2] + theirs[2:4]))
    small_ref[...] = small

    def rows(k):
        return sum_ref[pl.ds(pl.multiple_of(((at_ref[1] + k) % parts) * shard, 8), shard)]

    mine_ref[...] = rows(0)
    for k, ref in enumerate(sends, 1):
        ref[:shard] = rows(k).astype(BF)
        ref[shard:] = small


def to_ctx(at, top, top_came, low, low_came, own, parts):
    half, cols = top.shape
    shard = 2 * half // parts
    vmem = pl.BlockSpec(memory_space=pltpu.VMEM)
    message = jax.ShapeDtypeStruct((shard + 16, cols), BF)
    return pl.pallas_call(
        functools.partial(ctx_kernel, parts),
        in_specs=[pl.BlockSpec(memory_space=pltpu.SMEM)] + [vmem] * 5,
        out_shape=[jax.ShapeDtypeStruct((shard, cols), F32), jax.ShapeDtypeStruct((16, cols), BF)] + [message] * (parts - 1),
        scratch_shapes=[pltpu.VMEM((2 * half, cols), F32)],
        compiler_params=pltpu.CompilerParams(vmem_limit_bytes=VMEM_LIMIT),
        cost_estimate=pl.CostEstimate(flops=LATE, bytes_accessed=0, transcendentals=0),
        name="to_ctx",
    )(at, top, top_came, low, low_came, own)


def ffn_block(x, g, w_ref, inner_ref):
    units = w_ref.shape[1] // 3
    raised = dot(x, w_ref[:, : 2 * units], NN)
    gate = raised[:, :units]
    upper = raised[:, units:]
    sig = 1.0 / (1.0 + jnp.exp(-gate))
    silu = gate * sig
    act = (silu * upper).astype(BF)
    y = dot(act, w_ref[:, 2 * units :], NT).astype(BF)
    d_act = dot(g, w_ref[:, 2 * units :], NN)
    inner_ref[:, :units] = (d_act * upper * (sig + silu * (1.0 - sig))).astype(BF)
    inner_ref[:, units : 2 * units] = (d_act * silu).astype(BF)
    inner_ref[:, 2 * units :] = act
    d_x = dot(inner_ref[:, : 2 * units], w_ref[:, : 2 * units], NT)
    return y, d_x.astype(BF), jnp.sum(d_x * x.astype(F32), axis=0, keepdims=True)


def ffn_kernel(xm_ref, xo_ref, gm_ref, go_ref, w_ref, ym_ref, yo_ref, dm_ref, do_ref, inner_ref, gain_ref):
    half = xm_ref.shape[0]
    x = jnp.concatenate([xm_ref[...], xo_ref[...]])
    g = jnp.concatenate([gm_ref[...], go_ref[...]])
    y, d_x, gain_row = ffn_block(x, g, w_ref, inner_ref)
    ym_ref[...] = y[:half]
    yo_ref[...] = y[half:]
    dm_ref[...] = d_x[:half]
    do_ref[...] = d_x[half:]

    @pl.when(pl.program_id(0) == 0)
    def _():
        gain_ref[...] = gain_row

    @pl.when(pl.program_id(0) > 0)
    def _():
        gain_ref[...] += gain_row


def ffn_rest_kernel(
    xm_ref, xo_ref, gm_ref, go_ref, w_ref, first_ref, second_ref,
    ym_ref, yo_ref, dm_ref, do_ref, gain_ref, grad_ref, own_ref, inner_ref, sum_ref
):
    units = w_ref.shape[1] // 3
    half = ym_ref.shape[0]
    step = pl.program_id(0)

    def put(ref, place):
        inner_ref[place * half : (place + 1) * half] = ref[:half]
        inner_ref[(place + 2) * half : (place + 3) * half] = ref[half:]

    @pl.when(step == 0)
    def _():
        x = jnp.concatenate([xm_ref[:half], xo_ref[:half]])
        g = jnp.concatenate([gm_ref[:half], go_ref[:half]])
        y, d_x, gain_row = ffn_block(x, g, w_ref, own_ref)
        ym_ref[...] = y[:half]
        yo_ref[...] = y[half:]
        dm_ref[...] = d_x[:half]
        do_ref[...] = d_x[half:]
        gain_ref[...] = gain_row
        put(own_ref, 0)

    @pl.when(step > 0)
    def _():
        put(first_ref, 0)

    put(second_ref, 1)
    left = dot(jnp.concatenate([xm_ref[...], xo_ref[...]]), inner_ref[:, : 2 * units], TN)
    right = dot(jnp.concatenate([gm_ref[...], go_ref[...]]), inner_ref[:, 2 * units :], TN)

    @pl.when(step == 0)
    def _():
        sum_ref[:, : 2 * units] = left
        sum_ref[:, 2 * units :] = right

    @pl.when((step > 0) & (step < pl.num_programs(0) - 1))
    def _():
        sum_ref[:, : 2 * units] += left
        sum_ref[:, 2 * units :] += right

    @pl.when(step == pl.num_programs(0) - 1)
    def _():
        grad_ref[:, : 2 * units] = (sum_ref[:, : 2 * units] + left).astype(BF)
        grad_ref[:, 2 * units :] = (sum_ref[:, 2 * units :] + right).astype(BF)


def feed_forward(x_mine, x_other, g_mine, g_other, w, parts):
    tokens, width = x_mine.shape
    rows = tokens // parts
    units3 = w.shape[1]
    block = pl.BlockSpec((rows, width), lambda i: (i + 1, 0))
    out = pl.BlockSpec((rows, width), lambda i: (i, 0))
    part = jax.ShapeDtypeStruct((tokens - rows, width), BF)
    return pl.pallas_call(
        ffn_kernel,
        grid=(parts - 1,),
        in_specs=[block] * 4 + [pl.BlockSpec((width, units3), lambda i: (0, 0))],
        out_specs=[out] * 4 + [pl.BlockSpec((2 * rows, units3), lambda i: (i, 0)), pl.BlockSpec((1, width), lambda i: (0, 0))],
        out_shape=[part] * 4
        + [jax.ShapeDtypeStruct((2 * (tokens - rows), units3), BF), jax.ShapeDtypeStruct((1, width), F32)],
        compiler_params=pltpu.CompilerParams(vmem_limit_bytes=VMEM_LIMIT),
        cost_estimate=pl.CostEstimate(flops=8 * tokens * width * units3, bytes_accessed=24 << 20, transcendentals=0),
        name="feed_forward",
    )(x_mine, x_other, g_mine, g_other, w)


def ffn_rest(x_mine, x_other, g_mine, g_other, w, inside, parts):
    tokens, width = x_mine.shape
    rows = tokens // parts
    units3 = w.shape[1]
    block = pl.BlockSpec((2 * rows, width), lambda i: (i, 0))
    whole = pl.BlockSpec((width, units3), lambda i: (0, 0))
    first = pl.BlockSpec((2 * rows, units3), lambda i: (jnp.maximum(2 * i - 1, 0), 0))
    second = pl.BlockSpec((2 * rows, units3), lambda i: (2 * i, 0))
    own = pl.BlockSpec((rows, width), lambda i: (0, 0))
    part = jax.ShapeDtypeStruct((rows, width), BF)
    return pl.pallas_call(
        ffn_rest_kernel,
        grid=(parts // 2,),
        in_specs=[block] * 4 + [whole, first, second],
        out_specs=[own] * 4 + [pl.BlockSpec((1, width), lambda i: (0, 0)), whole],
        out_shape=[part] * 4
        + [jax.ShapeDtypeStruct((1, width), F32), jax.ShapeDtypeStruct((width, units3), BF)],
        scratch_shapes=[
            pltpu.VMEM((2 * rows, units3), BF), pltpu.VMEM((4 * rows, units3), BF), pltpu.VMEM((width, units3), F32)
        ],
        compiler_params=pltpu.CompilerParams(vmem_limit_bytes=VMEM_LIMIT),
        cost_estimate=pl.CostEstimate(flops=24 << 30, bytes_accessed=24 << 20, transcendentals=0),
        name="ffn_rest",
    )(x_mine, x_other, g_mine, g_other, w, inside, inside)


def same_kernel(in_ref, out_ref):
    pass


def same(value, flops):
    return pl.pallas_call(
        same_kernel,
        in_specs=[pl.BlockSpec(memory_space=pl.ANY)],
        out_specs=pl.BlockSpec(memory_space=pl.ANY),
        out_shape=jax.ShapeDtypeStruct(value.shape, value.dtype),
        input_output_aliases={0: 0},
        cost_estimate=pl.CostEstimate(flops=flops, bytes_accessed=0, transcendentals=0),
        name="same",
    )(value)


def pack_kernel(gate_ref, up_ref, down_ref, out_ref):
    parts, shard, units3 = out_ref.shape
    units = units3 // 3
    have = gate_ref.shape[1]
    for t in range(parts):
        for j, ref in enumerate((gate_ref, up_ref, down_ref)):
            first = min(t * units, have)
            count = min((t + 1) * units, have) - first
            if count:
                out_ref[t, :, j * units : j * units + count] = ref[:, first : first + count]
            if count < units:
                out_ref[t, :, j * units + count : (j + 1) * units] = jnp.zeros((shard, units - count), BF)


def pack(gate, up, down, parts, units):
    shard = gate.shape[0]
    return pl.pallas_call(
        pack_kernel,
        out_shape=jax.ShapeDtypeStruct((parts, shard, 3 * units), BF),
        compiler_params=pltpu.CompilerParams(vmem_limit_bytes=VMEM_LIMIT),
        name="pack",
    )(gate, up, down)


def finish_kernel(parts_ref, gate_ref, up_ref, down_ref):
    parts, shard, units3 = parts_ref.shape
    units = units3 // 3
    have = gate_ref.shape[1]
    for t in range(parts):
        for j, ref in enumerate((gate_ref, up_ref, down_ref)):
            first = min(t * units, have)
            count = min((t + 1) * units, have) - first
            if count:
                ref[:, first : first + count] = parts_ref[t, :, j * units : j * units + count].astype(F32)


def finish(parts, columns):
    whole = jax.ShapeDtypeStruct((parts.shape[1], columns), F32)
    return pl.pallas_call(
        finish_kernel,
        out_shape=[whole, whole, whole],
        compiler_params=pltpu.CompilerParams(vmem_limit_bytes=VMEM_LIMIT),
        name="finish",
    )(parts)


def inverse_rms(values):
    return lax.rsqrt(jnp.mean(values * values, axis=-1, keepdims=True) + EPS)


def norm_back(values, gain, grad):
    inverse = inverse_rms(values)
    normal = values * inverse
    scaled = grad * gain
    return inverse * (scaled - normal * jnp.mean(scaled * normal, axis=-1, keepdims=True))


def body(
    hidden_in,
    seq_lengths,
    attn_gain,
    query_gain,
    key_gain,
    query_weight,
    key_projection,
    value_projection,
    out_weight,
    ffn_gain,
    gate_weight,
    up_weight,
    down_weight,
    cotangent,
):
    slots, shard_rows, width = hidden_in.shape
    n_fsdp = lax.axis_size("fsdp")
    n_ctx = lax.axis_size("ctx")
    f = lax.axis_index("fsdp")
    c = lax.axis_index("ctx")
    core = lax.axis_index("tp")
    rows = 2 * shard_rows
    keys = n_ctx * rows
    q_cols = query_weight.shape[1]
    k_cols = key_projection.shape[1]
    shard = query_weight.shape[0]
    ff_half = gate_weight.shape[1]
    units = ff_half // n_fsdp
    padded = -(-units // TILE) * TILE

    at = jnp.arange(keys)
    places = (c - at // rows) * rows + ((at // shard_rows) % 2 ^ core) * shard_rows + at % shard_rows
    lanes = jnp.arange(TILE)
    freqs = THETA ** (-((lanes % (HEAD // 2)).astype(F32) * 2.0 / HEAD))
    angles = places.astype(F32)[:, None] * freqs[None, :]
    cosine = jnp.cos(angles)
    sine = jnp.sin(angles) * jnp.where(lanes % HEAD < HEAD // 2, -1.0, 1.0)[None, :]
    scal = jnp.concatenate([jnp.stack([c, core, f]).astype(jnp.int32), seq_lengths])
    own_places = places[:shard_rows]
    valid = own_places[None, :, None] < seq_lengths[:, None, None]

    hidden = hidden_in.astype(F32)
    inverse_one = inverse_rms(hidden)
    normed = (hidden * inverse_one * attn_gain).astype(BF)

    def ctx_stack(pieces):
        stack = jnp.zeros((n_ctx,) + pieces[0].shape, pieces[0].dtype)
        for k, piece in enumerate(pieces):
            stack = lax.dynamic_update_index_in_dim(stack, piece, (c - k) % n_ctx, 0)
        return stack

    def fsdp_stack(pieces):
        stack = jnp.zeros((n_fsdp,) + pieces[0].shape, pieces[0].dtype)
        for m, piece in enumerate(pieces):
            stack = lax.dynamic_update_index_in_dim(stack, piece, f ^ m, 0)
        return stack

    def spread_halves(value):
        masks = [1 << i for i in range(8) if 1 << i < n_fsdp]
        halves = []
        for half, order in zip(jnp.split(value, 2), (masks, masks[::-1])):
            half = half[None]
            for mask in order:
                half = jnp.concatenate([half, fsdp_xor(half, mask)])
            halves.append(half)
        return halves

    def in_order(half, order):
        got = jnp.zeros_like(half)
        for i in range(n_fsdp):
            mask = sum(bit for j, bit in enumerate(order) if i >> j & 1)
            got = lax.dynamic_update_index_in_dim(got, half[i], f ^ mask, 0)
        return got

    def over_ctx(value):
        return [value] + [ctx_shift(value, k) for k in range(1, n_ctx)]

    def over_fsdp(value):
        return [value] + [fsdp_xor(value, m) for m in range(1, n_fsdp)]

    def part(array, index):
        return lax.dynamic_index_in_dim(array, index, 0, keepdims=False)

    def trade_parts(parts):
        return [part(parts, f)] + [fsdp_xor(part(parts, f ^ m), m) for m in range(1, n_fsdp)]

    ffn_packed = pack(gate_weight, up_weight, down_weight.T, n_fsdp, padded)
    packed = jnp.concatenate([query_weight, key_projection, value_projection, out_weight.T], axis=1)
    grad_rows = jnp.where(valid, cotangent, jnp.zeros_like(cotangent))
    x_pieces = [normed, ctx_up(normed)]
    ffn_rows = lax.all_to_all(ffn_packed, "fsdp", 0, 0, tiled=True)
    held = tie(*x_pieces, *over_ctx(packed))
    x_pieces = list(held[:2])
    stack = ctx_stack(held[2:]).reshape(n_ctx * shard, -1)

    top, bottom = spread_halves(stack)
    others = [swap_cores(piece) for piece in x_pieces]
    while len(x_pieces) < n_ctx:
        x_pieces.append(ctx_up(x_pieces[-1]))
        if len(x_pieces) == 3:
            ffn_rows, x_pieces[-1] = tie(ffn_rows, x_pieces[-1])
        others.append(swap_cores(x_pieces[-1]))
    ffn_w = lax.all_gather(ffn_rows, "ctx", axis=1, tiled=True).reshape(width, 3 * padded)
    ffn_w = same(ffn_w, 60 << 30)
    held = tie(*x_pieces, *others, grad_rows, top, bottom)
    x_pieces = held[:n_ctx]
    others = held[n_ctx : 2 * n_ctx]
    grad_rows, top, bottom = held[2 * n_ctx :]

    query_gain2 = jnp.tile(query_gain, 2)[None, :]
    key_gain2 = jnp.tile(key_gain, 2)[None, :]
    attn, stats, q_raw, k_raw, value, q_hat, k_hat, x_all = attend(
        scal, [piece for pair in zip(x_pieces, others) for piece in pair], (top, bottom), (q_cols, k_cols), cosine, sine,
        query_gain2, key_gain2,
    )
    held = tie(attn, *over_fsdp(grad_rows))
    attn = held[0]
    g_mine = jnp.stack(held[1:])
    g_other = swap_cores(g_mine)
    bits = [mask for mask in (1 << i for i in range(8)) if mask < n_fsdp]
    attn_w = jnp.stack([in_order(top, bits), in_order(bottom, bits[::-1])], axis=1).reshape(width, -1)
    out_w = attn_w[:, q_cols + 2 * k_cols :]

    branch = jnp.einsum("sth,dh->std", attn, out_w, preferred_element_type=F32)
    middle = hidden + (branch[:, :shard_rows] + swap_cores(branch[:, shard_rows:]))
    normed_two = (middle * inverse_rms(middle) * ffn_gain).astype(BF)
    x_mine = jnp.stack(over_fsdp(normed_two))
    x_other = swap_cores(x_mine)

    def flat(value):
        return value.reshape(-1, width)

    place = jnp.stack([f]).astype(jnp.int32)

    tokens = (flat(x_mine), flat(x_other), flat(g_mine), flat(g_other))
    y_mine, y_other, dx_mine, dx_other, inside, gain_row = feed_forward(*tokens, ffn_w, n_fsdp)

    def core_sums(mine, other):
        mine = mine.reshape(n_fsdp - 1, slots, shard_rows, width)
        other = swap_cores(other.reshape(n_fsdp - 1, slots, shard_rows, width))
        return [(mine[m].astype(F32) + other[m].astype(F32)).astype(BF) for m in range(n_fsdp - 1)]

    def traded(sums):
        return [fsdp_xor(item, m) for m, item in enumerate(sums, 1)]

    def own(value):
        return value.reshape(slots, shard_rows, width)

    inside, *dx_sums = tie(inside, *core_sums(dx_mine, dx_other))
    inside, *y_sums = tie(inside, *core_sums(y_mine, y_other))
    y_mine, y_other, dx_mine, dx_other, own_gain_row, ffn_grads = ffn_rest(*tokens, ffn_w, inside, n_fsdp)
    ffn_gain_row = (gain_row + own_gain_row)[0]
    ffn_grads, dx_mine, dx_other, *held = tie(ffn_grads, dx_mine, dx_other, *traded(dx_sums))
    ffn_reduced = lax.psum_scatter(
        ffn_grads.reshape(n_fsdp, n_ctx * shard, 3 * padded), "ctx", scatter_dimension=1, tiled=True
    )
    d_normed_two = own(dx_mine).astype(F32) + swap_cores(own(dx_other)).astype(F32)
    d_normed_two = d_normed_two + sum(item.astype(F32) for item in held)
    d_middle = grad_rows.astype(F32) + norm_back(middle, ffn_gain, d_normed_two)
    d_mine = d_middle.astype(BF)
    d_other = swap_cores(d_mine)
    d_branch = jnp.concatenate([d_mine, d_other], axis=1)
    d_attn = jnp.einsum("std,dh->sth", d_branch, out_w, preferred_element_type=F32).astype(BF)
    held = tie(d_attn, *y_sums)
    d_attn = held[0]
    y_sums = held[1:]

    d_q, d_k, d_v, gq, gk = attend_back(
        scal, q_raw, k_raw, value, cosine, sine, query_gain2, key_gain2, q_hat, k_hat, attn, stats, d_attn
    )
    y_got = [own(y_mine), swap_cores(own(y_other))] + traded(y_sums)

    held = tie(d_q, d_k, d_v, gq, gk, ffn_gain_row, *y_got)
    d_q, d_k, d_v, gq, gk, ffn_gain_row = held[:6]
    result = jnp.where(valid, middle + sum(item.astype(F32) for item in held[6:]), 0.0).astype(BF)

    heads = jnp.concatenate([gq, gk])
    small = jnp.stack([jnp.zeros_like(ffn_gain), ffn_gain_row / ffn_gain])
    small = jnp.concatenate([small, heads], axis=1)
    small = jnp.pad(small, ((0, 0), (0, 2 * q_cols + 2 * k_cols - small.shape[1])))
    top_send, top, low_send, low, own = weight_grads(
        place, x_all, d_q, d_k, d_v, d_mine, d_other, attn, attn_w, attn_gain[None, :], two_parts(small), n_fsdp
    )
    top_send, top, low_send, low, own, d_q, d_k, d_v = tie(top_send, top, low_send, low, own, d_q, d_k, d_v)

    half = n_ctx * shard // 2
    bits = bits_of(n_fsdp)
    came = [fsdp_xor(top_send, bits[0]), fsdp_xor(low_send, bits[-1])]
    last_mine, last_other = input_grads(d_q, d_k, d_v, attn_w, n_ctx - 1, 1)
    last_other = swap_cores(last_other)
    mine, other = input_grads(d_q, d_k, d_v, attn_w, 0, n_ctx - 1)
    mine, other, last_other, result, *came = tie(mine, other, last_other, result, *came)
    other = swap_cores(other)
    total = ctx_round(down_add(last_mine, last_other, 0))
    block = n_ctx - 2
    for step in range(1, len(bits)):
        count = n_fsdp >> step
        sent = []
        kept = []
        for side, keep in enumerate((top, low)):
            order = bits if side == 0 else bits[::-1]
            masks = sorted(sum(bit for j, bit in enumerate(order[step:]) if i >> j & 1) for i in range(count))
            sends = [i for i, mask in enumerate(masks) if mask & order[step]]
            keeps = [i for i, mask in enumerate(masks) if not mask & order[step]]
            send, keep = half_sum(keep, came[side], own if side == 0 else None, half, sends, keeps)
            sent.append(send)
            kept.append(keep)
        if step == 1:
            total, other, mine, ffn_reduced, *held = tie(total, other, mine, ffn_reduced, *sent, *kept)
            sent, kept = held[:2], held[2:]
        top, low = kept
        own = sent[0][count // 2 * half :]
        came = [fsdp_xor(sent[0], bits[step]), fsdp_xor(sent[1], bits[-1 - step])]
        if block > 0:
            total = ctx_round(down_add(mine, other, block, total))
            block -= 1
            total, ffn_reduced, *came = tie(total, ffn_reduced, *came)
    ctx_place = jnp.stack([f, c]).astype(jnp.int32)
    mine_rows, small, *messages = to_ctx(ctx_place, top, came[0], low, came[1], own, n_ctx)
    while block > 0:
        total = ctx_down(down_add(mine, other, block, total))
        block -= 1
    got = [ctx_shift(message, k) for k, message in enumerate(messages, 1)]
    ffn_parts = lax.all_to_all(ffn_reduced, "fsdp", 0, 0, tiled=True)
    gate_grad, up_grad, down_grad = finish(ffn_parts, ff_half)
    total, gate_grad, up_grad, down_grad = tie(total, gate_grad, up_grad, down_grad)
    small = [one_part(small)] + [one_part(piece[shard:]) for piece in got]
    got = [mine_rows] + [piece[:shard].astype(F32) for piece in got]
    down_grad = down_grad.T
    attn_grads = sum(got)
    small = tree_sum(small)
    small = small + swap_cores(small)
    input_grad = last_step(mine, other, total, d_middle, hidden_in, attn_gain[None, :])
    qkv_total = attn_grads[:, : q_cols + 2 * k_cols]
    query_weight_grad = qkv_total[:, :q_cols]
    key_weight_grad = qkv_total[:, q_cols : q_cols + k_cols]
    value_weight_grad = qkv_total[:, q_cols + k_cols :]
    out_weight_grad = attn_grads[:, q_cols + 2 * k_cols :].T

    return (
        result,
        input_grad,
        small[0, :width],
        small[0, width : width + HEAD],
        small[1, width : width + HEAD],
        query_weight_grad,
        key_weight_grad,
        value_weight_grad,
        out_weight_grad,
        small[1, :width],
        gate_grad,
        up_grad,
        down_grad,
    )


def solution(mesh):
    in_specs = (
        P("fsdp", ("ctx", "tp"), None),
        P("fsdp"),
        P(),
        P(),
        P(),
        P(("fsdp", "ctx"), "tp"),
        P(("fsdp", "ctx"), "tp"),
        P(("fsdp", "ctx"), "tp"),
        P("tp", ("fsdp", "ctx")),
        P(),
        P(("fsdp", "ctx"), "tp"),
        P(("fsdp", "ctx"), "tp"),
        P("tp", ("fsdp", "ctx")),
        P("fsdp", ("ctx", "tp"), None),
    )
    out_specs = (
        P("fsdp", ("ctx", "tp"), None),
        P("fsdp", ("ctx", "tp"), None),
        P(),
        P(),
        P(),
        P(("fsdp", "ctx"), "tp"),
        P(("fsdp", "ctx"), "tp"),
        P(("fsdp", "ctx"), "tp"),
        P("tp", ("fsdp", "ctx")),
        P(),
        P(("fsdp", "ctx"), "tp"),
        P(("fsdp", "ctx"), "tp"),
        P("tp", ("fsdp", "ctx")),
    )
    return jax.shard_map(body, mesh=mesh, in_specs=in_specs, out_specs=out_specs, check_vma=False)
```

```python
import functools

import jax
import jax.numpy as jnp
import numpy as np
from jax import lax
from jax.experimental import pallas as pl
from jax.experimental.pallas import tpu as pltpu
from jax.sharding import PartitionSpec as P

HEAD = 64
TILE = 128
EPS = 1e-05
THETA = 1000000.0
SCALE = HEAD**-0.5
EXP2_SCALE = SCALE * float(np.log2(np.e))
FAR = -1e30
BF = jnp.bfloat16
F32 = jnp.float32
VMEM_LIMIT = 56 * 1024 * 1024
LATE = 12 << 30
LATER = 5 << 30


def dot(left, right, dims):
    return lax.dot_general(left, right, (dims, ((), ())), preferred_element_type=F32)


NN = ((1,), (0,))
NT = ((1,), (1,))
TN = ((0,), (0,))


def swap_cores(value):
    return lax.ppermute(value, "tp", [(0, 1), (1, 0)])


def fsdp_xor(value, mask):
    size = lax.axis_size("fsdp")
    return lax.ppermute(value, "fsdp", [(i, i ^ mask) for i in range(size)])


def ctx_up(value, step=1):
    size = lax.axis_size("ctx")
    return lax.ppermute(value, "ctx", [(i, i + step) for i in range(size - step)])


def ctx_down(value, step=1):
    size = lax.axis_size("ctx")
    return lax.ppermute(value, "ctx", [(i + step, i) for i in range(size - step)])


def ctx_round(value):
    return ctx_shift(value, lax.axis_size("ctx") - 1)


def ctx_shift(value, step):
    size = lax.axis_size("ctx")
    return lax.ppermute(value, "ctx", [(i, (i + step) % size) for i in range(size)])


def tree_sum(values):
    while len(values) > 1:
        half = len(values) // 2
        values = [values[i] + values[i + half] for i in range(half)]
    return values[0]


def two_parts(rows):
    first = rows.astype(BF)
    left = (rows - first.astype(F32)).astype(BF)
    return jnp.pad(jnp.concatenate([first, left]), ((0, 16 - 2 * rows.shape[0]), (0, 0)))


def one_part(rows):
    return rows[:2].astype(F32) + rows[2:4].astype(F32)


def tie(*values):
    return lax.optimization_barrier(values)


def lane_ids(rows):
    return lax.broadcasted_iota(jnp.int32, (rows, TILE), 1)


def half_swap(x):
    low = lane_ids(x.shape[0]) % HEAD < HEAD // 2
    return jnp.where(low, pltpu.roll(x, TILE - HEAD // 2, 1), pltpu.roll(x, HEAD // 2, 1))


def head_mean(x):
    first = lane_ids(x.shape[0]) < HEAD
    left = jnp.sum(jnp.where(first, x, 0.0), axis=1, keepdims=True)
    right = jnp.sum(jnp.where(first, 0.0, x), axis=1, keepdims=True)
    return jnp.where(first, left, right) * (1.0 / HEAD)


def prepare(x, gain, cosine, sine):
    scaled = x * lax.rsqrt(head_mean(x * x) + EPS) * gain
    return scaled * cosine + half_swap(scaled) * sine


def prepare_back(x, gain, cosine, sine, grad):
    grad = grad * cosine - half_swap(grad) * sine
    inverse = lax.rsqrt(head_mean(x * x) + EPS)
    normal = x * inverse
    gain_grad = jnp.sum(grad * normal, axis=0, keepdims=True)
    grad = grad * gain
    return inverse * (grad - normal * head_mean(grad * normal)), gain_grad


def key_bias(scal_ref, slot, keys, block_rows):
    c = scal_ref[0]
    core = scal_ref[1]
    length = scal_ref[3 + slot]
    half = block_rows // 2

    def places(index):
        block = index // block_rows
        side = (index // half) % 2
        return (c - block) * block_rows + (side + core - 2 * side * core) * half + index % half

    key_at = places(lax.broadcasted_iota(jnp.int32, (keys, block_rows), 0))
    query_at = places(lax.broadcasted_iota(jnp.int32, (keys, block_rows), 1))
    seen = (key_at >= 0) & (key_at <= query_at) & (key_at < length)
    return jnp.where(seen, 0.0, FAR)


def twins(x):
    first = lane_ids(x.shape[0]) < HEAD
    turned = pltpu.roll(x, HEAD, 1)
    return jnp.where(first, x, turned).astype(BF), jnp.where(first, turned, x).astype(BF)


def by_head(x):
    first = lane_ids(x.shape[0]) < HEAD
    none = jnp.zeros_like(x)
    return jnp.concatenate([jnp.where(first, x, none), jnp.where(first, none, x)])


def attend_kernel(n_pieces, n_parts, scal_ref, *refs):
    pieces = refs[:n_pieces]
    (
        tq_ref, tk_ref, tv_ref, bq_ref, bk_ref, bv_ref, cos_ref, sin_ref, qg_ref, kg_ref,
        o_ref, l_ref, qr_ref, kr_ref, v_ref, qh_ref, kh_ref, x_ref, bias_ref, wq_ref, wkv_ref,
    ) = refs[n_pieces:]
    rows = qr_ref.shape[1]
    keys = kr_ref.shape[1]
    half = rows // 2

    @pl.when(pl.program_id(1) == 0)
    def _():
        bias_ref[...] = key_bias(scal_ref, pl.program_id(0), keys, rows)
        for i, piece in enumerate(pieces):
            x_ref[0, i * half : (i + 1) * half] = piece[0]

    depth = tq_ref.shape[1]
    bits = [1 << i for i in range(8) if 1 << i < n_parts]
    for side, (query_w, key_w, value_w) in enumerate(((tq_ref, tk_ref, tv_ref), (bq_ref, bk_ref, bv_ref))):
        order = bits[::-1] if side else bits
        for i in range(n_parts):
            mask = sum(bit for j, bit in enumerate(order) if i >> j & 1)
            at = pl.ds(pl.multiple_of(((scal_ref[2] ^ mask) * 2 + side) * depth, depth), depth)
            wq_ref[at, :] = query_w[i]
            wkv_ref[at, :TILE] = key_w[i]
            wkv_ref[at, TILE:] = value_w[i]
    key_value = dot(x_ref[0], wkv_ref[...], NN)
    query_raw = dot(x_ref[0, :rows], wq_ref[...], NN)
    kr_ref[0] = key_value[:, :TILE]
    v_ref[0] = key_value[:, TILE:].astype(BF)
    qr_ref[0] = query_raw

    key = prepare(kr_ref[0], kg_ref[...], cos_ref[...], sin_ref[...]).astype(BF)
    kh_ref[0] = key
    key_twins = twins(key.astype(F32))
    value_twins = twins(v_ref[0].astype(F32))
    first = lane_ids(rows) < HEAD
    for pair in range(2):
        lanes = slice(pair * TILE, (pair + 1) * TILE)
        query = prepare(qr_ref[0, :, lanes], qg_ref[...], cos_ref[:rows], sin_ref[:rows]).astype(BF)
        qh_ref[0, :, lanes] = query
        scores = dot(key_twins[pair], by_head(query), NT)
        weights = jnp.exp2(scores * EXP2_SCALE + jnp.concatenate([bias_ref[...]] * 2, axis=1))
        inverse = 1.0 / jnp.sum(weights, axis=0, keepdims=True)
        l_ref[0, 0, pl.ds(2 * pair, 1), :] = inverse[:, :rows]
        l_ref[0, 0, pl.ds(2 * pair + 1, 1), :] = inverse[:, rows:]
        mixed = dot(weights.astype(BF), value_twins[pair], TN) * jnp.broadcast_to(inverse, (TILE, 2 * rows)).T
        o_ref[0, :, lanes] = jnp.where(first, mixed[:rows], mixed[rows:]).astype(BF)


def attend_back_kernel(
    scal_ref, q_ref, k_ref, v_ref, cos_ref, sin_ref, qg_ref, kg_ref, qh_ref, kh_ref, o_ref, l_ref, d_ref,
    dq_ref, dk_ref, dv_ref, gq_ref, gk_ref, bias_ref
):
    rows = q_ref.shape[1]
    keys = k_ref.shape[1]

    @pl.when(pl.program_id(1) == 0)
    def _():
        bias_ref[...] = key_bias(scal_ref, pl.program_id(0), keys, rows)

    key_twins = twins(kh_ref[0].astype(F32))
    value_twins = twins(v_ref[0].astype(F32))
    first = lane_ids(rows) < HEAD
    key_first = lane_ids(keys) < HEAD
    row_first = lax.broadcasted_iota(jnp.int32, (TILE, rows), 0) < HEAD
    key_grads = []
    value_grads = []
    query_gain = jnp.zeros((1, TILE), F32)
    for pair in range(2):
        lanes = slice(pair * TILE, (pair + 1) * TILE)
        query = qh_ref[0, :, lanes]
        grad = d_ref[0, :, lanes]
        product = (grad.astype(F32) * o_ref[0, :, lanes].astype(F32)).T
        key_grad = jnp.zeros((keys, TILE), F32)
        value_grad = jnp.zeros((keys, TILE), F32)
        query_grads = []
        for head in range(2):
            mine = first if head == 0 else jnp.logical_not(first)
            own_query = jnp.where(mine, query, jnp.zeros_like(query))
            own_grad = jnp.where(mine, grad, jnp.zeros_like(grad))
            inner = jnp.sum(product[head * HEAD : (head + 1) * HEAD], axis=0, keepdims=True)
            inverse = l_ref[0, 0, pl.ds(2 * pair + head, 1), :]
            scores = dot(key_twins[pair], own_query, NT)
            probs = jnp.exp2(scores * EXP2_SCALE + bias_ref[...]) * inverse
            grad_probs = dot(value_twins[pair], own_grad, NT)
            grad_scores = (probs * (grad_probs - inner)).astype(BF)
            query_grads.append(dot(grad_scores, key_twins[pair], TN))
            key_grad = key_grad + dot(grad_scores, own_query, NN)
            value_grad = value_grad + dot(probs.astype(BF), own_grad, NN)
        query_rot = jnp.where(first, query_grads[0], query_grads[1]) * SCALE
        raw, gain_part = prepare_back(q_ref[0, :, lanes], qg_ref[...], cos_ref[:rows], sin_ref[:rows], query_rot)
        dq_ref[0, :, lanes] = raw.astype(BF)
        query_gain = query_gain + gain_part
        key_grads.append(key_grad + pltpu.roll(key_grad, HEAD, 1))
        value_grads.append(value_grad + pltpu.roll(value_grad, HEAD, 1))
    dv_ref[0] = jnp.where(key_first, value_grads[0], value_grads[1]).astype(BF)
    key_rot = jnp.where(key_first, key_grads[0], key_grads[1]) * SCALE
    raw, key_gain = prepare_back(k_ref[0], kg_ref[...], cos_ref[...], sin_ref[...], key_rot)
    dk_ref[0] = raw.astype(BF)

    @pl.when((pl.program_id(0) == 0) & (pl.program_id(1) == 0))
    def _():
        gq_ref[...] = jnp.zeros_like(gq_ref)
        gk_ref[...] = jnp.zeros_like(gk_ref)

    gq_ref[...] += query_gain + pltpu.roll(query_gain, HEAD, 1)
    gk_ref[...] += key_gain + pltpu.roll(key_gain, HEAD, 1)


def attention_specs(slots, rows, keys):
    smem = pl.BlockSpec(memory_space=pltpu.SMEM)
    query = pl.BlockSpec((1, rows, 2 * TILE), lambda s, p: (s, 0, p))
    key = pl.BlockSpec((1, keys, TILE), lambda s, p: (s, 0, p))
    table = pl.BlockSpec((keys, TILE), lambda s, p: (0, 0))
    gain = pl.BlockSpec((1, TILE), lambda s, p: (0, 0))
    stat = pl.BlockSpec((1, 1, 8, rows), lambda s, p: (s, p, 0, 0))
    return smem, query, key, table, gain, stat


def attend(scal, pieces, weights, widths, cosine, sine, query_gain, key_gain):
    width, kv_width = widths
    slots, half, model = pieces[0].shape
    rows = 2 * half
    keys = len(pieces) * half
    smem, query, key, table, gain, stat = attention_specs(slots, rows, keys)
    pairs = kv_width // TILE
    piece = pl.BlockSpec((1, half, model), lambda s, p: (s, 0, 0))
    parts, depth = weights[0].shape[:2]
    w_query = pl.BlockSpec((parts, depth, 2 * TILE), lambda s, p: (0, 0, p))
    w_key = pl.BlockSpec((parts, depth, TILE), lambda s, p: (0, 0, width // TILE + p))
    w_value = pl.BlockSpec((parts, depth, TILE), lambda s, p: (0, 0, (width + kv_width) // TILE + p))
    return pl.pallas_call(
        functools.partial(attend_kernel, len(pieces), parts),
        grid=(slots, pairs),
        in_specs=[smem] + [piece] * len(pieces) + [w_query, w_key, w_value] * 2 + [table, table, gain, gain],
        out_specs=[
            query, stat, query, key, key, query, key, pl.BlockSpec((1, keys, model), lambda s, p: (s, 0, 0)),
        ],
        out_shape=[
            jax.ShapeDtypeStruct((slots, rows, width), BF),
            jax.ShapeDtypeStruct((slots, pairs, 8, rows), F32),
            jax.ShapeDtypeStruct((slots, rows, width), F32),
            jax.ShapeDtypeStruct((slots, keys, kv_width), F32),
            jax.ShapeDtypeStruct((slots, keys, kv_width), BF),
            jax.ShapeDtypeStruct((slots, rows, width), BF),
            jax.ShapeDtypeStruct((slots, keys, kv_width), BF),
            jax.ShapeDtypeStruct((slots, keys, model), BF),
        ],
        scratch_shapes=[
            pltpu.VMEM((keys, rows), F32),
            pltpu.VMEM((model, 2 * TILE), BF),
            pltpu.VMEM((model, 2 * TILE), BF),
        ],
        compiler_params=pltpu.CompilerParams(vmem_limit_bytes=VMEM_LIMIT),
        cost_estimate=pl.CostEstimate(flops=1 << 20, bytes_accessed=1 << 20, transcendentals=0),
        name="attend",
    )(scal, *pieces, *[item for item in weights for _ in range(3)], cosine, sine, query_gain, key_gain)


def attend_back(scal, q_raw, k_raw, value, cosine, sine, query_gain, key_gain, q_hat, k_hat, out, stats, grad):
    slots, rows, width = q_raw.shape
    keys, kv_width = k_raw.shape[1:]
    smem, query, key, table, gain, stat = attention_specs(slots, rows, keys)
    pairs = kv_width // TILE
    return pl.pallas_call(
        attend_back_kernel,
        grid=(slots, pairs),
        in_specs=[smem, query, key, key, table, table, gain, gain, query, key, query, stat, query],
        out_specs=[query, key, key, gain, gain],
        out_shape=[
            jax.ShapeDtypeStruct((slots, rows, width), BF),
            jax.ShapeDtypeStruct((slots, keys, kv_width), BF),
            jax.ShapeDtypeStruct((slots, keys, kv_width), BF),
            jax.ShapeDtypeStruct((1, TILE), F32),
            jax.ShapeDtypeStruct((1, TILE), F32),
        ],
        scratch_shapes=[pltpu.VMEM((keys, rows), F32)],
        compiler_params=pltpu.CompilerParams(vmem_limit_bytes=VMEM_LIMIT),
        cost_estimate=pl.CostEstimate(
            flops=24 << 30, bytes_accessed=12 << 20, transcendentals=0
        ),
        name="attend_back",
    )(scal, q_raw, k_raw, value, cosine, sine, query_gain, key_gain, q_hat, k_hat, out, stats, grad)


def bits_of(size):
    return [1 << i for i in range(8) if 1 << i < size]


def weight_kernel(parts, at_ref, x_ref, dq_ref, dk_ref, dv_ref, bm_ref, bo_ref, o_ref, w_ref, gain_ref, more_ref, *refs):
    top_send, top_keep, low_send, low_keep, own_ref, sum_ref = refs
    slots, rows, q_cols = dq_ref.shape
    k_cols = dk_ref.shape[2]
    depth = x_ref.shape[2]
    half = depth // 2
    m = pl.program_id(0)
    query = jnp.zeros((depth, q_cols), F32)
    key = jnp.zeros((depth, k_cols), F32)
    value = jnp.zeros((depth, k_cols), F32)
    out = jnp.zeros((depth, q_cols), F32)
    for s in range(slots):
        x = x_ref[s]
        query = query + dot(x[:rows], dq_ref[s], TN)
        key = key + dot(x, dk_ref[s], TN)
        value = value + dot(x, dv_ref[s], TN)
        out = out + dot(jnp.concatenate([bm_ref[s], bo_ref[s]]), o_ref[s], TN)
    total = jnp.concatenate([query, key, value, out], axis=1)
    product = total[:, : q_cols + 2 * k_cols] * w_ref[:, : q_cols + 2 * k_cols].astype(F32)
    column = jnp.sum(product, axis=1, keepdims=True)
    place = pl.ds(pl.multiple_of((at_ref[0] ^ m) * depth, TILE), depth)
    sum_ref[:, place] = jnp.broadcast_to(column, (depth, TILE)).T[:8]
    total = total.astype(BF)
    bits = bits_of(parts)
    for bit, rows_of, send, keep in (
        (bits[0], total[:half], top_send, top_keep),
        (bits[-1], total[half:], low_send, low_keep),
    ):
        chosen = [i for i in range(parts) if i & bit]
        for i in range(parts):
            ref = send if i & bit else keep
            rank = chosen.index(i | bit)

            @pl.when(m == i)
            def _(ref=ref, rank=rank, rows_of=rows_of):
                ref[rank * half : (rank + 1) * half] = rows_of

    @pl.when(m == parts - 1)
    def _():
        width = sum_ref.shape[1]
        row = sum_ref[:1] / gain_ref[...]
        first = row.astype(BF).astype(F32)
        left = row - first
        ids = lax.broadcasted_iota(jnp.int32, (16, width), 0)
        more = more_ref[...].astype(F32)
        here = jnp.where(ids == 0, first, jnp.where(ids == 2, left, more[:, :width]))
        for ref, rows_at in ((top_send, slice(parts // 2 * half, parts // 2 * half + 16)), (own_ref, slice(0, 16))):
            ref[rows_at, :width] = here.astype(BF)
            ref[rows_at, width:] = more_ref[:, width:]


def weight_grads(at, x, d_q, d_k, d_v, d_mine, d_other, attn, w, gain, more, parts):
    slots, keys, width = x.shape
    cols = 2 * d_q.shape[2] + 2 * d_k.shape[2]
    depth = width // parts
    rows = parts // 2 * (depth // 2)
    shapes = [(rows + more.shape[0], cols), (rows, cols), (rows, cols), (rows, cols), more.shape]
    spec = pltpu.PrefetchScalarGridSpec(
        num_scalar_prefetch=1,
        grid=(parts,),
        in_specs=[
            pl.BlockSpec((slots, keys, depth), lambda m, at: (0, 0, at[0] ^ m)),
            pl.BlockSpec(d_q.shape, lambda m, at: (0, 0, 0)),
            pl.BlockSpec(d_k.shape, lambda m, at: (0, 0, 0)),
            pl.BlockSpec(d_v.shape, lambda m, at: (0, 0, 0)),
            pl.BlockSpec(d_mine.shape[:2] + (depth,), lambda m, at: (0, 0, at[0] ^ m)),
            pl.BlockSpec(d_mine.shape[:2] + (depth,), lambda m, at: (0, 0, at[0] ^ m)),
            pl.BlockSpec(attn.shape, lambda m, at: (0, 0, 0)),
            pl.BlockSpec((depth, cols), lambda m, at: (at[0] ^ m, 0)),
            pl.BlockSpec(gain.shape, lambda m, at: (0, 0)),
            pl.BlockSpec(more.shape, lambda m, at: (0, 0)),
        ],
        out_specs=[pl.BlockSpec(shape, lambda m, at: (0, 0)) for shape in shapes],
        scratch_shapes=[pltpu.VMEM((8, width), F32)],
    )
    return pl.pallas_call(
        functools.partial(weight_kernel, parts),
        grid_spec=spec,
        out_shape=[jax.ShapeDtypeStruct(shape, BF) for shape in shapes],
        compiler_params=pltpu.CompilerParams(vmem_limit_bytes=VMEM_LIMIT),
        cost_estimate=pl.CostEstimate(flops=10 << 30, bytes_accessed=8 << 20, transcendentals=0),
        name="weight_grads",
    )(at, x, d_q, d_k, d_v, d_mine, d_other, attn, w, gain, more)


def input_kernel(with_own, dq_ref, dk_ref, dv_ref, w_ref, mine_ref, other_ref):
    slots, rows, q_cols = dq_ref.shape
    k_cols = dk_ref.shape[2]
    half = rows // 2
    for s in range(slots):
        d_x = dot(dk_ref[s], w_ref[:, q_cols : q_cols + k_cols], NT)
        d_x = d_x + dot(dv_ref[s], w_ref[:, q_cols + k_cols : q_cols + 2 * k_cols], NT)
        mine_ref[0, s] = d_x[:half]
        other_ref[0, s] = d_x[half:].astype(BF)

    @pl.when(with_own & (pl.program_id(0) == 0))
    def _():
        for s in range(slots):
            d_x = dot(dq_ref[s], w_ref[:, :q_cols], NT)
            mine_ref[0, s] += d_x[:half]
            other_ref[0, s] = (other_ref[0, s].astype(F32) + d_x[half:]).astype(BF)


def input_grads(d_q, d_k, d_v, w, first, blocks):
    slots, rows, q_cols = d_q.shape
    k_cols = d_k.shape[2]
    width = w.shape[0]
    part = pl.BlockSpec((slots, rows, k_cols), lambda r: (0, r + first, 0))
    out = pl.BlockSpec((1, slots, rows // 2, width), lambda r: (r, 0, 0, 0))
    return pl.pallas_call(
        functools.partial(input_kernel, first == 0),
        grid=(blocks,),
        in_specs=[
            pl.BlockSpec(d_q.shape, lambda r: (0, 0, 0)),
            part,
            part,
            pl.BlockSpec(w.shape, lambda r: (0, 0)),
        ],
        out_specs=[out, out],
        out_shape=[
            jax.ShapeDtypeStruct((blocks, slots, rows // 2, width), F32),
            jax.ShapeDtypeStruct((blocks, slots, rows // 2, width), BF),
        ],
        compiler_params=pltpu.CompilerParams(vmem_limit_bytes=VMEM_LIMIT),
        cost_estimate=pl.CostEstimate(flops=6 << 30, bytes_accessed=1 << 20, transcendentals=0),
        name="input_grads",
    )(d_q, d_k, d_v, w)


def in_parts(rows):
    first = rows.astype(BF).astype(F32)
    return jnp.concatenate([first, rows - first, jnp.zeros((12, rows.shape[1]), F32)]).astype(BF)


def down_kernel(*refs):
    mine_ref, other_ref, *came, out_ref = refs
    total = mine_ref[0] + other_ref[0].astype(F32)
    if came:
        total = total + came[0][...].astype(F32)
    out_ref[...] = total.astype(BF)


def down_add(mine, other, block, *came):
    shape = mine.shape[1:]
    one = pl.BlockSpec((1, 1) + shape[1:], lambda s: (block, s, 0, 0))
    here = pl.BlockSpec((1,) + shape[1:], lambda s: (s, 0, 0))
    return pl.pallas_call(
        down_kernel,
        grid=(shape[0],),
        in_specs=[one, one] + [here] * len(came),
        out_specs=here,
        out_shape=jax.ShapeDtypeStruct(shape, BF),
        cost_estimate=pl.CostEstimate(flops=LATER, bytes_accessed=0, transcendentals=0),
        name="down_add",
    )(mine, other, *came)


def last_kernel(mine_ref, other_ref, came_ref, middle_ref, hidden_ref, gain_ref, out_ref):
    grad = (mine_ref[0, 0] + other_ref[0, 0].astype(F32) + came_ref[0].astype(F32)) * gain_ref[...]
    values = hidden_ref[0].astype(F32)
    inverse = lax.rsqrt(jnp.mean(values * values, axis=1, keepdims=True) + EPS)
    normal = values * inverse
    back = inverse * (grad - normal * jnp.mean(grad * normal, axis=1, keepdims=True))
    out_ref[0] = (middle_ref[0] + back).astype(BF)


def last_step(mine, other, came, d_middle, hidden, gain):
    slots, rows, width = hidden.shape
    block = pl.BlockSpec((1, 1, rows, width), lambda s: (0, s, 0, 0))
    here = pl.BlockSpec((1, rows, width), lambda s: (s, 0, 0))
    return pl.pallas_call(
        last_kernel,
        grid=(slots,),
        in_specs=[block, block, here, here, here, pl.BlockSpec((1, width), lambda s: (0, 0))],
        out_specs=here,
        out_shape=jax.ShapeDtypeStruct((slots, rows, width), BF),
        cost_estimate=pl.CostEstimate(flops=2 << 30, bytes_accessed=0, transcendentals=0),
        name="last_step",
    )(mine, other, came, d_middle, hidden, gain)


def half_kernel(half, sends, keeps, extra, keep_ref, came_ref, *refs):
    own_ref = refs[0] if extra else None
    send_ref, left_ref = refs[-2:]
    for ranks, ref in ((sends, send_ref), (keeps, left_ref)):
        for place, i in enumerate(ranks):
            rows = slice(i * half, (i + 1) * half)
            total = keep_ref[rows].astype(F32) + came_ref[rows].astype(F32)
            ref[place * half : (place + 1) * half] = total.astype(BF)
    if extra:
        ours, theirs = own_ref[...].astype(F32), came_ref[-16:].astype(F32)
        send_ref[len(sends) * half :] = in_parts((ours[:2] + ours[2:4]) + (theirs[:2] + theirs[2:4]))


def half_sum(keep, came, own, half, sends, keeps):
    cols = keep.shape[1]
    riding = 0 if own is None else 16
    return pl.pallas_call(
        functools.partial(half_kernel, half, sends, keeps, own is not None),
        out_shape=[
            jax.ShapeDtypeStruct((len(sends) * half + riding, cols), BF),
            jax.ShapeDtypeStruct((len(keeps) * half, cols), BF),
        ],
        compiler_params=pltpu.CompilerParams(vmem_limit_bytes=VMEM_LIMIT),
        cost_estimate=pl.CostEstimate(flops=LATE, bytes_accessed=0, transcendentals=0),
        name="half_sum",
    )(keep, came, *(() if own is None else (own,)))


def ctx_kernel(parts, at_ref, top_ref, top_came, low_ref, low_came, own_ref, mine_ref, small_ref, *refs):
    *sends, sum_ref = refs
    half = top_ref.shape[0]
    shard = mine_ref.shape[0]
    sum_ref[:half] = top_ref[...].astype(F32) + top_came[:half].astype(F32)
    sum_ref[half:] = low_ref[...].astype(F32) + low_came[...].astype(F32)
    ours, theirs = own_ref[...].astype(F32), top_came[half:].astype(F32)
    small = in_parts((ours[:2] + ours[2:4]) + (theirs[:2] + theirs[2:4]))
    small_ref[...] = small

    def rows(k):
        return sum_ref[pl.ds(pl.multiple_of(((at_ref[1] + k) % parts) * shard, 8), shard)]

    mine_ref[...] = rows(0)
    for k, ref in enumerate(sends, 1):
        ref[:shard] = rows(k).astype(BF)
        ref[shard:] = small


def to_ctx(at, top, top_came, low, low_came, own, parts):
    half, cols = top.shape
    shard = 2 * half // parts
    vmem = pl.BlockSpec(memory_space=pltpu.VMEM)
    message = jax.ShapeDtypeStruct((shard + 16, cols), BF)
    return pl.pallas_call(
        functools.partial(ctx_kernel, parts),
        in_specs=[pl.BlockSpec(memory_space=pltpu.SMEM)] + [vmem] * 5,
        out_shape=[jax.ShapeDtypeStruct((shard, cols), F32), jax.ShapeDtypeStruct((16, cols), BF)] + [message] * (parts - 1),
        scratch_shapes=[pltpu.VMEM((2 * half, cols), F32)],
        compiler_params=pltpu.CompilerParams(vmem_limit_bytes=VMEM_LIMIT),
        cost_estimate=pl.CostEstimate(flops=LATE, bytes_accessed=0, transcendentals=0),
        name="to_ctx",
    )(at, top, top_came, low, low_came, own)


def ffn_block(x, g, w_ref, inner_ref):
    units = w_ref.shape[1] // 3
    raised = dot(x, w_ref[:, : 2 * units], NN)
    gate = raised[:, :units]
    upper = raised[:, units:]
    sig = 1.0 / (1.0 + jnp.exp(-gate))
    silu = gate * sig
    act = (silu * upper).astype(BF)
    y = dot(act, w_ref[:, 2 * units :], NT).astype(BF)
    d_act = dot(g, w_ref[:, 2 * units :], NN)
    inner_ref[:, :units] = (d_act * upper * (sig + silu * (1.0 - sig))).astype(BF)
    inner_ref[:, units : 2 * units] = (d_act * silu).astype(BF)
    inner_ref[:, 2 * units :] = act
    d_x = dot(inner_ref[:, : 2 * units], w_ref[:, : 2 * units], NT)
    return y, d_x.astype(BF), jnp.sum(d_x * x.astype(F32), axis=0, keepdims=True)


def ffn_kernel(xm_ref, xo_ref, gm_ref, go_ref, w_ref, ym_ref, yo_ref, dm_ref, do_ref, inner_ref, gain_ref):
    half = xm_ref.shape[0]
    x = jnp.concatenate([xm_ref[...], xo_ref[...]])
    g = jnp.concatenate([gm_ref[...], go_ref[...]])
    y, d_x, gain_row = ffn_block(x, g, w_ref, inner_ref)
    ym_ref[...] = y[:half]
    yo_ref[...] = y[half:]
    dm_ref[...] = d_x[:half]
    do_ref[...] = d_x[half:]

    @pl.when(pl.program_id(0) == 0)
    def _():
        gain_ref[...] = gain_row

    @pl.when(pl.program_id(0) > 0)
    def _():
        gain_ref[...] += gain_row


def ffn_rest_kernel(
    xm_ref, xo_ref, gm_ref, go_ref, w_ref, first_ref, second_ref,
    ym_ref, yo_ref, dm_ref, do_ref, gain_ref, grad_ref, own_ref, inner_ref, sum_ref
):
    units = w_ref.shape[1] // 3
    half = ym_ref.shape[0]
    step = pl.program_id(0)

    def put(ref, place):
        inner_ref[place * half : (place + 1) * half] = ref[:half]
        inner_ref[(place + 2) * half : (place + 3) * half] = ref[half:]

    @pl.when(step == 0)
    def _():
        x = jnp.concatenate([xm_ref[:half], xo_ref[:half]])
        g = jnp.concatenate([gm_ref[:half], go_ref[:half]])
        y, d_x, gain_row = ffn_block(x, g, w_ref, own_ref)
        ym_ref[...] = y[:half]
        yo_ref[...] = y[half:]
        dm_ref[...] = d_x[:half]
        do_ref[...] = d_x[half:]
        gain_ref[...] = gain_row
        put(own_ref, 0)

    @pl.when(step > 0)
    def _():
        put(first_ref, 0)

    put(second_ref, 1)
    left = dot(jnp.concatenate([xm_ref[...], xo_ref[...]]), inner_ref[:, : 2 * units], TN)
    right = dot(jnp.concatenate([gm_ref[...], go_ref[...]]), inner_ref[:, 2 * units :], TN)

    @pl.when(step == 0)
    def _():
        sum_ref[:, : 2 * units] = left
        sum_ref[:, 2 * units :] = right

    @pl.when((step > 0) & (step < pl.num_programs(0) - 1))
    def _():
        sum_ref[:, : 2 * units] += left
        sum_ref[:, 2 * units :] += right

    @pl.when(step == pl.num_programs(0) - 1)
    def _():
        grad_ref[:, : 2 * units] = (sum_ref[:, : 2 * units] + left).astype(BF)
        grad_ref[:, 2 * units :] = (sum_ref[:, 2 * units :] + right).astype(BF)


def feed_forward(x_mine, x_other, g_mine, g_other, w, parts):
    tokens, width = x_mine.shape
    rows = tokens // parts
    units3 = w.shape[1]
    block = pl.BlockSpec((rows, width), lambda i: (i + 1, 0))
    out = pl.BlockSpec((rows, width), lambda i: (i, 0))
    part = jax.ShapeDtypeStruct((tokens - rows, width), BF)
    return pl.pallas_call(
        ffn_kernel,
        grid=(parts - 1,),
        in_specs=[block] * 4 + [pl.BlockSpec((width, units3), lambda i: (0, 0))],
        out_specs=[out] * 4 + [pl.BlockSpec((2 * rows, units3), lambda i: (i, 0)), pl.BlockSpec((1, width), lambda i: (0, 0))],
        out_shape=[part] * 4
        + [jax.ShapeDtypeStruct((2 * (tokens - rows), units3), BF), jax.ShapeDtypeStruct((1, width), F32)],
        compiler_params=pltpu.CompilerParams(vmem_limit_bytes=VMEM_LIMIT),
        cost_estimate=pl.CostEstimate(flops=8 * tokens * width * units3, bytes_accessed=24 << 20, transcendentals=0),
        name="feed_forward",
    )(x_mine, x_other, g_mine, g_other, w)


def ffn_rest(x_mine, x_other, g_mine, g_other, w, inside, parts):
    tokens, width = x_mine.shape
    rows = tokens // parts
    units3 = w.shape[1]
    block = pl.BlockSpec((2 * rows, width), lambda i: (i, 0))
    whole = pl.BlockSpec((width, units3), lambda i: (0, 0))
    first = pl.BlockSpec((2 * rows, units3), lambda i: (jnp.maximum(2 * i - 1, 0), 0))
    second = pl.BlockSpec((2 * rows, units3), lambda i: (2 * i, 0))
    own = pl.BlockSpec((rows, width), lambda i: (0, 0))
    part = jax.ShapeDtypeStruct((rows, width), BF)
    return pl.pallas_call(
        ffn_rest_kernel,
        grid=(parts // 2,),
        in_specs=[block] * 4 + [whole, first, second],
        out_specs=[own] * 4 + [pl.BlockSpec((1, width), lambda i: (0, 0)), whole],
        out_shape=[part] * 4
        + [jax.ShapeDtypeStruct((1, width), F32), jax.ShapeDtypeStruct((width, units3), BF)],
        scratch_shapes=[
            pltpu.VMEM((2 * rows, units3), BF), pltpu.VMEM((4 * rows, units3), BF), pltpu.VMEM((width, units3), F32)
        ],
        compiler_params=pltpu.CompilerParams(vmem_limit_bytes=VMEM_LIMIT),
        cost_estimate=pl.CostEstimate(flops=24 << 30, bytes_accessed=24 << 20, transcendentals=0),
        name="ffn_rest",
    )(x_mine, x_other, g_mine, g_other, w, inside, inside)


def same_kernel(in_ref, out_ref):
    pass


def same(value, flops):
    return pl.pallas_call(
        same_kernel,
        in_specs=[pl.BlockSpec(memory_space=pl.ANY)],
        out_specs=pl.BlockSpec(memory_space=pl.ANY),
        out_shape=jax.ShapeDtypeStruct(value.shape, value.dtype),
        input_output_aliases={0: 0},
        cost_estimate=pl.CostEstimate(flops=flops, bytes_accessed=0, transcendentals=0),
        name="same",
    )(value)


def pack_kernel(gate_ref, up_ref, down_ref, out_ref):
    parts, shard, units3 = out_ref.shape
    units = units3 // 3
    have = gate_ref.shape[1]
    for t in range(parts):
        for j, ref in enumerate((gate_ref, up_ref, down_ref)):
            first = min(t * units, have)
            count = min((t + 1) * units, have) - first
            if count:
                out_ref[t, :, j * units : j * units + count] = ref[:, first : first + count]
            if count < units:
                out_ref[t, :, j * units + count : (j + 1) * units] = jnp.zeros((shard, units - count), BF)


def pack(gate, up, down, parts, units):
    shard = gate.shape[0]
    return pl.pallas_call(
        pack_kernel,
        out_shape=jax.ShapeDtypeStruct((parts, shard, 3 * units), BF),
        compiler_params=pltpu.CompilerParams(vmem_limit_bytes=VMEM_LIMIT),
        name="pack",
    )(gate, up, down)


def finish_kernel(parts_ref, gate_ref, up_ref, down_ref):
    parts, shard, units3 = parts_ref.shape
    units = units3 // 3
    have = gate_ref.shape[1]
    for t in range(parts):
        for j, ref in enumerate((gate_ref, up_ref, down_ref)):
            first = min(t * units, have)
            count = min((t + 1) * units, have) - first
            if count:
                ref[:, first : first + count] = parts_ref[t, :, j * units : j * units + count].astype(F32)


def finish(parts, columns):
    whole = jax.ShapeDtypeStruct((parts.shape[1], columns), F32)
    return pl.pallas_call(
        finish_kernel,
        out_shape=[whole, whole, whole],
        compiler_params=pltpu.CompilerParams(vmem_limit_bytes=VMEM_LIMIT),
        name="finish",
    )(parts)


def inverse_rms(values):
    return lax.rsqrt(jnp.mean(values * values, axis=-1, keepdims=True) + EPS)


def norm_back(values, gain, grad):
    inverse = inverse_rms(values)
    normal = values * inverse
    scaled = grad * gain
    return inverse * (scaled - normal * jnp.mean(scaled * normal, axis=-1, keepdims=True))


def body(
    hidden_in,
    seq_lengths,
    attn_gain,
    query_gain,
    key_gain,
    query_weight,
    key_projection,
    value_projection,
    out_weight,
    ffn_gain,
    gate_weight,
    up_weight,
    down_weight,
    cotangent,
):
    slots, shard_rows, width = hidden_in.shape
    n_fsdp = lax.axis_size("fsdp")
    n_ctx = lax.axis_size("ctx")
    f = lax.axis_index("fsdp")
    c = lax.axis_index("ctx")
    core = lax.axis_index("tp")
    rows = 2 * shard_rows
    keys = n_ctx * rows
    q_cols = query_weight.shape[1]
    k_cols = key_projection.shape[1]
    shard = query_weight.shape[0]
    ff_half = gate_weight.shape[1]
    units = ff_half // n_fsdp
    padded = -(-units // TILE) * TILE

    at = jnp.arange(keys)
    places = (c - at // rows) * rows + ((at // shard_rows) % 2 ^ core) * shard_rows + at % shard_rows
    lanes = jnp.arange(TILE)
    freqs = THETA ** (-((lanes % (HEAD // 2)).astype(F32) * 2.0 / HEAD))
    angles = places.astype(F32)[:, None] * freqs[None, :]
    cosine = jnp.cos(angles)
    sine = jnp.sin(angles) * jnp.where(lanes % HEAD < HEAD // 2, -1.0, 1.0)[None, :]
    scal = jnp.concatenate([jnp.stack([c, core, f]).astype(jnp.int32), seq_lengths])
    own_places = places[:shard_rows]
    valid = own_places[None, :, None] < seq_lengths[:, None, None]

    hidden = hidden_in.astype(F32)
    inverse_one = inverse_rms(hidden)
    normed = (hidden * inverse_one * attn_gain).astype(BF)

    def ctx_stack(pieces):
        stack = jnp.zeros((n_ctx,) + pieces[0].shape, pieces[0].dtype)
        for k, piece in enumerate(pieces):
            stack = lax.dynamic_update_index_in_dim(stack, piece, (c - k) % n_ctx, 0)
        return stack

    def fsdp_stack(pieces):
        stack = jnp.zeros((n_fsdp,) + pieces[0].shape, pieces[0].dtype)
        for m, piece in enumerate(pieces):
            stack = lax.dynamic_update_index_in_dim(stack, piece, f ^ m, 0)
        return stack

    def spread_halves(value):
        masks = [1 << i for i in range(8) if 1 << i < n_fsdp]
        halves = []
        for half, order in zip(jnp.split(value, 2), (masks, masks[::-1])):
            half = half[None]
            for mask in order:
                half = jnp.concatenate([half, fsdp_xor(half, mask)])
            halves.append(half)
        return halves

    def in_order(half, order):
        got = jnp.zeros_like(half)
        for i in range(n_fsdp):
            mask = sum(bit for j, bit in enumerate(order) if i >> j & 1)
            got = lax.dynamic_update_index_in_dim(got, half[i], f ^ mask, 0)
        return got

    def over_ctx(value):
        return [value] + [ctx_shift(value, k) for k in range(1, n_ctx)]

    def over_fsdp(value):
        return [value] + [fsdp_xor(value, m) for m in range(1, n_fsdp)]

    def part(array, index):
        return lax.dynamic_index_in_dim(array, index, 0, keepdims=False)

    def trade_parts(parts):
        return [part(parts, f)] + [fsdp_xor(part(parts, f ^ m), m) for m in range(1, n_fsdp)]

    ffn_packed = pack(gate_weight, up_weight, down_weight.T, n_fsdp, padded)
    packed = jnp.concatenate([query_weight, key_projection, value_projection, out_weight.T], axis=1)
    grad_rows = jnp.where(valid, cotangent, jnp.zeros_like(cotangent))
    x_pieces = [normed, ctx_up(normed)]
    ffn_rows = lax.all_to_all(ffn_packed, "fsdp", 0, 0, tiled=True)
    held = tie(*x_pieces, *over_ctx(packed))
    x_pieces = list(held[:2])
    stack = ctx_stack(held[2:]).reshape(n_ctx * shard, -1)

    top, bottom = spread_halves(stack)
    others = [swap_cores(piece) for piece in x_pieces]
    while len(x_pieces) < n_ctx:
        x_pieces.append(ctx_up(x_pieces[-1]))
        if len(x_pieces) == 3:
            ffn_rows, x_pieces[-1] = tie(ffn_rows, x_pieces[-1])
        others.append(swap_cores(x_pieces[-1]))
    ffn_w = lax.all_gather(ffn_rows, "ctx", axis=1, tiled=True).reshape(width, 3 * padded)
    ffn_w = same(ffn_w, 60 << 30)
    held = tie(*x_pieces, *others, grad_rows, top, bottom)
    x_pieces = held[:n_ctx]
    others = held[n_ctx : 2 * n_ctx]
    grad_rows, top, bottom = held[2 * n_ctx :]

    query_gain2 = jnp.tile(query_gain, 2)[None, :]
    key_gain2 = jnp.tile(key_gain, 2)[None, :]
    attn, stats, q_raw, k_raw, value, q_hat, k_hat, x_all = attend(
        scal, [piece for pair in zip(x_pieces, others) for piece in pair], (top, bottom), (q_cols, k_cols), cosine, sine,
        query_gain2, key_gain2,
    )
    held = tie(attn, *over_fsdp(grad_rows))
    attn = held[0]
    g_mine = jnp.stack(held[1:])
    g_other = swap_cores(g_mine)
    bits = [mask for mask in (1 << i for i in range(8)) if mask < n_fsdp]
    attn_w = jnp.stack([in_order(top, bits), in_order(bottom, bits[::-1])], axis=1).reshape(width, -1)
    out_w = attn_w[:, q_cols + 2 * k_cols :]

    branch = jnp.einsum("sth,dh->std", attn, out_w, preferred_element_type=F32)
    middle = hidden + (branch[:, :shard_rows] + swap_cores(branch[:, shard_rows:]))
    normed_two = (middle * inverse_rms(middle) * ffn_gain).astype(BF)
    x_mine = jnp.stack(over_fsdp(normed_two))
    x_other = swap_cores(x_mine)

    def flat(value):
        return value.reshape(-1, width)

    place = jnp.stack([f]).astype(jnp.int32)

    tokens = (flat(x_mine), flat(x_other), flat(g_mine), flat(g_other))
    y_mine, y_other, dx_mine, dx_other, inside, gain_row = feed_forward(*tokens, ffn_w, n_fsdp)

    def core_sums(mine, other):
        mine = mine.reshape(n_fsdp - 1, slots, shard_rows, width)
        other = swap_cores(other.reshape(n_fsdp - 1, slots, shard_rows, width))
        return [(mine[m].astype(F32) + other[m].astype(F32)).astype(BF) for m in range(n_fsdp - 1)]

    def traded(sums):
        return [fsdp_xor(item, m) for m, item in enumerate(sums, 1)]

    def own(value):
        return value.reshape(slots, shard_rows, width)

    inside, *dx_sums = tie(inside, *core_sums(dx_mine, dx_other))
    inside, *y_sums = tie(inside, *core_sums(y_mine, y_other))
    y_mine, y_other, dx_mine, dx_other, own_gain_row, ffn_grads = ffn_rest(*tokens, ffn_w, inside, n_fsdp)
    ffn_gain_row = (gain_row + own_gain_row)[0]
    ffn_grads, dx_mine, dx_other, *held = tie(ffn_grads, dx_mine, dx_other, *traded(dx_sums))
    ffn_reduced = lax.psum_scatter(
        ffn_grads.reshape(n_fsdp, n_ctx * shard, 3 * padded), "ctx", scatter_dimension=1, tiled=True
    )
    d_normed_two = own(dx_mine).astype(F32) + swap_cores(own(dx_other)).astype(F32)
    d_normed_two = d_normed_two + sum(item.astype(F32) for item in held)
    d_middle = grad_rows.astype(F32) + norm_back(middle, ffn_gain, d_normed_two)
    d_mine = d_middle.astype(BF)
    d_other = swap_cores(d_mine)
    d_branch = jnp.concatenate([d_mine, d_other], axis=1)
    d_attn = jnp.einsum("std,dh->sth", d_branch, out_w, preferred_element_type=F32).astype(BF)
    held = tie(d_attn, *y_sums)
    d_attn = held[0]
    y_sums = held[1:]

    d_q, d_k, d_v, gq, gk = attend_back(
        scal, q_raw, k_raw, value, cosine, sine, query_gain2, key_gain2, q_hat, k_hat, attn, stats, d_attn
    )
    y_got = [own(y_mine), swap_cores(own(y_other))] + traded(y_sums)

    held = tie(d_q, d_k, d_v, gq, gk, ffn_gain_row, *y_got)
    d_q, d_k, d_v, gq, gk, ffn_gain_row = held[:6]
    result = jnp.where(valid, middle + sum(item.astype(F32) for item in held[6:]), 0.0).astype(BF)

    heads = jnp.concatenate([gq, gk])
    small = jnp.stack([jnp.zeros_like(ffn_gain), ffn_gain_row / ffn_gain])
    small = jnp.concatenate([small, heads], axis=1)
    small = jnp.pad(small, ((0, 0), (0, 2 * q_cols + 2 * k_cols - small.shape[1])))
    top_send, top, low_send, low, own = weight_grads(
        place, x_all, d_q, d_k, d_v, d_mine, d_other, attn, attn_w, attn_gain[None, :], two_parts(small), n_fsdp
    )
    top_send, top, low_send, low, own, d_q, d_k, d_v = tie(top_send, top, low_send, low, own, d_q, d_k, d_v)

    half = n_ctx * shard // 2
    bits = bits_of(n_fsdp)
    came = [fsdp_xor(top_send, bits[0]), fsdp_xor(low_send, bits[-1])]
    last_mine, last_other = input_grads(d_q, d_k, d_v, attn_w, n_ctx - 1, 1)
    last_other = swap_cores(last_other)
    mine, other = input_grads(d_q, d_k, d_v, attn_w, 0, n_ctx - 1)
    mine, other, last_other, result, *came = tie(mine, other, last_other, result, *came)
    other = swap_cores(other)
    total = ctx_round(down_add(last_mine, last_other, 0))
    block = n_ctx - 2
    for step in range(1, len(bits)):
        count = n_fsdp >> step
        sent = []
        kept = []
        for side, keep in enumerate((top, low)):
            order = bits if side == 0 else bits[::-1]
            masks = sorted(sum(bit for j, bit in enumerate(order[step:]) if i >> j & 1) for i in range(count))
            sends = [i for i, mask in enumerate(masks) if mask & order[step]]
            keeps = [i for i, mask in enumerate(masks) if not mask & order[step]]
            send, keep = half_sum(keep, came[side], own if side == 0 else None, half, sends, keeps)
            sent.append(send)
            kept.append(keep)
        if step == 1:
            total, other, mine, ffn_reduced, *held = tie(total, other, mine, ffn_reduced, *sent, *kept)
            sent, kept = held[:2], held[2:]
        top, low = kept
        own = sent[0][count // 2 * half :]
        came = [fsdp_xor(sent[0], bits[step]), fsdp_xor(sent[1], bits[-1 - step])]
        if block > 0:
            total = ctx_round(down_add(mine, other, block, total))
            block -= 1
            total, ffn_reduced, *came = tie(total, ffn_reduced, *came)
    ctx_place = jnp.stack([f, c]).astype(jnp.int32)
    mine_rows, small, *messages = to_ctx(ctx_place, top, came[0], low, came[1], own, n_ctx)
    while block > 0:
        total = ctx_down(down_add(mine, other, block, total))
        block -= 1
    got = [ctx_shift(message, k) for k, message in enumerate(messages, 1)]
    ffn_parts = lax.all_to_all(ffn_reduced, "fsdp", 0, 0, tiled=True)
    gate_grad, up_grad, down_grad = finish(ffn_parts, ff_half)
    total, gate_grad, up_grad, down_grad = tie(total, gate_grad, up_grad, down_grad)
    small = [one_part(small)] + [one_part(piece[shard:]) for piece in got]
    got = [mine_rows] + [piece[:shard].astype(F32) for piece in got]
    down_grad = down_grad.T
    attn_grads = sum(got)
    small = tree_sum(small)
    small = small + swap_cores(small)
    input_grad = last_step(mine, other, total, d_middle, hidden_in, attn_gain[None, :])
    qkv_total = attn_grads[:, : q_cols + 2 * k_cols]
    query_weight_grad = qkv_total[:, :q_cols]
    key_weight_grad = qkv_total[:, q_cols : q_cols + k_cols]
    value_weight_grad = qkv_total[:, q_cols + k_cols :]
    out_weight_grad = attn_grads[:, q_cols + 2 * k_cols :].T

    return (
        result,
        input_grad,
        small[0, :width],
        small[0, width : width + HEAD],
        small[1, width : width + HEAD],
        query_weight_grad,
        key_weight_grad,
        value_weight_grad,
        out_weight_grad,
        small[1, :width],
        gate_grad,
        up_grad,
        down_grad,
    )


def solution(mesh):
    in_specs = (
        P("fsdp", ("ctx", "tp"), None),
        P("fsdp"),
        P(),
        P(),
        P(),
        P(("fsdp", "ctx"), "tp"),
        P(("fsdp", "ctx"), "tp"),
        P(("fsdp", "ctx"), "tp"),
        P("tp", ("fsdp", "ctx")),
        P(),
        P(("fsdp", "ctx"), "tp"),
        P(("fsdp", "ctx"), "tp"),
        P("tp", ("fsdp", "ctx")),
        P("fsdp", ("ctx", "tp"), None),
    )
    out_specs = (
        P("fsdp", ("ctx", "tp"), None),
        P("fsdp", ("ctx", "tp"), None),
        P(),
        P(),
        P(),
        P(("fsdp", "ctx"), "tp"),
        P(("fsdp", "ctx"), "tp"),
        P(("fsdp", "ctx"), "tp"),
        P("tp", ("fsdp", "ctx")),
        P(),
        P(("fsdp", "ctx"), "tp"),
        P(("fsdp", "ctx"), "tp"),
        P("tp", ("fsdp", "ctx")),
    )
    return jax.shard_map(body, mesh=mesh, in_specs=in_specs, out_specs=out_specs, check_vma=False)
```
